512 devices in a mesh: fsdp: 2 (over z_hi), seq: 32 (over x, y, core), tp: 8 (over z_lo).
Axes of the slice: x: 4, y: 4, z: 16 (z_hi: 2, z_lo: 8; z = z_hi * 8 + z_lo), core: 2. Of those that a mesh axis runs over, the one named last changes fastest.
Arguments:
- tokens: bfloat16 [16384, 8192], P(('fsdp', 'seq', 'tp')), may hold values from -6 to 6
- proj_mean: bfloat16 [8192, 4096], P(('fsdp', 'seq'), 'tp'), may hold values from -0.0625 to 0.0625
- proj_devs: bfloat16 [4, 8192, 4096], P(None, ('fsdp', 'seq'), 'tp'), may hold values from -0.0625 to 0.0625
- bc_mean: bfloat16 [8192, 2, 1024], P(('fsdp', 'seq'), None, 'tp'), may hold values from -0.0625 to 0.0625
- bc_devs: bfloat16 [4, 8192, 2, 1024], P(None, ('fsdp', 'seq'), None, 'tp'), may hold values from -0.0625 to 0.0625
- swag_coef: float32 [4], replicated, may hold values from -4 to 4
- dt_weight: bfloat16 [8192, 64], P(('fsdp', 'seq'), 'tp'), may hold values from -0.0625 to 0.0625
- dt_bias: float32 [64], P('tp'), may hold values from -12 to -2, as said below
- decay_rate: float32 [64], P('tp'), may hold values from 0 to 16, as said below
- skip_gain: float32 [64], P('tp'), may hold values from 0.5 to 1.5
- conv_proj: float32 [4, 4096], P(None, 'tp'), may hold values from -3 to 3
- conv_bc: float32 [4, 2, 1024], P(None, None, 'tp'), may hold values from -1.5 to 1.5
Outputs:
- ssm_out: bfloat16 [16384, 4096], P(('fsdp', 'seq'), 'tp')
The draws below stay inside these ranges and needn't reach their ends.
Inputs may be any that keep to these rules, and one draw needn't show every extreme that they name: `dt_bias`: every bias is the inverse softplus of a positive step size. `decay_rate`: every rate is positive.
All inputs are finite; a program needn't handle non-finite values.
Results may differ from the reference program's by a relative error of at most 0.0059.
Values may be sent and summed in bfloat16 or wider, within the bound.
A program may use at most 64 MiB of HBM per device.

```python
import math
import jax
import jax.numpy as jnp
from jax import lax

D = 8192
HEADS = 64
P_SIZE = 64
N = 128
GROUPS = 8
DEVS = 4
CONV = 4
SPAN = 128
LENGTH = 8192
DOCS = 2
TOKENS = 16384


def head_law(key):
    base = jax.random.fold_in(key, 11)
    pick_key, reach_key, keep_key, step_key, rate_key = jax.random.split(base, 5)
    slow_share = 0.5
    reach = jnp.exp(jax.random.uniform(reach_key, (HEADS,), jnp.float32, math.log(2.0), math.log(4.0)))
    keep = jnp.exp(jax.random.uniform(keep_key, (HEADS,), jnp.float32, math.log(0.3), math.log(1.2)))
    fast_step = jnp.exp(jax.random.uniform(step_key, (HEADS,), jnp.float32, math.log(0.01), math.log(0.1)))
    fast_rate = jnp.exp(jax.random.uniform(rate_key, (HEADS,), jnp.float32, math.log(1.0), math.log(16.0)))
    is_slow = jax.random.uniform(pick_key, (HEADS,), jnp.float32) < slow_share
    step_level = jnp.where(is_slow, reach / LENGTH, fast_step)
    rate_level = jnp.where(is_slow, keep / reach, fast_rate)
    return (step_level, rate_level)


def draw_decay_rate(key, part):
    step_level, rate_level = head_law(key)
    return rate_level


def draw_dt_bias(key, part):
    step_level, rate_level = head_law(key)
    return jnp.log(jnp.expm1(step_level))


def level_of(key, dims, shards, least, high):
    loudness = 1.0
    for axis_at, shards_of in shards:
        steps = jax.random.uniform(jax.random.fold_in(jax.random.fold_in(key, 6), axis_at), (shards_of,), jnp.float32, least / len(shards), high / len(shards))
        loudness = loudness * jnp.repeat(jnp.exp(steps), dims[axis_at] // shards_of).reshape((-1,) + (1,) * (len(dims) - 1 - axis_at))
    return loudness


def bell_draw(rng, dims, deviation, bound, pieces=(), dtype=jnp.bfloat16):
    factor_of = level_of(rng, dims, pieces, -0.22, 0.18) if pieces else 1.0
    entries = jax.random.normal(rng, dims, jnp.float32) * deviation * factor_of
    return jnp.minimum(jnp.maximum(entries, -bound), bound).astype(dtype)


def setup_inputs(seed: int = 0) -> dict:
    seeds = jax.random.split(jax.random.key(seed), 13)
    tokens = bell_draw(seeds[0], (TOKENS, D), 1.0, 6.0, ((0, 512),))
    proj_mean = bell_draw(seeds[1], (D, HEADS * P_SIZE), D ** -0.5, 0.0625, ((0, 64), (1, 8)))
    proj_devs = bell_draw(seeds[2], (DEVS, D, HEADS * P_SIZE), D ** -0.5, 0.0625, ((1, 64), (2, 8)))
    bc_mean = bell_draw(seeds[3], (D, 2, GROUPS * N), D ** -0.5, 0.0625, ((0, 64), (2, 8)))
    bc_devs = bell_draw(seeds[4], (DEVS, D, 2, GROUPS * N), D ** -0.5, 0.0625, ((1, 64), (3, 8)))
    swag_coef = bell_draw(seeds[5], (DEVS,), 1.0, 4.0, (), jnp.float32)
    dt_weight = bell_draw(seeds[6], (D, HEADS), D ** -0.5, 0.0625, ((0, 64), (1, 8)))
    dt_bias = draw_dt_bias(jax.random.fold_in(seeds[12], 71), 0)
    decay_rate = draw_decay_rate(jax.random.fold_in(seeds[12], 71), 0)
    skip_gain = jnp.clip(0.5 + 1.0 * jax.random.uniform(seeds[9], (HEADS,), jnp.float32) ** level_of(seeds[9], (HEADS,), ((0, 8),), -0.2, 0.2), 0.5, 1.5)
    conv_proj = bell_draw(seeds[10], (CONV, HEADS * P_SIZE), CONV ** -0.5, 3.0, ((1, 8),), jnp.float32)
    conv_bc = bell_draw(seeds[11], (CONV, 2, GROUPS * N), 0.25, 1.5, ((2, 8),), jnp.float32)
    return {"tokens": tokens, "proj_mean": proj_mean, "proj_devs": proj_devs, "bc_mean": bc_mean, "bc_devs": bc_devs, "swag_coef": swag_coef, "dt_weight": dt_weight, "dt_bias": dt_bias, "decay_rate": decay_rate, "skip_gain": skip_gain, "conv_proj": conv_proj, "conv_bc": conv_bc}


def sampled(mean_part, dev_part, swag_coef):
    factor = (2.0 * (DEVS - 1)) ** -0.5
    accum = mean_part.astype(jnp.float32)
    for member in range(DEVS):
        accum = accum + factor * swag_coef[member] * dev_part[member].astype(jnp.float32)
    return accum.astype(jnp.bfloat16)


def rounded(source):
    narrow = lax.optimization_barrier(source.astype(jnp.bfloat16))
    return narrow.astype(jnp.float32)


def causal_conv(projected, kernel):
    padded = jnp.concatenate([jnp.zeros((CONV - 1, projected.shape[1]), jnp.float32), projected.astype(jnp.float32)], axis=0)
    conv_sum = kernel[0] * padded[0:LENGTH]
    for offset in range(1, CONV):
        conv_sum = conv_sum + kernel[offset] * padded[offset:offset + LENGTH]
    return jax.nn.silu(conv_sum).astype(jnp.bfloat16)


def reference(tokens, proj_mean, proj_devs, bc_mean, bc_devs, swag_coef, dt_weight, dt_bias, decay_rate, skip_gain, conv_proj, conv_bc):
    weight_x = sampled(proj_mean, proj_devs, swag_coef)
    weight_bc = sampled(bc_mean, bc_devs, swag_coef).reshape(D, 2 * GROUPS * N)
    proj_x = jnp.dot(tokens, weight_x, preferred_element_type=jnp.float32).astype(jnp.bfloat16)
    proj_bc = jnp.dot(tokens, weight_bc, preferred_element_type=jnp.float32).astype(jnp.bfloat16)
    logits = jnp.dot(tokens, dt_weight, preferred_element_type=jnp.float32)
    kernel_bc = conv_bc.reshape(CONV, 2 * GROUPS * N)
    per_group = HEADS // GROUPS
    blocks = LENGTH // SPAN
    causal_mask = jnp.tril(jnp.ones((SPAN, SPAN), bool))

    def document(items):
        doc_x, doc_bc, doc_logits = items
        values = causal_conv(doc_x, conv_proj).astype(jnp.float32).reshape(blocks, SPAN, HEADS, P_SIZE)
        both_parts = causal_conv(doc_bc, kernel_bc).astype(jnp.float32).reshape(LENGTH, 2, GROUPS, N)
        keys_h = jnp.repeat(both_parts[:, 0], per_group, axis=1).reshape(blocks, SPAN, HEADS, N)
        reads_h = jnp.repeat(both_parts[:, 1], per_group, axis=1).reshape(blocks, SPAN, HEADS, N)
        steps_b = jax.nn.softplus(doc_logits + dt_bias).reshape(blocks, SPAN, HEADS)
        cum_log = jnp.cumsum(-steps_b * decay_rate, axis=1)
        scores = jnp.einsum("bqhn,bshn->bhqs", reads_h, keys_h)
        later_cum = jnp.transpose(cum_log, (0, 2, 1))
        cum_gaps = later_cum[:, :, :, None] - later_cum[:, :, None, :]
        decays = jnp.where(causal_mask, jnp.exp(jnp.minimum(cum_gaps, 0.0)), 0.0)
        weights = rounded(scores * decays * jnp.transpose(steps_b, (0, 2, 1))[:, :, None, :])
        inner_part = jnp.einsum("bhqs,bshp->bqhp", weights, values)
        last_cum = cum_log[:, SPAN - 1:, :]
        scaled = rounded(values * (jnp.exp(last_cum - cum_log) * steps_b)[..., None])
        states = jnp.einsum("bshn,bshp->bhnp", keys_h, scaled)
        block_decay = jnp.exp(last_cum[:, 0, :])

        def advance(carried, pair):
            return pair[0][:, None, None] * carried + pair[1], carried

        unused, entering = lax.scan(advance, jnp.zeros((HEADS, N, P_SIZE), jnp.float32), (block_decay, states))
        entering_bf = rounded(entering)
        outer_part = jnp.exp(cum_log)[..., None] * jnp.einsum("bqhn,bhnp->bqhp", reads_h, entering_bf)
        result = inner_part + outer_part + skip_gain[:, None] * values
        return result.reshape(LENGTH, HEADS * P_SIZE).astype(jnp.bfloat16)

    outputs = lax.map(document, (proj_x.reshape(DOCS, LENGTH, HEADS * P_SIZE), proj_bc.reshape(DOCS, LENGTH, 2 * GROUPS * N), logits.reshape(DOCS, LENGTH, HEADS)))
    return outputs.reshape(TOKENS, HEADS * P_SIZE)
```

```python
import jax
import jax.numpy as jnp
from jax import lax
from jax.experimental import pallas as pl
from jax.experimental.pallas import tpu as pltpu
from jax.sharding import PartitionSpec as P

P_SIZE = 64
N = 128
CONV = 4
SPAN = 128
MESH = pl.DeviceIdType.MESH
WIDTH = 896
ROWS = 32


def sampled(mean_part, dev_part, swag_coef):
    factor = (2.0 * (dev_part.shape[0] - 1)) ** (-0.5)
    accum = mean_part.astype(jnp.float32)
    for member in range(dev_part.shape[0]):
        accum = accum + factor * swag_coef[member] * dev_part[member].astype(jnp.float32)
    return accum.astype(jnp.bfloat16)


def project_kernel(
    tok_ref, w_ref, out_ref, dt_ref,
    x_buf, w_buf, stage, relay, part, other,
    tok_send, tok_recv, pair_send, pair_recv, w_send, w_recv, fx_send, fx_recv, ex_send, ex_recv, own_sem,
):
    f = lax.axis_index("fsdp")
    s = lax.axis_index("seq")
    t = lax.axis_index("tp")
    core = lax.rem(s, 2)
    y = lax.rem(lax.div(s, 2), 4)
    x = lax.div(s, 8)

    def wrap(value):
        return lax.rem(value + 4, 4)

    def place(x_at, y_at, core_at):
        return (f, x_at * 8 + y_at * 2 + core_at, t)

    sibling = place(x, y, 1 - core)
    nexts = {"y": place(x, wrap(y + 1), core), "x": place(wrap(x + 1), y, core)}
    prevs = {"y": place(x, wrap(y - 1), core), "x": place(wrap(x - 1), y, core)}
    z_next, z_prev = (f, s, lax.min(t + 1, 7)), (f, s, lax.max(t - 1, 0))
    z = f * 8 + t
    up, down = lax.rem(z + 4, 16), lax.rem(z + 12, 16)
    f_up, f_down = lax.div(up, 8), lax.div(down, 8)
    z_up, z_down = (f_up, s, lax.rem(up, 8)), (f_down, s, lax.rem(down, 8))

    own = pltpu.make_async_copy(w_ref, w_buf.at[f, x, y], own_sem)
    own.start()
    barrier = pltpu.get_barrier_semaphore()
    for peer in (sibling, nexts["y"], prevs["y"], nexts["x"], prevs["x"], z_up, z_down):
        pl.semaphore_signal(barrier, inc=1, device_id=peer, device_id_type=MESH)

    @pl.when(t < 7)
    def _():
        pl.semaphore_signal(barrier, inc=1, device_id=z_next, device_id_type=MESH)

    @pl.when(t > 0)
    def _():
        pl.semaphore_signal(barrier, inc=1, device_id=z_prev, device_id_type=MESH)

    for mine in range(2):

        @pl.when(core == mine)
        def _():
            for j in range(32):
                here = slice(j * 128, (j + 1) * 128)
                keep, give = 2 * j + mine, 2 * j + 1 - mine
                x_buf[t, mine * ROWS:(mine + 1) * ROWS, here] = tok_ref[:, keep * 128:(keep + 1) * 128]
                stage[:, here] = tok_ref[:, give * 128:(give + 1) * 128]

    @pl.when((t > 0) & (t < 7))
    def _():
        pl.semaphore_wait(barrier, 9)

    @pl.when((t == 0) | (t == 7))
    def _():
        pl.semaphore_wait(barrier, 8)

    rows = [pl.ds(core * ROWS, ROWS), pl.ds((1 - core) * ROWS, ROWS)]
    sends = []

    def remote(src, dst, send_sem, recv_sem, peer):
        return pltpu.make_async_remote_copy(
            src_ref=src, dst_ref=dst, send_sem=send_sem, recv_sem=recv_sem,
            device_id=peer, device_id_type=MESH,
        )

    def launch(copy, condition=None):
        if condition is None:
            copy.start()
        else:
            pl.when(condition)(copy.start)
        sends.append((copy, condition))

    def token_send(k, b):
        for way, (unit, peer, condition) in enumerate((
            (lax.max(t - k, 0), z_next, (t < 7) & (t >= k)),
            (lax.min(t + k, 7), z_prev, (t > 0) & (t + k <= 7)),
        )):
            piece = x_buf.at[unit, rows[b]]
            launch(remote(piece, piece, tok_send.at[way, k, b], tok_recv.at[way, k, b], peer), condition)

    def token_wait(k, b):
        for way, (unit, condition) in enumerate((
            (lax.max(t - 1 - k, 0), t - 1 >= k),
            (lax.min(t + 1 + k, 7), t + 1 + k <= 7),
        )):
            piece = x_buf.at[unit, rows[b]]

            @pl.when(condition)
            def _():
                remote(piece, piece, tok_send.at[way, k, b], tok_recv.at[way, k, b], z_next).wait_recv()

    def token_step(k, b):
        token_wait(k, b)
        token_send(k + 1, b)

    halves = (pl.ds(0, 64), pl.ds(64, 64))
    lines = (y, wrap(y - 1), wrap(y + 1), wrap(y + 2))

    def block(g, phase, shift):
        source = f if g == 0 else 1 - f
        if phase == 0:
            return w_buf.at[source, x, wrap(y + shift)]
        return w_buf.at[source, wrap(x + shift), lines[phase - 1]]

    def axis(phase):
        return "y" if phase == 0 else "x"

    def w_copy(g, phase, kind, piece):
        peer = (nexts if kind % 2 == 0 else prevs)[axis(phase)]
        return remote(piece, piece, w_send.at[g, phase, kind], w_recv.at[g, phase, kind], peer)

    def w_start(g, phase):
        for kind in range(2):
            launch(w_copy(g, phase, kind, block(g, phase, 0)))

    def w_forward(g, phase):
        for kind, shift in ((0, -1), (1, 1)):
            w_copy(g, phase, kind, block(g, phase, shift)).wait_recv()
            launch(w_copy(g, phase, 2 + kind, block(g, phase, shift).at[halves[kind]]))

    def w_finish(g, phase):
        for kind in range(2):
            w_copy(g, phase, 2 + kind, block(g, phase, 2).at[halves[kind]]).wait_recv()

    pair = remote(stage, x_buf.at[t, rows[0]], pair_send, pair_recv, sibling)
    launch(pair)
    token_send(0, 0)
    own.wait()
    w_start(0, 0)
    w_start(0, 1)
    for kind, peer in ((0, z_up), (1, z_down)):
        launch(remote(w_buf.at[f, x, y, halves[kind]], relay.at[kind], fx_send.at[0, kind], fx_recv.at[0, kind], peer))
    remote(stage, x_buf.at[t, rows[1]], pair_send, pair_recv, sibling).wait_recv()
    token_send(0, 1)

    w_forward(0, 0)
    w_start(0, 2)
    token_step(0, 0)
    w_forward(0, 1)
    w_start(0, 3)
    for kind, (peer, source) in enumerate(((z_up, f_down), (z_down, f_up))):
        remote(relay.at[kind], relay.at[kind], fx_send.at[0, kind], fx_recv.at[0, kind], peer).wait_recv()
        launch(remote(relay.at[kind], w_buf.at[source, x, y, halves[kind]], fx_send.at[1, kind], fx_recv.at[1, kind], peer))
    w_finish(0, 0)
    w_start(0, 4)
    token_step(0, 1)
    w_forward(0, 2)
    token_step(1, 0)
    for kind, peer in ((0, z_up), (1, z_down)):
        there = w_buf.at[1 - f, x, y, halves[kind]]
        remote(relay.at[kind], there, fx_send.at[1, kind], fx_recv.at[1, kind], peer).wait_recv()
    w_start(1, 0)
    w_start(1, 1)
    w_forward(0, 3)
    token_step(1, 1)
    w_forward(1, 0)
    w_start(1, 2)
    w_forward(0, 4)
    token_step(2, 0)
    w_start(1, 3)
    w_finish(1, 0)
    w_start(1, 4)
    token_step(2, 1)
    w_forward(1, 1)
    token_step(3, 0)
    w_forward(1, 2)
    token_step(3, 1)
    token_step(4, 0)
    w_forward(1, 3)
    token_step(4, 1)
    w_forward(1, 4)
    token_step(5, 0)
    token_step(5, 1)
    for g in range(2):
        for phase in range(1, 5):
            w_finish(g, phase)

    def multiply(first, count, kind):
        for start in range(0, WIDTH, 256):
            stop = min(start + 256, WIDTH)
            weight = w_buf[:, :, :, :, start:stop].reshape(4096, stop - start)
            units = x_buf[pl.ds(first, count)].reshape(count * 64, 4096)
            product = jnp.dot(units, weight, preferred_element_type=jnp.float32)
            part[pl.ds(first, count), :, :, start:stop] = product.reshape(count, 2, ROWS, stop - start)
        swap = remote(
            part.at[pl.ds(first, count), 1 - core], other.at[pl.ds(first, count)],
            ex_send.at[kind], ex_recv.at[kind], sibling,
        )
        launch(swap)
        return swap

    low = t < 4
    near = multiply(jnp.where(low, 0, 2), 6, 0)
    token_wait(6, 0)
    token_wait(6, 1)
    far = multiply(jnp.where(low, 6, 0), 2, 1)
    near.wait_recv()
    far.wait_recv()
    total = part[:, core] + other[...]
    out_ref[...] = total[:, :, :768].reshape(8 * ROWS, 768).astype(jnp.bfloat16)
    dt_ref[...] = total[:, :, 768:].reshape(8 * ROWS, WIDTH - 768)
    for copy, condition in sends:
        if condition is None:
            copy.wait_send()
        else:
            pl.when(condition)(copy.wait_send)


def project(tokens, weight):
    vmem = pl.BlockSpec(memory_space=pltpu.VMEM)
    dma = pltpu.SemaphoreType.DMA
    return pl.pallas_call(
        project_kernel,
        out_shape=(
            jax.ShapeDtypeStruct((256, 768), jnp.bfloat16),
            jax.ShapeDtypeStruct((256, WIDTH - 768), jnp.float32),
        ),
        in_specs=[vmem, vmem],
        out_specs=(vmem, vmem),
        scratch_shapes=[
            pltpu.VMEM((8, 2 * ROWS, 4096), jnp.bfloat16),
            pltpu.VMEM((2, 4, 4, 128, WIDTH), jnp.bfloat16),
            pltpu.VMEM((ROWS, 4096), jnp.bfloat16),
            pltpu.VMEM((2, 64, WIDTH), jnp.bfloat16),
            pltpu.VMEM((8, 2, ROWS, WIDTH), jnp.float32),
            pltpu.VMEM((8, ROWS, WIDTH), jnp.float32),
            dma((2, 7, 2)), dma((2, 7, 2)), dma(()), dma(()),
            dma((2, 5, 4)), dma((2, 5, 4)), dma((2, 2)), dma((2, 2)), dma((2,)), dma((2,)), dma(()),
        ],
        compiler_params=pltpu.CompilerParams(
            collective_id=0, has_side_effects=True, vmem_limit_bytes=56 * 2**20
        ),
        name="project",
    )(tokens, weight)

def shifted(shard, axis, by):
    count = lax.axis_size(axis)
    pairs = [(i, i + by) for i in range(count) if 0 <= i + by < count]
    return lax.ppermute(shard, axis, pairs)


def prefix(part, axis, combine, identity):
    place = lax.axis_index(axis)
    gathered = jax.tree.map(lambda a: lax.all_gather(a, axis), part)
    state = jax.tree.map(lambda a, e: jnp.zeros_like(a) + jnp.asarray(e, a.dtype), part, identity)

    def one(hop, state):
        return combine(
            state, jax.tree.map(lambda a: lax.dynamic_index_in_dim(a, hop, 0, False), gathered)
        )

    return lax.fori_loop(0, place, one, state)


def combine(former, latter):
    return (former[0] * latter[0], latter[0][:, None, None] * former[1] + latter[1])


def body(
    tokens,
    proj_mean,
    proj_devs,
    bc_mean,
    bc_devs,
    swag_coef,
    dt_weight,
    dt_bias,
    decay_rate,
    skip_gain,
    conv_proj,
    conv_bc,
):
    heads_here = decay_rate.shape[0]
    groups_here = bc_mean.shape[2] // N
    width_x = proj_mean.shape[1]
    width_bc = 2 * bc_mean.shape[2]
    tok_count = 256
    weight_x = sampled(proj_mean, proj_devs, swag_coef)
    weight_bc = sampled(bc_mean, bc_devs, swag_coef).reshape(bc_mean.shape[0], width_bc)
    padding = jnp.zeros((bc_mean.shape[0], WIDTH - width_x - width_bc - heads_here), jnp.bfloat16)
    weight_all = jnp.concatenate([weight_x, weight_bc, dt_weight, padding], axis=1)
    projected, logits = project(tokens, weight_all)
    step_size = jax.nn.softplus(logits[:, :heads_here] + dt_bias)
    rim_rows = shifted(projected[tok_count - (CONV - 1) :], "seq", 1)
    padded = jnp.concatenate([rim_rows, projected], axis=0).astype(jnp.float32)
    kernel = jnp.concatenate([conv_proj, conv_bc.reshape(CONV, width_bc)], axis=1)
    conv_sum = kernel[0] * padded[0:tok_count]
    for offset in range(1, CONV):
        conv_sum = conv_sum + kernel[offset] * padded[offset : offset + tok_count]
    conved = jax.nn.silu(conv_sum).astype(jnp.bfloat16)
    blocks = tok_count // SPAN
    per_group = heads_here // groups_here
    values = conved[:, :width_x].reshape(blocks, SPAN, heads_here, P_SIZE)
    keys_b = conved[:, width_x : width_x + width_bc // 2].reshape(blocks, SPAN, groups_here, N)
    reads_c = conved[:, width_x + width_bc // 2 :].reshape(blocks, SPAN, groups_here, N)
    steps_b = step_size.reshape(blocks, SPAN, heads_here)
    cum_log = jnp.einsum(
        "ts,bsh->bth", jnp.tril(jnp.ones((SPAN, SPAN), jnp.float32)), -steps_b * decay_rate,
        precision=lax.Precision.HIGHEST,
    )
    last_cum = cum_log[:, SPAN - 1 :, :]
    scaled = (
        values.astype(jnp.float32) * (jnp.exp(last_cum - cum_log) * steps_b)[..., None]
    ).astype(jnp.bfloat16)
    keys_h = jnp.repeat(keys_b, per_group, axis=2)
    states = jnp.einsum("bshn,bshp->bhnp", keys_h, scaled, preferred_element_type=jnp.float32)
    block_decay = jnp.exp(last_cum[:, 0, :])
    total_decay = block_decay[0]
    total_state = states[0]
    member = 1
    total_decay, total_state = combine(
        (total_decay, total_state), (block_decay[member], states[member])
    )
    incoming = prefix(
        (total_decay, total_state),
        "seq",
        combine,
        (jnp.ones((heads_here,), jnp.float32), jnp.zeros((heads_here, N, P_SIZE), jnp.float32)),
    )
    scores = jnp.einsum("bqgn,bsgn->bgqs", reads_c, keys_b, preferred_element_type=jnp.float32)
    scores = jnp.repeat(scores, per_group, axis=1)
    causal_mask = jnp.tril(jnp.ones((SPAN, SPAN), bool))
    later_cum = jnp.transpose(cum_log, (0, 2, 1))
    cum_gaps = later_cum[:, :, :, None] - later_cum[:, :, None, :]
    decays = jnp.where(causal_mask, jnp.exp(jnp.minimum(cum_gaps, 0.0)), 0.0)
    weights = (scores * decays * jnp.transpose(steps_b, (0, 2, 1))[:, :, None, :]).astype(
        jnp.bfloat16
    )
    inner_part = jnp.einsum("bhqs,bshp->bqhp", weights, values, preferred_element_type=jnp.float32)
    carried = incoming[1]
    entering = []
    for member in range(blocks):
        entering.append(carried)
        carried = block_decay[member][:, None, None] * carried + states[member]
    entering_bf = jnp.stack(entering).astype(jnp.bfloat16)
    reads_h = jnp.repeat(reads_c, per_group, axis=2)
    outer_part = jnp.exp(cum_log)[..., None] * jnp.einsum(
        "bqhn,bhnp->bqhp", reads_h, entering_bf, preferred_element_type=jnp.float32
    )
    result = inner_part + outer_part + skip_gain[:, None] * values.astype(jnp.float32)
    return result.reshape(tok_count, width_x).astype(jnp.bfloat16)


def solution(mesh):
    return jax.shard_map(
        body,
        mesh=mesh,
        in_specs=(
            P(("fsdp", "seq", "tp"), None),
            P(("fsdp", "seq"), "tp"),
            P(None, ("fsdp", "seq"), "tp"),
            P(("fsdp", "seq"), None, "tp"),
            P(None, ("fsdp", "seq"), None, "tp"),
            P(),
            P(("fsdp", "seq"), "tp"),
            P("tp"),
            P("tp"),
            P("tp"),
            P(None, "tp"),
            P(None, None, "tp"),
        ),
        out_specs=P(("fsdp", "seq"), "tp"),
        check_vma=False,
    )
```

```python
import jax
import jax.numpy as jnp
from jax import lax
from jax.experimental import pallas as pl
from jax.experimental.pallas import tpu as pltpu
from jax.sharding import PartitionSpec as P

P_SIZE = 64
N = 128
CONV = 4
SPAN = 128
MESH = pl.DeviceIdType.MESH
WIDTH = 896
ROWS = 32


def sampled(mean_part, dev_part, swag_coef):
    factor = (2.0 * (dev_part.shape[0] - 1)) ** (-0.5)
    accum = mean_part.astype(jnp.float32)
    for member in range(dev_part.shape[0]):
        accum = accum + factor * swag_coef[member] * dev_part[member].astype(jnp.float32)
    return accum.astype(jnp.bfloat16)


def expand(heads):
    lane = lax.broadcasted_iota(jnp.int32, (heads.shape[0], 128), 1)
    return jnp.concatenate(
        [jnp.where(lane < P_SIZE, heads[:, 2 * j:2 * j + 1], heads[:, 2 * j + 1:2 * j + 2]) for j in range(4)],
        axis=1,
    )


def softplus(value):
    small = jnp.exp(-jnp.abs(value))
    series = small * (1.0 - small * (0.5 - small * (1.0 / 3.0 - small * 0.25)))
    return jnp.maximum(value, 0.0) + jnp.where(small < 0.01, series, jnp.log(1.0 + small))


def layer_kernel(
    tok_ref, w_ref, conv_x_ref, conv_bc_ref, bias_ref, rate_ref, skip_ref, out_ref,
    x_buf, w_buf, stage, relay, part, other, padded, edge, values, keys, reads, inner, states,
    pair_state, pair_decay, y_state, y_decay, x_state, x_decay, give_state, give_decay, inflow, outflow, dt_buf,
    tok_send, tok_recv, pair_send, pair_recv, w_send, w_recv, fx_send, fx_recv, ex_send, ex_recv, own_sem,
    halo_send, halo_recv, p1_send, p1_recv, p2_send, p2_recv, p4_send, p4_recv,
):
    f = lax.axis_index("fsdp")
    s = lax.axis_index("seq")
    t = lax.axis_index("tp")
    core = lax.rem(s, 2)
    y = lax.rem(lax.div(s, 2), 4)
    x = lax.div(s, 8)

    def wrap(value):
        return lax.rem(value + 4, 4)

    def place(x_at, y_at, core_at):
        return (f, x_at * 8 + y_at * 2 + core_at, t)

    sibling = place(x, y, 1 - core)
    nexts = {"y": place(x, wrap(y + 1), core), "x": place(wrap(x + 1), y, core)}
    prevs = {"y": place(x, wrap(y - 1), core), "x": place(wrap(x - 1), y, core)}
    z_next, z_prev = (f, s, lax.min(t + 1, 7)), (f, s, lax.max(t - 1, 0))
    z = f * 8 + t
    up, down = lax.rem(z + 4, 16), lax.rem(z + 12, 16)
    f_up, f_down = lax.div(up, 8), lax.div(down, 8)
    z_up, z_down = (f_up, s, lax.rem(up, 8)), (f_down, s, lax.rem(down, 8))

    own = pltpu.make_async_copy(w_ref, w_buf.at[f, x, y], own_sem)
    own.start()
    barrier = pltpu.get_barrier_semaphore()
    y_far, x_far = place(x, wrap(y + 2), core), place(wrap(x + 2), y, core)
    seq_next, seq_prev = (f, lax.min(s + 1, 31), t), (f, lax.max(s - 1, 0), t)
    for peer in (sibling, nexts["y"], prevs["y"], y_far, nexts["x"], prevs["x"], x_far, z_up, z_down):
        pl.semaphore_signal(barrier, inc=1, device_id=peer, device_id_type=MESH)

    @pl.when(t < 7)
    def _():
        pl.semaphore_signal(barrier, inc=1, device_id=z_next, device_id_type=MESH)

    @pl.when(t > 0)
    def _():
        pl.semaphore_signal(barrier, inc=1, device_id=z_prev, device_id_type=MESH)

    @pl.when(s < 31)
    def _():
        pl.semaphore_signal(barrier, inc=1, device_id=seq_next, device_id_type=MESH)

    @pl.when(s > 0)
    def _():
        pl.semaphore_signal(barrier, inc=1, device_id=seq_prev, device_id_type=MESH)

    for mine in range(2):

        @pl.when(core == mine)
        def _():
            for j in range(32):
                here = slice(j * 128, (j + 1) * 128)
                keep, give = 2 * j + mine, 2 * j + 1 - mine
                x_buf[t, mine * ROWS:(mine + 1) * ROWS, here] = tok_ref[:, keep * 128:(keep + 1) * 128]
                stage[:, here] = tok_ref[:, give * 128:(give + 1) * 128]

    ends = [t > 0, t < 7, s > 0, s < 31]
    pl.semaphore_wait(barrier, 9 + sum(jnp.where(end, 1, 0) for end in ends))

    rows = [pl.ds(core * ROWS, ROWS), pl.ds((1 - core) * ROWS, ROWS)]
    sends = []

    def remote(src, dst, send_sem, recv_sem, peer):
        return pltpu.make_async_remote_copy(
            src_ref=src, dst_ref=dst, send_sem=send_sem, recv_sem=recv_sem,
            device_id=peer, device_id_type=MESH,
        )

    def launch(copy, condition=None):
        if condition is None:
            copy.start()
        else:
            pl.when(condition)(copy.start)
        sends.append((copy, condition))

    def token_send(k, b):
        for way, (unit, peer, condition) in enumerate((
            (lax.max(t - k, 0), z_next, (t < 7) & (t >= k)),
            (lax.min(t + k, 7), z_prev, (t > 0) & (t + k <= 7)),
        )):
            piece = x_buf.at[unit, rows[b]]
            launch(remote(piece, piece, tok_send.at[way, k, b], tok_recv.at[way, k, b], peer), condition)

    def token_wait(k, b):
        for way, (unit, condition) in enumerate((
            (lax.max(t - 1 - k, 0), t - 1 >= k),
            (lax.min(t + 1 + k, 7), t + 1 + k <= 7),
        )):
            piece = x_buf.at[unit, rows[b]]

            @pl.when(condition)
            def _():
                remote(piece, piece, tok_send.at[way, k, b], tok_recv.at[way, k, b], z_next).wait_recv()

    def token_step(k, b):
        token_wait(k, b)
        token_send(k + 1, b)

    halves = (pl.ds(0, 64), pl.ds(64, 64))
    lines = (y, wrap(y - 1), wrap(y + 1), wrap(y + 2))

    def block(g, phase, shift):
        source = f if g == 0 else 1 - f
        if phase == 0:
            return w_buf.at[source, x, wrap(y + shift)]
        return w_buf.at[source, wrap(x + shift), lines[phase - 1]]

    def axis(phase):
        return "y" if phase == 0 else "x"

    def w_copy(g, phase, kind, piece):
        peer = (nexts if kind % 2 == 0 else prevs)[axis(phase)]
        return remote(piece, piece, w_send.at[g, phase, kind], w_recv.at[g, phase, kind], peer)

    def w_start(g, phase):
        for kind in range(2):
            launch(w_copy(g, phase, kind, block(g, phase, 0)))

    def w_forward(g, phase):
        for kind, shift in ((0, -1), (1, 1)):
            w_copy(g, phase, kind, block(g, phase, shift)).wait_recv()
            launch(w_copy(g, phase, 2 + kind, block(g, phase, shift).at[halves[kind]]))

    def w_finish(g, phase):
        for kind in range(2):
            w_copy(g, phase, 2 + kind, block(g, phase, 2).at[halves[kind]]).wait_recv()

    pair = remote(stage, x_buf.at[t, rows[0]], pair_send, pair_recv, sibling)
    launch(pair)
    token_send(0, 0)
    own.wait()
    w_start(0, 0)
    w_start(0, 1)
    for kind, peer in ((0, z_up), (1, z_down)):
        launch(remote(w_buf.at[f, x, y, halves[kind]], relay.at[kind], fx_send.at[0, kind], fx_recv.at[0, kind], peer))
    remote(stage, x_buf.at[t, rows[1]], pair_send, pair_recv, sibling).wait_recv()
    token_send(0, 1)

    w_forward(0, 0)
    w_start(0, 2)
    token_step(0, 0)
    w_forward(0, 1)
    w_start(0, 3)
    for kind, (peer, source) in enumerate(((z_up, f_down), (z_down, f_up))):
        remote(relay.at[kind], relay.at[kind], fx_send.at[0, kind], fx_recv.at[0, kind], peer).wait_recv()
        launch(remote(relay.at[kind], w_buf.at[source, x, y, halves[kind]], fx_send.at[1, kind], fx_recv.at[1, kind], peer))
    w_finish(0, 0)
    w_start(0, 4)
    token_step(0, 1)
    w_forward(0, 2)
    token_step(1, 0)
    for kind, peer in ((0, z_up), (1, z_down)):
        there = w_buf.at[1 - f, x, y, halves[kind]]
        remote(relay.at[kind], there, fx_send.at[1, kind], fx_recv.at[1, kind], peer).wait_recv()
    w_start(1, 0)
    w_start(1, 1)
    w_forward(0, 3)
    token_step(1, 1)
    w_forward(1, 0)
    w_start(1, 2)
    w_forward(0, 4)
    token_step(2, 0)
    w_start(1, 3)
    w_finish(1, 0)
    w_start(1, 4)
    token_step(2, 1)
    w_forward(1, 1)
    token_step(3, 0)
    w_forward(1, 2)
    token_step(3, 1)
    token_step(4, 0)
    w_forward(1, 3)
    token_step(4, 1)
    w_forward(1, 4)
    token_step(5, 0)
    token_step(5, 1)
    for g in range(2):
        for phase in range(1, 5):
            w_finish(g, phase)

    def multiply(first, count, kind):
        for start in range(0, WIDTH, 256):
            stop = min(start + 256, WIDTH)
            weight = w_buf[:, :, :, :, start:stop].reshape(4096, stop - start)
            units = x_buf[pl.ds(first, count)].reshape(count * 64, 4096)
            product = jnp.dot(units, weight, preferred_element_type=jnp.float32)
            part[pl.ds(first, count), :, :, start:stop] = product.reshape(count, 2, ROWS, stop - start)
        swap = remote(
            part.at[pl.ds(first, count), 1 - core], other.at[pl.ds(first, count)],
            ex_send.at[kind], ex_recv.at[kind], sibling,
        )
        launch(swap)
        return swap

    low = t < 4
    near = multiply(jnp.where(low, 0, 2), 6, 0)
    token_wait(6, 0)
    token_wait(6, 1)
    far = multiply(jnp.where(low, 6, 0), 2, 1)
    near.wait_recv()
    far.wait_recv()
    for unit in (7, 0, 1, 2, 3, 4, 5, 6):
        total = part[unit, core] + other[unit]
        narrow = total[:, :768].astype(jnp.bfloat16)
        padded[16 + unit * ROWS:16 + (unit + 1) * ROWS, :] = narrow.astype(jnp.float32)
        dt_buf[unit * ROWS:(unit + 1) * ROWS, :] = total[:, 768:]
        if unit == 7:
            edge[0] = narrow[16:, :]
            launch(remote(edge.at[0], edge.at[1], halo_send, halo_recv, seq_next), s < 31)

    lane = lax.broadcasted_iota(jnp.int32, (1, 128), 1)

    def row_of(ref):
        row = jnp.zeros((1, 128), jnp.float32)
        for head in range(8):
            row = jnp.where(lane == head, ref[head], row)
        return row

    step = softplus(dt_buf[...] + row_of(bias_ref))
    rise = -step * row_of(rate_ref)
    down_to = lax.broadcasted_iota(jnp.int32, (SPAN, SPAN), 0)
    across = lax.broadcasted_iota(jnp.int32, (SPAN, SPAN), 1)
    causal = across <= down_to
    triangle = jnp.where(causal, 1.0, 0.0).astype(jnp.float32)
    steps, cums, step_rows, cum_rows, lasts = [], [], [], [], []
    for b in range(2):
        here = slice(b * SPAN, (b + 1) * SPAN)
        cum = jnp.dot(
            triangle, rise[here], precision=lax.Precision.HIGHEST, preferred_element_type=jnp.float32
        )
        steps.append(step[here])
        cums.append(cum)
        step_rows.append(step[here].T)
        cum_rows.append(cum.T)
        lasts.append(cum[SPAN - 1:, :])

    @pl.when(s > 0)
    def _():
        remote(edge.at[0], edge.at[1], halo_send, halo_recv, seq_next).wait_recv()
        padded[:16, :] = edge[1].astype(jnp.float32)

    @pl.when(s == 0)
    def _():
        padded[:16, :] = jnp.zeros((16, 768), jnp.float32)

    for tile in range(6):
        columns = slice(tile * 128, (tile + 1) * 128)
        gained = None
        for tap in range(CONV):
            if tile < 4:
                gain = conv_x_ref[tap:tap + 1, columns]
            else:
                gain = conv_bc_ref[tap, tile - 4:tile - 3, :]
            term = gain * padded[13 + tap:13 + tap + 256, columns]
            gained = term if gained is None else gained + term
        smooth = (gained * (1.0 / (1.0 + jnp.exp(-gained)))).astype(jnp.bfloat16)
        if tile < 4:
            values[:, columns] = smooth
        elif tile == 4:
            keys[...] = smooth
        else:
            reads[...] = smooth

    for b in range(2):
        here = slice(b * SPAN, (b + 1) * SPAN)
        factor = expand(jnp.exp(lasts[b] - cums[b]) * steps[b])
        scaled = (values[here, :].astype(jnp.float32) * factor).astype(jnp.bfloat16)
        states[b] = lax.dot_general(
            keys[here, :], scaled, (((0,), (0,)), ((), ())), preferred_element_type=jnp.float32
        )
    fades = [expand(jnp.exp(last)) for last in lasts]
    range_state = fades[1] * states[0] + states[1]
    range_decay = jnp.broadcast_to(fades[0] * fades[1], (8, 512))

    for side in range(2):
        half = slice(side * 256, (side + 1) * 256)
        give_state[side] = range_state[:, half].astype(jnp.bfloat16)
        give_decay[side] = range_decay[:, half]
    launch(remote(give_state.at[1 - core], pair_state, p1_send.at[0], p1_recv.at[0], sibling))
    launch(remote(give_decay.at[1 - core], pair_decay, p1_send.at[1], p1_recv.at[1], sibling))

    def inside(b):
        here = slice(b * SPAN, (b + 1) * SPAN)
        scores = lax.dot_general(
            reads[here, :], keys[here, :], (((1,), (1,)), ((), ())), preferred_element_type=jnp.float32
        )
        masked = jnp.where(causal, scores, 0.0)
        for pair_at in range(4):
            both = []
            for head in (2 * pair_at, 2 * pair_at + 1):
                gap = cums[b][:, head:head + 1] - cum_rows[b][head:head + 1, :]
                weight = masked * jnp.exp(jnp.minimum(gap, 0.0)) * step_rows[b][head:head + 1, :]
                both.append(jnp.dot(
                    weight.astype(jnp.bfloat16), values[here, head * P_SIZE:(head + 1) * P_SIZE],
                    preferred_element_type=jnp.float32,
                ))
            inner[here, pair_at * 128:(pair_at + 1) * 128] = jnp.concatenate(both, axis=1)

    remote(give_state.at[1 - core], pair_state, p1_send.at[0], p1_recv.at[0], sibling).wait_recv()
    remote(give_decay.at[1 - core], pair_decay, p1_send.at[1], p1_recv.at[1], sibling).wait_recv()
    first = core == 0
    near_state, near_decay = give_state[core].astype(jnp.float32), give_decay[core][:1]
    far_state, far_decay = pair_state[...].astype(jnp.float32), pair_decay[:1]
    state_0, decay_0 = jnp.where(first, near_state, far_state), jnp.where(first, near_decay, far_decay)
    state_1, decay_1 = jnp.where(first, far_state, near_state), jnp.where(first, far_decay, near_decay)

    def level(which, slots, decays, mine, state, decay, peers):
        slots[mine] = state.astype(jnp.bfloat16)
        decays[mine] = jnp.broadcast_to(decay, (8, 256))
        for shift, peer in enumerate(peers):
            launch(remote(slots.at[mine], slots.at[mine], p2_send.at[which, 0, shift], p2_recv.at[which, 0, shift], peer))
            launch(remote(decays.at[mine], decays.at[mine], p2_send.at[which, 1, shift], p2_recv.at[which, 1, shift], peer))

    def gather(which, slots, decays, mine, peers):
        for shift, peer in enumerate(peers):
            there = wrap(mine - 1 - shift)
            remote(slots.at[there], slots.at[there], p2_send.at[which, 0, shift], p2_recv.at[which, 0, shift], peer).wait_recv()
            remote(decays.at[there], decays.at[there], p2_send.at[which, 1, shift], p2_recv.at[which, 1, shift], peer).wait_recv()
        state, decay = jnp.zeros((N, 256), jnp.float32), jnp.ones((1, 256), jnp.float32)
        before, before_decay = state, decay
        for member in range(4):
            before = jnp.where(mine == member, state, before)
            before_decay = jnp.where(mine == member, decay, before_decay)
            fade = decays[member][:1]
            state = fade * state + slots[member].astype(jnp.float32)
            decay = decay * fade
        return before, before_decay, state, decay

    y_peers = [nexts["y"], y_far, prevs["y"]]
    x_peers = [nexts["x"], x_far, prevs["x"]]
    level(0, y_state, y_decay, y, decay_1 * state_0 + state_1, decay_0 * decay_1, y_peers)
    inside(0)
    before_y, before_y_decay, row_state, row_decay = gather(0, y_state, y_decay, y, y_peers)
    level(1, x_state, x_decay, x, row_state, row_decay, x_peers)
    inside(1)
    before_x, _, _, _ = gather(1, x_state, x_decay, x, x_peers)
    into_0 = before_y_decay * before_x + before_y
    into_1 = decay_0 * into_0 + state_0
    outflow[...] = jnp.where(first, into_1, into_0).astype(jnp.bfloat16)
    launch(remote(outflow, inflow.at[core], p4_send, p4_recv, sibling))
    inflow[core] = jnp.where(first, into_0, into_1).astype(jnp.bfloat16)
    remote(outflow, inflow.at[1 - core], p4_send, p4_recv, sibling).wait_recv()
    entering = jnp.concatenate([inflow[0], inflow[1]], axis=1)
    skips = expand(row_of(skip_ref))
    for b in range(2):
        here = slice(b * SPAN, (b + 1) * SPAN)
        outer = jnp.dot(reads[here, :], entering, preferred_element_type=jnp.float32)
        outer = expand(jnp.exp(cums[b])) * outer
        result = inner[here, :] + outer + skips * values[here, :].astype(jnp.float32)
        out_ref[here, :] = result.astype(jnp.bfloat16)
        if b == 0:
            entering = (fades[0] * entering.astype(jnp.float32) + states[0]).astype(jnp.bfloat16)
    for copy, condition in sends:
        if condition is None:
            copy.wait_send()
        else:
            pl.when(condition)(copy.wait_send)


def layer(tokens, weight, conv_x, conv_bc, bias, rate, skip):
    vmem = pl.BlockSpec(memory_space=pltpu.VMEM)
    smem = pl.BlockSpec(memory_space=pltpu.SMEM)
    dma = pltpu.SemaphoreType.DMA
    bf16, f32 = jnp.bfloat16, jnp.float32
    return pl.pallas_call(
        layer_kernel,
        out_shape=jax.ShapeDtypeStruct((256, 512), bf16),
        in_specs=[vmem, vmem, vmem, vmem, smem, smem, smem],
        out_specs=vmem,
        scratch_shapes=[
            pltpu.VMEM((8, 2 * ROWS, 4096), bf16),
            pltpu.VMEM((2, 4, 4, 128, WIDTH), bf16),
            pltpu.VMEM((ROWS, 4096), bf16),
            pltpu.VMEM((2, 64, WIDTH), bf16),
            pltpu.VMEM((8, 2, ROWS, WIDTH), f32),
            pltpu.VMEM((8, ROWS, WIDTH), f32),
            pltpu.VMEM((16 + 256, 768), f32),
            pltpu.VMEM((2, 16, 768), bf16),
            pltpu.VMEM((256, 512), bf16),
            pltpu.VMEM((256, N), bf16),
            pltpu.VMEM((256, N), bf16),
            pltpu.VMEM((256, 512), f32),
            pltpu.VMEM((2, N, 512), f32),
            pltpu.VMEM((N, 256), bf16),
            pltpu.VMEM((8, 256), f32),
            pltpu.VMEM((4, N, 256), bf16),
            pltpu.VMEM((4, 8, 256), f32),
            pltpu.VMEM((4, N, 256), bf16),
            pltpu.VMEM((4, 8, 256), f32),
            pltpu.VMEM((2, N, 256), bf16),
            pltpu.VMEM((2, 8, 256), f32),
            pltpu.VMEM((2, N, 256), bf16),
            pltpu.VMEM((N, 256), bf16),
            pltpu.VMEM((256, 128), f32),
            dma((2, 7, 2)), dma((2, 7, 2)), dma(()), dma(()),
            dma((2, 5, 4)), dma((2, 5, 4)), dma((2, 2)), dma((2, 2)), dma((2,)), dma((2,)), dma(()),
            dma(()), dma(()), dma((2,)), dma((2,)), dma((2, 2, 3)), dma((2, 2, 3)), dma(()), dma(()),
        ],
        compiler_params=pltpu.CompilerParams(
            collective_id=0, has_side_effects=True, vmem_limit_bytes=56 * 2**20
        ),
        name="layer",
    )(tokens, weight, conv_x, conv_bc, bias, rate, skip)


def body(
    tokens,
    proj_mean,
    proj_devs,
    bc_mean,
    bc_devs,
    swag_coef,
    dt_weight,
    dt_bias,
    decay_rate,
    skip_gain,
    conv_proj,
    conv_bc,
):
    weight_x = sampled(proj_mean, proj_devs, swag_coef)
    weight_bc = sampled(bc_mean, bc_devs, swag_coef).reshape(128, 256)
    padding = jnp.zeros((128, WIDTH - 768 - 8), jnp.bfloat16)
    weight = jnp.concatenate([weight_x, weight_bc, dt_weight, padding], axis=1)
    return layer(tokens, weight, conv_proj, conv_bc, dt_bias, decay_rate, skip_gain)


def solution(mesh):
    return jax.shard_map(
        body,
        mesh=mesh,
        in_specs=(
            P(("fsdp", "seq", "tp"), None),
            P(("fsdp", "seq"), "tp"),
            P(None, ("fsdp", "seq"), "tp"),
            P(("fsdp", "seq"), None, "tp"),
            P(None, ("fsdp", "seq"), None, "tp"),
            P(),
            P(("fsdp", "seq"), "tp"),
            P("tp"),
            P("tp"),
            P("tp"),
            P(None, "tp"),
            P(None, None, "tp"),
        ),
        out_specs=P(("fsdp", "seq"), "tp"),
        check_vma=False,
    )
```

```python
import jax
import jax.numpy as jnp
from jax import lax
from jax.experimental import pallas as pl
from jax.experimental.pallas import tpu as pltpu
from jax.sharding import PartitionSpec as P

P_SIZE = 64
N = 128
CONV = 4
SPAN = 128
MESH = pl.DeviceIdType.MESH
SHARE = 112
ROWS = 32


def sampled(mean_part, dev_part, swag_coef):
    factor = (2.0 * (dev_part.shape[0] - 1)) ** (-0.5)
    accum = mean_part.astype(jnp.float32)
    for member in range(dev_part.shape[0]):
        accum = accum + factor * swag_coef[member] * dev_part[member].astype(jnp.float32)
    return accum.astype(jnp.bfloat16)


def expand(heads):
    lane = lax.broadcasted_iota(jnp.int32, (heads.shape[0], 128), 1)
    return jnp.concatenate(
        [jnp.where(lane < P_SIZE, heads[:, 2 * j:2 * j + 1], heads[:, 2 * j + 1:2 * j + 2]) for j in range(4)],
        axis=1,
    )


def softplus(value):
    small = jnp.exp(-jnp.abs(value))
    series = small * (1.0 - small * (0.5 - small * (1.0 / 3.0 - small * 0.25)))
    return jnp.maximum(value, 0.0) + jnp.where(small < 0.01, series, jnp.log(1.0 + small))


def fold(tile):
    lane = lax.broadcasted_iota(jnp.int32, tile.shape, 1)
    joined = jnp.where(lane == 96, tile + pltpu.roll(tile, 127, 1), tile)
    return jnp.where(lane == 97, 0.0, joined)


def pack(tile):
    lane = lax.broadcasted_iota(jnp.int32, tile.shape, 1)
    high = tile.astype(jnp.bfloat16).astype(jnp.float32)
    low = pltpu.roll(tile - high, 1, 1)
    return jnp.where(lane == 97, low, high).astype(jnp.bfloat16)


def layer_kernel(
    tok_ref, w_ref, conv_x_ref, conv_bc_ref, bias_ref, rate_ref, skip_ref, out_ref,
    x_buf, ring, rs_out, rs_own, rs_in, z_out, z_in, y_in, padded, edge, values, keys, reads, inner, states,
    pair_state, pair_decay, y_state, y_decay, x_state, x_decay, give_state, give_decay, inflow, outflow, dt_buf,
    own_sem, p_send, p_recv, a_send, a_recv, u_send, u_recv, c_send, c_recv, r_send, r_recv, rs_send, rs_recv,
    z_send, z_recv, y_send, y_recv,
    halo_send, halo_recv, p1_send, p1_recv, p2_send, p2_recv, p4_send, p4_recv,
):
    f = lax.axis_index("fsdp")
    s = lax.axis_index("seq")
    t = lax.axis_index("tp")
    q = lax.rem(s, 8)
    x = lax.div(s, 8)
    core = lax.rem(s, 2)
    y = lax.div(q, 2)
    z = f * 8 + t

    def wrap(value):
        return lax.rem(value + 4, 4)

    def place(x_at, y_at, core_at):
        return (f, x_at * 8 + y_at * 2 + core_at, t)

    def plane(z_at):
        z_at = lax.rem(z_at + 16, 16)
        return (lax.div(z_at, 8), s, lax.rem(z_at, 8))

    sibling = place(x, y, 1 - core)
    y_next, y_far, y_prev = (place(x, wrap(y + by), core) for by in (1, 2, 3))
    x_next, x_far, x_prev = (place(wrap(x + by), y, core) for by in (1, 2, 3))
    z_next, z_prev = plane(z + 1), plane(z - 1)
    q_at = [lax.rem(q + 1 + i, 8) for i in range(7)]
    q_peers = [(f, x * 8 + at, t) for at in q_at]
    t_at = [lax.rem(t + by, 8) for by in range(8)]
    t_peers = [(f, s, at) for at in t_at]
    seq_next, seq_prev = (f, lax.min(s + 1, 31), t), (f, lax.max(s - 1, 0), t)

    barrier = pltpu.get_barrier_semaphore()
    for peer in (x_next, x_far, x_prev, z_next, z_prev, *q_peers, *t_peers[1:]):
        pl.semaphore_signal(barrier, inc=1, device_id=peer, device_id_type=MESH)

    @pl.when(s < 31)
    def _():
        pl.semaphore_signal(barrier, inc=1, device_id=seq_next, device_id_type=MESH)

    @pl.when(s > 0)
    def _():
        pl.semaphore_signal(barrier, inc=1, device_id=seq_prev, device_id_type=MESH)

    sends = []

    def remote(src, dst, send_sem, recv_sem, peer):
        return pltpu.make_async_remote_copy(
            src_ref=src, dst_ref=dst, send_sem=send_sem, recv_sem=recv_sem,
            device_id=peer, device_id_type=MESH,
        )

    def launch(copy, condition=None):
        if condition is None:
            copy.start()
        else:
            pl.when(condition)(copy.start)
        sends.append((copy, condition))

    def token_columns(half, x_at):
        return tok_ref.at[:, pl.ds(pl.multiple_of(half * 4096 + x_at * 1024, 1024), 1024)]

    def token_place(half, x_at, q_here):
        return x_buf.at[x_at, q_here, :, pl.ds(half * 1024, 1024)]

    locals_ = [
        pltpu.make_async_copy(token_columns(half, x), token_place(half, x, q), own_sem.at[half]) for half in range(2)
    ]
    lanes = pl.ds(pl.multiple_of(q * 128, 128), 128)
    locals_.append(pltpu.make_async_copy(w_ref.at[q], ring.at[z, :, lanes], own_sem.at[2]))
    for copy in locals_:
        copy.start()
    pl.semaphore_wait(barrier, 19 + jnp.where(s > 0, 1, 0) + jnp.where(s < 31, 1, 0))

    for i in range(7):
        launch(remote(w_ref.at[q_at[i]], ring.at[z, :, lanes], p_send.at[i], p_recv.at[i], q_peers[i]))
    for i, peer in enumerate((x_next, x_far, x_prev)):
        for half in range(2):
            launch(remote(
                token_columns(half, wrap(x + 1 + i)), token_place(half, x, q), a_send.at[i, half], a_recv.at[i, half], peer
            ))

    pieces = (pl.ds(0, 48), pl.ds(48, 64))

    def ring_copy(way, k, b, slot):
        piece = ring.at[lax.rem(slot + 32, 16), pieces[b]]
        return remote(piece, piece, r_send.at[way, k, b], r_recv.at[way, k, b], z_next if way == 0 else z_prev)

    def ring_send(k, b):
        for way in range(2):
            if k < 7 or way == b:
                launch(ring_copy(way, k, b, z - k if way == 0 else z + k))

    def ring_wait(k, b):
        for way in range(2):
            if k < 7 or way == b:
                ring_copy(way, k, b, z - 1 - k if way == 0 else z + 1 + k).wait_recv()

    def ring_step(k):
        for b in range(2):
            ring_wait(k, b)
            ring_send(k + 1, b)

    for i in range(7):
        from_q = pl.ds(pl.multiple_of(lax.rem(q + 7 - i, 8) * 128, 128), 128)
        remote(w_ref.at[q_at[i]], ring.at[z, :, from_q], p_send.at[i], p_recv.at[i], q_peers[i]).wait_recv()
    for copy in locals_:
        copy.wait()
    ring_send(0, 0)
    ring_send(0, 1)
    for i, peer in enumerate((x_next, x_far, x_prev)):
        for half in range(2):
            here = token_place(half, wrap(x - 1 - i), q)
            remote(here, here, a_send.at[i, half], a_recv.at[i, half], peer).wait_recv()

    def unit(y_by, core_at, part=None):
        member = wrap(y + y_by) * 2 + core_at
        return x_buf.at[:, member] if part is None else x_buf.at[pl.ds(2 * part, 2), member]

    def unit_copy(kind, piece):
        return remote(piece, piece, u_send.at[kind], u_recv.at[kind], y_next if kind % 2 == 0 else y_prev)

    def share(index, y_by):
        launch(remote(unit(y_by, core), unit(y_by, core), c_send.at[index], c_recv.at[index], sibling))

    launch(unit_copy(0, unit(0, core)))
    launch(unit_copy(1, unit(0, core)))
    share(0, 0)
    ring_step(0)
    ring_step(1)
    ring_step(2)
    for kind, y_by in ((0, -1), (1, 1)):
        unit_copy(kind, unit(y_by, core)).wait_recv()
        launch(unit_copy(2 + kind, unit(y_by, core, kind)))
        share(1 + kind, y_by)
    ring_step(3)
    for kind in range(2):
        unit_copy(2 + kind, unit(2, core, kind)).wait_recv()
    share(3, 2)
    ring_step(4)
    for index, y_by in enumerate((0, -1, 1, 2)):
        here = unit(y_by, 1 - core)
        remote(here, here, c_send.at[index], c_recv.at[index], sibling).wait_recv()

    def multiply(by):
        tau = t_at[by]
        for owner in range(4):
            total = jnp.zeros((256, SHARE), jnp.float32)
            for half in range(2):
                total = total + lax.dot_general(
                    x_buf[owner, :, :, half * 1024:(half + 1) * 1024].reshape(256, 1024), ring[tau + 8 * half],
                    (((1,), (1,)), ((), ())), preferred_element_type=jnp.float32,
                )
            total = jnp.concatenate([total, jnp.zeros((256, 128 - SHARE), jnp.float32)], axis=1)
            rs_out[by, owner] = pack(total)

            @pl.when(x == owner)
            def _():
                rs_own[by] = total

        for i, peer in enumerate((x_next, x_far, x_prev)):
            launch(remote(rs_out.at[by, wrap(x + 1 + i)], rs_in.at[by, i], rs_send.at[by, i], rs_recv.at[by, i], peer))

    def settle(by):
        total = rs_own[by]
        for i, peer in enumerate((x_next, x_far, x_prev)):
            remote(rs_in.at[by, i], rs_in.at[by, i], rs_send.at[by, i], rs_recv.at[by, i], peer).wait_recv()
            total = total + rs_in[by, i].astype(jnp.float32)
        packed = pack(fold(total))
        if by == 0:
            z_in[t] = packed
        else:
            z_out[by] = packed
            launch(remote(z_out.at[by], z_in.at[t], z_send.at[by], z_recv.at[by], t_peers[by]))

    multiply(4)
    ring_step(5)
    multiply(3)
    multiply(5)
    settle(4)
    ring_step(6)
    multiply(2)
    multiply(6)
    settle(3)
    settle(5)
    multiply(1)
    multiply(7)
    settle(2)
    settle(6)
    ring_wait(7, 0)
    ring_wait(7, 1)
    multiply(0)
    settle(1)
    settle(7)
    settle(0)
    for by in range(1, 8):
        here = z_in.at[lax.rem(t + 8 - by, 8)]
        remote(here, here, z_send.at[by], z_recv.at[by], t_peers[by]).wait_recv()
    mine = pltpu.make_async_copy(z_in.at[:, pl.ds(pl.multiple_of(q * ROWS, ROWS), ROWS)], y_in.at[q], own_sem.at[0])
    mine.start()
    for i in range(7):
        piece = z_in.at[:, pl.ds(pl.multiple_of(q_at[i] * ROWS, ROWS), ROWS)]
        launch(remote(piece, y_in.at[q], y_send.at[i], y_recv.at[i], q_peers[i]))
    mine.wait()
    for i in range(7):
        here = y_in.at[lax.rem(q + 7 - i, 8)]
        remote(here, here, y_send.at[i], y_recv.at[i], q_peers[i]).wait_recv()

    lane = lax.broadcasted_iota(jnp.int32, (1, 128), 1)
    tiles = [y_in[g].reshape(256, 128).astype(jnp.float32) for g in range(8)]
    for pair_at in range(4):
        both = [tiles[2 * pair_at][:, :P_SIZE], tiles[2 * pair_at + 1][:, :P_SIZE]]
        padded[16:, pair_at * 128:(pair_at + 1) * 128] = jnp.concatenate(both, axis=1)
    padded[16:, 512:640] = jnp.concatenate([tile[:, 64:80] for tile in tiles], axis=1)
    padded[16:, 640:768] = jnp.concatenate([tile[:, 80:96] for tile in tiles], axis=1)
    edge[0] = padded[256:272, :].astype(jnp.bfloat16)
    launch(remote(edge.at[0], edge.at[1], halo_send, halo_recv, seq_next), s < 31)
    logits = jnp.zeros((256, 128), jnp.float32)
    for g in range(8):
        logits = jnp.where(lane == g, tiles[g][:, 96:97] + tiles[g][:, 97:98], logits)
    dt_buf[...] = logits

    def row_of(ref):
        row = jnp.zeros((1, 128), jnp.float32)
        for head in range(8):
            row = jnp.where(lane == head, ref[head], row)
        return row

    step = softplus(dt_buf[...] + row_of(bias_ref))
    rise = -step * row_of(rate_ref)
    down_to = lax.broadcasted_iota(jnp.int32, (SPAN, SPAN), 0)
    across = lax.broadcasted_iota(jnp.int32, (SPAN, SPAN), 1)
    causal = across <= down_to
    triangle = jnp.where(causal, 1.0, 0.0).astype(jnp.float32)
    steps, cums, step_rows, cum_rows, lasts = [], [], [], [], []
    for b in range(2):
        here = slice(b * SPAN, (b + 1) * SPAN)
        cum = jnp.dot(
            triangle, rise[here], precision=lax.Precision.HIGHEST, preferred_element_type=jnp.float32
        )
        steps.append(step[here])
        cums.append(cum)
        step_rows.append(step[here].T)
        cum_rows.append(cum.T)
        lasts.append(cum[SPAN - 1:, :])

    @pl.when(s > 0)
    def _():
        remote(edge.at[0], edge.at[1], halo_send, halo_recv, seq_next).wait_recv()
        padded[:16, :] = edge[1].astype(jnp.float32)

    @pl.when(s == 0)
    def _():
        padded[:16, :] = jnp.zeros((16, 768), jnp.float32)

    for tile in range(6):
        columns = slice(tile * 128, (tile + 1) * 128)
        gained = None
        for tap in range(CONV):
            if tile < 4:
                gain = conv_x_ref[tap:tap + 1, columns]
            else:
                gain = conv_bc_ref[tap, tile - 4:tile - 3, :]
            term = gain * padded[13 + tap:13 + tap + 256, columns]
            gained = term if gained is None else gained + term
        smooth = (gained * (1.0 / (1.0 + jnp.exp(-gained)))).astype(jnp.bfloat16)
        if tile < 4:
            values[:, columns] = smooth
        elif tile == 4:
            keys[...] = smooth
        else:
            reads[...] = smooth

    for b in range(2):
        here = slice(b * SPAN, (b + 1) * SPAN)
        factor = expand(jnp.exp(lasts[b] - cums[b]) * steps[b])
        scaled = (values[here, :].astype(jnp.float32) * factor).astype(jnp.bfloat16)
        states[b] = lax.dot_general(
            keys[here, :], scaled, (((0,), (0,)), ((), ())), preferred_element_type=jnp.float32
        )
    fades = [expand(jnp.exp(last)) for last in lasts]
    range_state = fades[1] * states[0] + states[1]
    range_decay = jnp.broadcast_to(fades[0] * fades[1], (8, 512))

    for side in range(2):
        half = slice(side * 256, (side + 1) * 256)
        give_state[side] = range_state[:, half].astype(jnp.bfloat16)
        give_decay[side] = range_decay[:, half]
    launch(remote(give_state.at[1 - core], pair_state, p1_send.at[0], p1_recv.at[0], sibling))
    launch(remote(give_decay.at[1 - core], pair_decay, p1_send.at[1], p1_recv.at[1], sibling))

    def inside(b):
        here = slice(b * SPAN, (b + 1) * SPAN)
        scores = lax.dot_general(
            reads[here, :], keys[here, :], (((1,), (1,)), ((), ())), preferred_element_type=jnp.float32
        )
        masked = jnp.where(causal, scores, 0.0)
        for pair_at in range(4):
            both = []
            for head in (2 * pair_at, 2 * pair_at + 1):
                gap = cums[b][:, head:head + 1] - cum_rows[b][head:head + 1, :]
                weight = masked * jnp.exp(jnp.minimum(gap, 0.0)) * step_rows[b][head:head + 1, :]
                both.append(jnp.dot(
                    weight.astype(jnp.bfloat16), values[here, head * P_SIZE:(head + 1) * P_SIZE],
                    preferred_element_type=jnp.float32,
                ))
            inner[here, pair_at * 128:(pair_at + 1) * 128] = jnp.concatenate(both, axis=1)

    remote(give_state.at[1 - core], pair_state, p1_send.at[0], p1_recv.at[0], sibling).wait_recv()
    remote(give_decay.at[1 - core], pair_decay, p1_send.at[1], p1_recv.at[1], sibling).wait_recv()
    first = core == 0
    near_state, near_decay = give_state[core].astype(jnp.float32), give_decay[core][:1]
    far_state, far_decay = pair_state[...].astype(jnp.float32), pair_decay[:1]
    state_0, decay_0 = jnp.where(first, near_state, far_state), jnp.where(first, near_decay, far_decay)
    state_1, decay_1 = jnp.where(first, far_state, near_state), jnp.where(first, far_decay, near_decay)

    def level(which, slots, decays, mine, state, decay, peers):
        slots[mine] = state.astype(jnp.bfloat16)
        decays[mine] = jnp.broadcast_to(decay, (8, 256))
        for shift, peer in enumerate(peers):
            launch(remote(slots.at[mine], slots.at[mine], p2_send.at[which, 0, shift], p2_recv.at[which, 0, shift], peer))
            launch(remote(decays.at[mine], decays.at[mine], p2_send.at[which, 1, shift], p2_recv.at[which, 1, shift], peer))

    def gather(which, slots, decays, mine, peers):
        for shift, peer in enumerate(peers):
            there = wrap(mine - 1 - shift)
            remote(slots.at[there], slots.at[there], p2_send.at[which, 0, shift], p2_recv.at[which, 0, shift], peer).wait_recv()
            remote(decays.at[there], decays.at[there], p2_send.at[which, 1, shift], p2_recv.at[which, 1, shift], peer).wait_recv()
        state, decay = jnp.zeros((N, 256), jnp.float32), jnp.ones((1, 256), jnp.float32)
        before, before_decay = state, decay
        for member in range(4):
            before = jnp.where(mine == member, state, before)
            before_decay = jnp.where(mine == member, decay, before_decay)
            fade = decays[member][:1]
            state = fade * state + slots[member].astype(jnp.float32)
            decay = decay * fade
        return before, before_decay, state, decay

    y_peers = [y_next, y_far, y_prev]
    x_peers = [x_next, x_far, x_prev]
    level(0, y_state, y_decay, y, decay_1 * state_0 + state_1, decay_0 * decay_1, y_peers)
    inside(0)
    before_y, before_y_decay, row_state, row_decay = gather(0, y_state, y_decay, y, y_peers)
    level(1, x_state, x_decay, x, row_state, row_decay, x_peers)
    inside(1)
    before_x, _, _, _ = gather(1, x_state, x_decay, x, x_peers)
    into_0 = before_y_decay * before_x + before_y
    into_1 = decay_0 * into_0 + state_0
    outflow[...] = jnp.where(first, into_1, into_0).astype(jnp.bfloat16)
    launch(remote(outflow, inflow.at[core], p4_send, p4_recv, sibling))
    inflow[core] = jnp.where(first, into_0, into_1).astype(jnp.bfloat16)
    remote(outflow, inflow.at[1 - core], p4_send, p4_recv, sibling).wait_recv()
    entering = jnp.concatenate([inflow[0], inflow[1]], axis=1)
    skips = expand(row_of(skip_ref))
    for b in range(2):
        here = slice(b * SPAN, (b + 1) * SPAN)
        outer = jnp.dot(reads[here, :], entering, preferred_element_type=jnp.float32)
        outer = expand(jnp.exp(cums[b])) * outer
        result = inner[here, :] + outer + skips * values[here, :].astype(jnp.float32)
        out_ref[here, :] = result.astype(jnp.bfloat16)
        if b == 0:
            entering = (fades[0] * entering.astype(jnp.float32) + states[0]).astype(jnp.bfloat16)
    for copy, condition in sends:
        if condition is None:
            copy.wait_send()
        else:
            pl.when(condition)(copy.wait_send)


def layer(tokens, weight, conv_x, conv_bc, bias, rate, skip):
    vmem = pl.BlockSpec(memory_space=pltpu.VMEM)
    smem = pl.BlockSpec(memory_space=pltpu.SMEM)
    dma = pltpu.SemaphoreType.DMA
    bf16, f32 = jnp.bfloat16, jnp.float32
    return pl.pallas_call(
        layer_kernel,
        out_shape=jax.ShapeDtypeStruct((256, 512), bf16),
        in_specs=[vmem, vmem, vmem, vmem, smem, smem, smem],
        out_specs=vmem,
        scratch_shapes=[
            pltpu.VMEM((4, 8, ROWS, 2048), bf16),
            pltpu.VMEM((16, SHARE, 1024), bf16),
            pltpu.VMEM((8, 4, 256, 128), bf16),
            pltpu.VMEM((8, 256, 128), f32),
            pltpu.VMEM((8, 3, 256, 128), bf16),
            pltpu.VMEM((8, 256, 128), bf16),
            pltpu.VMEM((8, 256, 128), bf16),
            pltpu.VMEM((8, 8, ROWS, 128), bf16),
            pltpu.VMEM((16 + 256, 768), f32),
            pltpu.VMEM((2, 16, 768), bf16),
            pltpu.VMEM((256, 512), bf16),
            pltpu.VMEM((256, N), bf16),
            pltpu.VMEM((256, N), bf16),
            pltpu.VMEM((256, 512), f32),
            pltpu.VMEM((2, N, 512), f32),
            pltpu.VMEM((N, 256), bf16),
            pltpu.VMEM((8, 256), f32),
            pltpu.VMEM((4, N, 256), bf16),
            pltpu.VMEM((4, 8, 256), f32),
            pltpu.VMEM((4, N, 256), bf16),
            pltpu.VMEM((4, 8, 256), f32),
            pltpu.VMEM((2, N, 256), bf16),
            pltpu.VMEM((2, 8, 256), f32),
            pltpu.VMEM((2, N, 256), bf16),
            pltpu.VMEM((N, 256), bf16),
            pltpu.VMEM((256, 128), f32),
            dma((3,)), dma((7,)), dma((7,)), dma((3, 2)), dma((3, 2)), dma((4,)), dma((4,)), dma((4,)), dma((4,)),
            dma((2, 8, 2)), dma((2, 8, 2)), dma((8, 3)), dma((8, 3)), dma((8,)), dma((8,)), dma((7,)), dma((7,)),
            dma(()), dma(()), dma((2,)), dma((2,)), dma((2, 2, 3)), dma((2, 2, 3)), dma(()), dma(()),
        ],
        compiler_params=pltpu.CompilerParams(
            collective_id=0, has_side_effects=True, vmem_limit_bytes=56 * 2**20
        ),
        name="layer",
    )(tokens, weight, conv_x, conv_bc, bias, rate, skip)


def body(
    tokens,
    proj_mean,
    proj_devs,
    bc_mean,
    bc_devs,
    swag_coef,
    dt_weight,
    dt_bias,
    decay_rate,
    skip_gain,
    conv_proj,
    conv_bc,
):
    weight_x = sampled(proj_mean, proj_devs, swag_coef)
    weight_bc = sampled(bc_mean, bc_devs, swag_coef).reshape(128, 256)
    turned = weight_bc.T
    parts = [
        weight_x.T.reshape(8, 64, 128),
        turned[:128].reshape(8, 16, 128),
        turned[128:].reshape(8, 16, 128),
        jnp.pad(dt_weight.T[:, None, :], ((0, 0), (0, 15), (0, 0))),
    ]
    weight = jnp.concatenate(parts, axis=1)
    return layer(tokens, weight, conv_proj, conv_bc, dt_bias, decay_rate, skip_gain)


def solution(mesh):
    return jax.shard_map(
        body,
        mesh=mesh,
        in_specs=(
            P(("fsdp", "seq", "tp"), None),
            P(("fsdp", "seq"), "tp"),
            P(None, ("fsdp", "seq"), "tp"),
            P(("fsdp", "seq"), None, "tp"),
            P(None, ("fsdp", "seq"), None, "tp"),
            P(),
            P(("fsdp", "seq"), "tp"),
            P("tp"),
            P("tp"),
            P("tp"),
            P(None, "tp"),
            P(None, None, "tp"),
        ),
        out_specs=P(("fsdp", "seq"), "tp"),
        check_vma=False,
    )
```

```python
import jax
import jax.numpy as jnp
from jax import lax
from jax.experimental import pallas as pl
from jax.experimental.pallas import tpu as pltpu
from jax.sharding import PartitionSpec as P

P_SIZE = 64
N = 128
CONV = 4
SPAN = 128
MESH = pl.DeviceIdType.MESH
SHARE = 112
ROWS = 32
GROUPS_AT = (slice(0, 5), slice(5, 8))
ORDER = (4, 3, 5, 2, 6, 1, 7, 0)


def sampled(mean, devs, coef_ref):
    factor = (2.0 * (len(devs) - 1)) ** (-0.5)
    accum = mean.astype(jnp.float32)
    for member, dev in enumerate(devs):
        accum = accum + factor * coef_ref[member] * dev.astype(jnp.float32)
    return accum.astype(jnp.bfloat16)


def expand(heads):
    lane = lax.broadcasted_iota(jnp.int32, (heads.shape[0], 128), 1)
    return jnp.concatenate(
        [jnp.where(lane < P_SIZE, heads[:, 2 * j:2 * j + 1], heads[:, 2 * j + 1:2 * j + 2]) for j in range(4)],
        axis=1,
    )


def softplus(value):
    small = jnp.exp(-jnp.abs(value))
    series = small * (1.0 - small * (0.5 - small * (1.0 / 3.0 - small * 0.25)))
    return jnp.maximum(value, 0.0) + jnp.where(small < 0.01, series, jnp.log(1.0 + small))


def fold(tile):
    lane = lax.broadcasted_iota(jnp.int32, tile.shape, 1)
    joined = jnp.where((lane >= 96) & (lane < 104), tile + pltpu.roll(tile, 120, 1), tile)
    return jnp.where(lane >= 104, 0.0, joined)


def pack(tile):
    lane = lax.broadcasted_iota(jnp.int32, tile.shape, 1)
    high = tile.astype(jnp.bfloat16).astype(jnp.float32)
    low = pltpu.roll(tile - high, 8, 1)
    return jnp.where((lane >= 104) & (lane < 112), low, high).astype(jnp.bfloat16)


def layer_kernel(
    tok_ref, mean_ref, devs_ref, bc_mean_ref, bc_devs_ref, dt_ref, coef_ref, conv_x_ref, conv_bc_ref, bias_ref, rate_ref, skip_ref, out_ref,
    x_buf, w_ref, ring, rs_out, rs_own, rs_in, z_out, z_in, y_in, padded, edge, values, keys, reads, inner, states,
    pair_state, pair_decay, y_state, y_decay, x_state, x_decay, give_state, give_decay, inflow, outflow, dt_buf,
    own_sem, p_send, p_recv, a_send, a_recv, u_send, u_recv, c_send, c_recv, r_send, r_recv, rs_send, rs_recv,
    z_send, z_recv, y_send, y_recv,
    halo_send, halo_recv, p1_send, p1_recv, p2_send, p2_recv, p4_send, p4_recv,
):
    f = lax.axis_index("fsdp")
    s = lax.axis_index("seq")
    t = lax.axis_index("tp")
    q = lax.rem(s, 8)
    x = lax.div(s, 8)
    core = lax.rem(s, 2)
    y = lax.div(q, 2)
    z = f * 8 + t

    def wrap(value):
        return lax.rem(value + 4, 4)

    def place(x_at, y_at, core_at):
        return (f, x_at * 8 + y_at * 2 + core_at, t)

    def plane(z_at):
        z_at = lax.rem(z_at + 16, 16)
        return (lax.div(z_at, 8), s, lax.rem(z_at, 8))

    sibling = place(x, y, 1 - core)
    y_next, y_far, y_prev = (place(x, wrap(y + by), core) for by in (1, 2, 3))
    x_next, x_far, x_prev = (place(wrap(x + by), y, core) for by in (1, 2, 3))
    z_next, z_prev = plane(z + 1), plane(z - 1)
    q_at = [lax.rem(q + 1 + i, 8) for i in range(7)]
    q_peers = [(f, x * 8 + at, t) for at in q_at]
    t_at = [lax.rem(t + by, 8) for by in range(8)]
    t_peers = [(f, s, at) for at in t_at]
    seq_next, seq_prev = (f, lax.min(s + 1, 31), t), (f, lax.max(s - 1, 0), t)

    ring[:, 96:, :] = jnp.zeros((16, SHARE - 96, 1024), jnp.bfloat16)
    barrier = pltpu.get_barrier_semaphore()
    for peer in (x_next, x_far, x_prev, z_next, z_prev, *q_peers, *t_peers[1:]):
        pl.semaphore_signal(barrier, inc=1, device_id=peer, device_id_type=MESH)

    @pl.when(s < 31)
    def _():
        pl.semaphore_signal(barrier, inc=1, device_id=seq_next, device_id_type=MESH)

    @pl.when(s > 0)
    def _():
        pl.semaphore_signal(barrier, inc=1, device_id=seq_prev, device_id_type=MESH)

    sends = []

    def remote(src, dst, send_sem, recv_sem, peer):
        return pltpu.make_async_remote_copy(
            src_ref=src, dst_ref=dst, send_sem=send_sem, recv_sem=recv_sem,
            device_id=peer, device_id_type=MESH,
        )

    def launch(copy, condition=None):
        if condition is None:
            copy.start()
        else:
            pl.when(condition)(copy.start)
        sends.append((copy, condition))

    def token_columns(half, x_at):
        return tok_ref.at[:, pl.ds(pl.multiple_of(half * 4096 + x_at * 1024, 1024), 1024)]

    def token_place(half, x_at, q_here):
        return x_buf.at[x_at, q_here, :, pl.ds(half * 1024, 1024)]

    locals_ = [
        pltpu.make_async_copy(token_columns(half, x), token_place(half, x, q), own_sem.at[half]) for half in range(2)
    ]
    for copy in locals_:
        copy.start()
    for tile in range(4):
        columns = slice(tile * 128, (tile + 1) * 128)
        weight = sampled(mean_ref[:, columns], [devs_ref[m, :, columns] for m in range(4)], coef_ref)
        turned = weight.astype(jnp.float32).T.astype(jnp.bfloat16)
        w_ref[2 * tile, :64, :] = turned[:64]
        w_ref[2 * tile + 1, :64, :] = turned[64:]
    for kind in range(2):
        weight = sampled(bc_mean_ref[:, kind, :], [bc_devs_ref[m, :, kind, :] for m in range(4)], coef_ref)
        turned = weight.astype(jnp.float32).T.astype(jnp.bfloat16)
        for g in range(8):
            w_ref[g, 64 + 16 * kind:80 + 16 * kind, :] = turned[16 * g:16 * g + 16]
    dt_rows = jnp.concatenate([dt_ref[...].astype(jnp.float32), jnp.zeros((8, 128), jnp.float32)], axis=0)
    for g in range(8):
        w_ref[g, 96:, :] = dt_rows.astype(jnp.bfloat16)
    lanes = pl.ds(pl.multiple_of(q * 128, 128), 128)
    locals_.append(pltpu.make_async_copy(w_ref.at[q], ring.at[z, :, lanes], own_sem.at[2]))
    locals_[2].start()
    pl.semaphore_wait(barrier, 19 + jnp.where(s > 0, 1, 0) + jnp.where(s < 31, 1, 0))

    for i in range(7):
        launch(remote(w_ref.at[q_at[i]], ring.at[z, :, lanes], p_send.at[i], p_recv.at[i], q_peers[i]))
    for i, peer in enumerate((x_next, x_far, x_prev)):
        for half in range(2):
            launch(remote(
                token_columns(half, wrap(x + 1 + i)), token_place(half, x, q), a_send.at[i, half], a_recv.at[i, half], peer
            ))

    pieces = (pl.ds(0, 48), pl.ds(48, 48), pl.ds(96, 16))

    def ring_copy(way, k, b, slot):
        piece = ring.at[lax.rem(slot + 32, 16), pieces[b]]
        return remote(piece, piece, r_send.at[way, k, b], r_recv.at[way, k, b], z_next if way == 0 else z_prev)

    def steps_here(slot):
        return lax.rem(slot + 32, 8) == q

    def ring_send(k, b):
        for way in range(2):
            slot = z - k if way == 0 else z + k
            if k < 7 or way == b:
                launch(ring_copy(way, k, b, slot))
            if b == 1 and (k < 7 or way == 0):
                launch(ring_copy(way, k, 2, slot), steps_here(slot))

    def ring_wait(k, b):
        for way in range(2):
            slot = z - 1 - k if way == 0 else z + 1 + k
            if k < 7 or way == b:
                ring_copy(way, k, b, slot).wait_recv()
            if b == 1 and (k < 7 or way == 0):
                pl.when(steps_here(slot))(ring_copy(way, k, 2, slot).wait_recv)

    def ring_step(k):
        for b in range(2):
            ring_wait(k, b)
            ring_send(k + 1, b)

    for i in range(7):
        from_q = pl.ds(pl.multiple_of(lax.rem(q + 7 - i, 8) * 128, 128), 128)
        remote(w_ref.at[q_at[i]], ring.at[z, :, from_q], p_send.at[i], p_recv.at[i], q_peers[i]).wait_recv()
    for copy in locals_:
        copy.wait()
    ring_send(0, 0)
    ring_send(0, 1)
    for i, peer in enumerate((x_next, x_far, x_prev)):
        for half in range(2):
            here = token_place(half, wrap(x - 1 - i), q)
            remote(here, here, a_send.at[i, half], a_recv.at[i, half], peer).wait_recv()

    def unit(y_by, core_at, part=None):
        member = wrap(y + y_by) * 2 + core_at
        return x_buf.at[:, member] if part is None else x_buf.at[pl.ds(2 * part, 2), member]

    def unit_copy(kind, piece):
        return remote(piece, piece, u_send.at[kind], u_recv.at[kind], y_next if kind % 2 == 0 else y_prev)

    def share(index, y_by):
        launch(remote(unit(y_by, core), unit(y_by, core), c_send.at[index], c_recv.at[index], sibling))

    launch(unit_copy(0, unit(0, core)))
    launch(unit_copy(1, unit(0, core)))
    share(0, 0)
    ring_step(0)
    ring_step(1)
    ring_step(2)
    for kind, y_by in ((0, -1), (1, 1)):
        unit_copy(kind, unit(y_by, core)).wait_recv()
        launch(unit_copy(2 + kind, unit(y_by, core, kind)))
        share(1 + kind, y_by)
    ring_step(3)
    for kind in range(2):
        unit_copy(2 + kind, unit(2, core, kind)).wait_recv()
    share(3, 2)
    ring_step(4)
    for index, y_by in enumerate((0, -1, 1, 2)):
        here = unit(y_by, 1 - core)
        remote(here, here, c_send.at[index], c_recv.at[index], sibling).wait_recv()

    def multiply(by):
        tau = t_at[by]
        for owner in range(4):
            total = jnp.zeros((256, SHARE), jnp.float32)
            for half in range(2):
                total = total + lax.dot_general(
                    x_buf[owner, :, :, half * 1024:(half + 1) * 1024].reshape(256, 1024), ring[tau + 8 * half],
                    (((1,), (1,)), ((), ())), preferred_element_type=jnp.float32,
                )
            total = jnp.concatenate([total, jnp.zeros((256, 128 - SHARE), jnp.float32)], axis=1)
            rs_out[by, owner] = pack(total)

            @pl.when(x == owner)
            def _():
                rs_own[by] = total

        for i, peer in enumerate((x_next, x_far, x_prev)):
            launch(remote(rs_out.at[by, wrap(x + 1 + i)], rs_in.at[by, i], rs_send.at[by, i], rs_recv.at[by, i], peer))

    def settle(by):
        total = rs_own[by]
        for i, peer in enumerate((x_next, x_far, x_prev)):
            remote(rs_in.at[by, i], rs_in.at[by, i], rs_send.at[by, i], rs_recv.at[by, i], peer).wait_recv()
            total = total + rs_in[by, i].astype(jnp.float32)
        packed = pack(fold(total))
        if by == 0:
            z_in[ORDER.index(by)] = packed
        else:
            z_out[by] = packed
            launch(remote(z_out.at[by], z_in.at[ORDER.index(by)], z_send.at[by], z_recv.at[by], t_peers[by]))

    def spread_copy(group, i):
        slots = GROUPS_AT[group]
        owner = q if i == 7 else q_at[i]
        piece = z_in.at[slots, pl.ds(pl.multiple_of(owner * ROWS, ROWS), ROWS)]
        there = y_in.at[q, slots]
        if i == 7:
            return pltpu.make_async_copy(piece, there, own_sem.at[group])
        return remote(piece, there, y_send.at[group, i], y_recv.at[group, i], q_peers[i])

    def spread(group):
        for by in ORDER[GROUPS_AT[group]]:
            if by:
                here = z_in.at[ORDER.index(by)]
                remote(here, here, z_send.at[by], z_recv.at[by], t_peers[by]).wait_recv()
        spread_copy(group, 7).start()
        for i in range(7):
            launch(spread_copy(group, i))

    multiply(4)
    ring_step(5)
    multiply(3)
    multiply(5)
    settle(4)
    ring_step(6)
    multiply(2)
    multiply(6)
    settle(3)
    settle(5)
    multiply(1)
    multiply(7)
    settle(2)
    settle(6)
    ring_wait(7, 0)
    ring_wait(7, 1)
    multiply(0)
    settle(1)
    settle(7)
    settle(0)
    spread(0)
    spread(1)
    for group in range(2):
        spread_copy(group, 7).wait()
        for i in range(7):
            slots = GROUPS_AT[group]
            here = y_in.at[lax.rem(q + 7 - i, 8), slots]
            remote(here, here, y_send.at[group, i], y_recv.at[group, i], q_peers[i]).wait_recv()

    lane = lax.broadcasted_iota(jnp.int32, (1, 128), 1)
    for at, by in enumerate(ORDER):
        first_row = pl.multiple_of(lax.rem(t + 8 - by, 8) * ROWS, ROWS)
        rows = pl.ds(16 + first_row, ROWS)
        tiles = [y_in[g, at].astype(jnp.float32) for g in range(8)]
        for pair_at in range(4):
            both = [tiles[2 * pair_at][:, :P_SIZE], tiles[2 * pair_at + 1][:, :P_SIZE]]
            padded[rows, pair_at * 128:(pair_at + 1) * 128] = jnp.concatenate(both, axis=1)
        padded[rows, 512:640] = jnp.concatenate([tile[:, 64:80] for tile in tiles], axis=1)
        padded[rows, 640:768] = jnp.concatenate([tile[:, 80:96] for tile in tiles], axis=1)
        logits = y_in[t, at].astype(jnp.float32)
        dt_buf[pl.ds(first_row, ROWS), :] = pltpu.roll(logits, 32, 1) + pltpu.roll(logits, 24, 1)
    edge[0] = padded[256:272, :].astype(jnp.bfloat16)
    launch(remote(edge.at[0], edge.at[1], halo_send, halo_recv, seq_next), s < 31)

    def row_of(ref):
        row = jnp.zeros((1, 128), jnp.float32)
        for head in range(8):
            row = jnp.where(lane == head, ref[head], row)
        return row

    step = softplus(dt_buf[...] + row_of(bias_ref))
    rise = -step * row_of(rate_ref)
    down_to = lax.broadcasted_iota(jnp.int32, (SPAN, SPAN), 0)
    across = lax.broadcasted_iota(jnp.int32, (SPAN, SPAN), 1)
    causal = across <= down_to
    triangle = jnp.where(causal, 1.0, 0.0).astype(jnp.float32)
    steps, cums, step_rows, cum_rows, lasts = [], [], [], [], []
    for b in range(2):
        here = slice(b * SPAN, (b + 1) * SPAN)
        cum = jnp.dot(
            triangle, rise[here], precision=lax.Precision.HIGHEST, preferred_element_type=jnp.float32
        )
        steps.append(step[here])
        cums.append(cum)
        step_rows.append(step[here].T)
        cum_rows.append(cum.T)
        lasts.append(cum[SPAN - 1:, :])

    @pl.when(s > 0)
    def _():
        remote(edge.at[0], edge.at[1], halo_send, halo_recv, seq_next).wait_recv()
        padded[:16, :] = edge[1].astype(jnp.float32)

    @pl.when(s == 0)
    def _():
        padded[:16, :] = jnp.zeros((16, 768), jnp.float32)

    for tile in range(6):
        columns = slice(tile * 128, (tile + 1) * 128)
        gained = None
        for tap in range(CONV):
            if tile < 4:
                gain = conv_x_ref[tap:tap + 1, columns]
            else:
                gain = conv_bc_ref[tap, tile - 4:tile - 3, :]
            term = gain * padded[13 + tap:13 + tap + 256, columns]
            gained = term if gained is None else gained + term
        smooth = (gained * (1.0 / (1.0 + jnp.exp(-gained)))).astype(jnp.bfloat16)
        if tile < 4:
            values[:, columns] = smooth
        elif tile == 4:
            keys[...] = smooth
        else:
            reads[...] = smooth

    for b in range(2):
        here = slice(b * SPAN, (b + 1) * SPAN)
        factor = expand(jnp.exp(lasts[b] - cums[b]) * steps[b])
        scaled = (values[here, :].astype(jnp.float32) * factor).astype(jnp.bfloat16)
        states[b] = lax.dot_general(
            keys[here, :], scaled, (((0,), (0,)), ((), ())), preferred_element_type=jnp.float32
        )
    fades = [expand(jnp.exp(last)) for last in lasts]
    range_state = fades[1] * states[0] + states[1]
    range_decay = jnp.broadcast_to(fades[0] * fades[1], (8, 512))

    for side in range(2):
        half = slice(side * 256, (side + 1) * 256)
        give_state[side] = range_state[:, half].astype(jnp.bfloat16)
        give_decay[side] = range_decay[:, half]
    launch(remote(give_state.at[1 - core], pair_state, p1_send.at[0], p1_recv.at[0], sibling))
    launch(remote(give_decay.at[1 - core], pair_decay, p1_send.at[1], p1_recv.at[1], sibling))

    def inside(b):
        here = slice(b * SPAN, (b + 1) * SPAN)
        scores = lax.dot_general(
            reads[here, :], keys[here, :], (((1,), (1,)), ((), ())), preferred_element_type=jnp.float32
        )
        masked = jnp.where(causal, scores, 0.0)
        for pair_at in range(4):
            both = []
            for head in (2 * pair_at, 2 * pair_at + 1):
                gap = cums[b][:, head:head + 1] - cum_rows[b][head:head + 1, :]
                weight = masked * jnp.exp(jnp.minimum(gap, 0.0)) * step_rows[b][head:head + 1, :]
                both.append(jnp.dot(
                    weight.astype(jnp.bfloat16), values[here, head * P_SIZE:(head + 1) * P_SIZE],
                    preferred_element_type=jnp.float32,
                ))
            inner[here, pair_at * 128:(pair_at + 1) * 128] = jnp.concatenate(both, axis=1)

    remote(give_state.at[1 - core], pair_state, p1_send.at[0], p1_recv.at[0], sibling).wait_recv()
    remote(give_decay.at[1 - core], pair_decay, p1_send.at[1], p1_recv.at[1], sibling).wait_recv()
    first = core == 0
    near_state, near_decay = give_state[core].astype(jnp.float32), give_decay[core][:1]
    far_state, far_decay = pair_state[...].astype(jnp.float32), pair_decay[:1]
    state_0, decay_0 = jnp.where(first, near_state, far_state), jnp.where(first, near_decay, far_decay)
    state_1, decay_1 = jnp.where(first, far_state, near_state), jnp.where(first, far_decay, near_decay)

    def level(which, slots, decays, mine, state, decay, peers):
        slots[mine] = state.astype(jnp.bfloat16)
        decays[mine] = jnp.broadcast_to(decay, (8, 256))
        for shift, peer in enumerate(peers):
            launch(remote(slots.at[mine], slots.at[mine], p2_send.at[which, 0, shift], p2_recv.at[which, 0, shift], peer))
            launch(remote(decays.at[mine], decays.at[mine], p2_send.at[which, 1, shift], p2_recv.at[which, 1, shift], peer))

    def gather(which, slots, decays, mine, peers):
        for shift, peer in enumerate(peers):
            there = wrap(mine - 1 - shift)
            remote(slots.at[there], slots.at[there], p2_send.at[which, 0, shift], p2_recv.at[which, 0, shift], peer).wait_recv()
            remote(decays.at[there], decays.at[there], p2_send.at[which, 1, shift], p2_recv.at[which, 1, shift], peer).wait_recv()
        state, decay = jnp.zeros((N, 256), jnp.float32), jnp.ones((1, 256), jnp.float32)
        before, before_decay = state, decay
        for member in range(4):
            before = jnp.where(mine == member, state, before)
            before_decay = jnp.where(mine == member, decay, before_decay)
            fade = decays[member][:1]
            state = fade * state + slots[member].astype(jnp.float32)
            decay = decay * fade
        return before, before_decay, state, decay

    y_peers = [y_next, y_far, y_prev]
    x_peers = [x_next, x_far, x_prev]
    level(0, y_state, y_decay, y, decay_1 * state_0 + state_1, decay_0 * decay_1, y_peers)
    inside(0)
    before_y, before_y_decay, row_state, row_decay = gather(0, y_state, y_decay, y, y_peers)
    level(1, x_state, x_decay, x, row_state, row_decay, x_peers)
    inside(1)
    before_x, _, _, _ = gather(1, x_state, x_decay, x, x_peers)
    into_0 = before_y_decay * before_x + before_y
    into_1 = decay_0 * into_0 + state_0
    outflow[...] = jnp.where(first, into_1, into_0).astype(jnp.bfloat16)
    launch(remote(outflow, inflow.at[core], p4_send, p4_recv, sibling))
    inflow[core] = jnp.where(first, into_0, into_1).astype(jnp.bfloat16)
    remote(outflow, inflow.at[1 - core], p4_send, p4_recv, sibling).wait_recv()
    entering = jnp.concatenate([inflow[0], inflow[1]], axis=1)
    skips = expand(row_of(skip_ref))
    for b in range(2):
        here = slice(b * SPAN, (b + 1) * SPAN)
        outer = jnp.dot(reads[here, :], entering, preferred_element_type=jnp.float32)
        outer = expand(jnp.exp(cums[b])) * outer
        result = inner[here, :] + outer + skips * values[here, :].astype(jnp.float32)
        out_ref[here, :] = result.astype(jnp.bfloat16)
        if b == 0:
            entering = (fades[0] * entering.astype(jnp.float32) + states[0]).astype(jnp.bfloat16)
    for copy, condition in sends:
        if condition is None:
            copy.wait_send()
        else:
            pl.when(condition)(copy.wait_send)


def layer(*operands):
    vmem = pl.BlockSpec(memory_space=pltpu.VMEM)
    smem = pl.BlockSpec(memory_space=pltpu.SMEM)
    dma = pltpu.SemaphoreType.DMA
    bf16, f32 = jnp.bfloat16, jnp.float32
    return pl.pallas_call(
        layer_kernel,
        out_shape=jax.ShapeDtypeStruct((256, 512), bf16),
        in_specs=[vmem] * 6 + [smem, vmem, vmem, smem, smem, smem],
        out_specs=vmem,
        scratch_shapes=[
            pltpu.VMEM((4, 8, ROWS, 2048), bf16),
            pltpu.VMEM((8, SHARE, 128), bf16),
            pltpu.VMEM((16, SHARE, 1024), bf16),
            pltpu.VMEM((8, 4, 256, 128), bf16),
            pltpu.VMEM((8, 256, 128), f32),
            pltpu.VMEM((8, 3, 256, 128), bf16),
            pltpu.VMEM((8, 256, 128), bf16),
            pltpu.VMEM((8, 256, 128), bf16),
            pltpu.VMEM((8, 8, ROWS, 128), bf16),
            pltpu.VMEM((16 + 256, 768), f32),
            pltpu.VMEM((2, 16, 768), bf16),
            pltpu.VMEM((256, 512), bf16),
            pltpu.VMEM((256, N), bf16),
            pltpu.VMEM((256, N), bf16),
            pltpu.VMEM((256, 512), f32),
            pltpu.VMEM((2, N, 512), f32),
            pltpu.VMEM((N, 256), bf16),
            pltpu.VMEM((8, 256), f32),
            pltpu.VMEM((4, N, 256), bf16),
            pltpu.VMEM((4, 8, 256), f32),
            pltpu.VMEM((4, N, 256), bf16),
            pltpu.VMEM((4, 8, 256), f32),
            pltpu.VMEM((2, N, 256), bf16),
            pltpu.VMEM((2, 8, 256), f32),
            pltpu.VMEM((2, N, 256), bf16),
            pltpu.VMEM((N, 256), bf16),
            pltpu.VMEM((256, 128), f32),
            dma((3,)), dma((7,)), dma((7,)), dma((3, 2)), dma((3, 2)), dma((4,)), dma((4,)), dma((4,)), dma((4,)),
            dma((2, 8, 3)), dma((2, 8, 3)), dma((8, 3)), dma((8, 3)), dma((8,)), dma((8,)), dma((2, 7)), dma((2, 7)),
            dma(()), dma(()), dma((2,)), dma((2,)), dma((2, 2, 3)), dma((2, 2, 3)), dma(()), dma(()),
        ],
        compiler_params=pltpu.CompilerParams(
            collective_id=0, has_side_effects=True, vmem_limit_bytes=56 * 2**20
        ),
        name="layer",
    )(*operands)


def body(
    tokens,
    proj_mean,
    proj_devs,
    bc_mean,
    bc_devs,
    swag_coef,
    dt_weight,
    dt_bias,
    decay_rate,
    skip_gain,
    conv_proj,
    conv_bc,
):
    return layer(
        tokens, proj_mean, proj_devs, bc_mean, bc_devs, dt_weight.T, swag_coef,
        conv_proj, conv_bc, dt_bias, decay_rate, skip_gain,
    )


def solution(mesh):
    return jax.shard_map(
        body,
        mesh=mesh,
        in_specs=(
            P(("fsdp", "seq", "tp"), None),
            P(("fsdp", "seq"), "tp"),
            P(None, ("fsdp", "seq"), "tp"),
            P(("fsdp", "seq"), None, "tp"),
            P(None, ("fsdp", "seq"), None, "tp"),
            P(),
            P(("fsdp", "seq"), "tp"),
            P("tp"),
            P("tp"),
            P("tp"),
            P(None, "tp"),
            P(None, None, "tp"),
        ),
        out_specs=P(("fsdp", "seq"), "tp"),
        check_vma=False,
    )
```

```python
import jax
import jax.numpy as jnp
from jax import lax
from jax.experimental import pallas as pl
from jax.experimental.pallas import tpu as pltpu
from jax.sharding import PartitionSpec as P

P_SIZE = 64
N = 128
CONV = 4
SPAN = 128
MESH = pl.DeviceIdType.MESH
SHARE = 112
ROWS = 32
GROUPS_AT = (slice(0, 3), slice(3, 5), slice(5, 8))
ORDER = (4, 3, 5, 2, 6, 1, 7, 0)


def sampled(mean, devs, coef_ref):
    factor = (2.0 * (len(devs) - 1)) ** (-0.5)
    accum = mean.astype(jnp.float32)
    for member, dev in enumerate(devs):
        accum = accum + factor * coef_ref[member] * dev.astype(jnp.float32)
    return accum.astype(jnp.bfloat16)


def expand(heads):
    lane = lax.broadcasted_iota(jnp.int32, (heads.shape[0], 128), 1)
    return jnp.concatenate(
        [jnp.where(lane < P_SIZE, heads[:, 2 * j:2 * j + 1], heads[:, 2 * j + 1:2 * j + 2]) for j in range(4)],
        axis=1,
    )


def softplus(value):
    small = jnp.exp(-jnp.abs(value))
    series = small * (1.0 - small * (0.5 - small * (1.0 / 3.0 - small * 0.25)))
    return jnp.maximum(value, 0.0) + jnp.where(small < 0.01, series, jnp.log(1.0 + small))


def fold(tile):
    lane = lax.broadcasted_iota(jnp.int32, tile.shape, 1)
    joined = jnp.where((lane >= 96) & (lane < 104), tile + pltpu.roll(tile, 120, 1), tile)
    return jnp.where(lane >= 104, 0.0, joined)


def pack(tile):
    lane = lax.broadcasted_iota(jnp.int32, tile.shape, 1)
    high = tile.astype(jnp.bfloat16).astype(jnp.float32)
    low = pltpu.roll(tile - high, 8, 1)
    return jnp.where((lane >= 104) & (lane < 112), low, high).astype(jnp.bfloat16)


def layer_kernel(
    tok_ref, mean_ref, devs_ref, bc_mean_ref, bc_devs_ref, dt_ref, coef_ref, conv_x_ref, conv_bc_ref, bias_ref, rate_ref, skip_ref, out_ref,
    x_buf, w_ref, ring, rs_out, rs_own, rs_in, z_out, z_in, y_in, padded, edge, values, keys, reads, inner, states,
    pair_state, pair_decay, y_state, y_decay, x_state, x_decay, give_state, give_decay, inflow, outflow, dt_buf,
    own_sem, p_send, p_recv, a_send, a_recv, u_send, u_recv, c_send, c_recv, r_send, r_recv, rs_send, rs_recv,
    z_send, z_recv, y_send, y_recv,
    halo_send, halo_recv, p1_send, p1_recv, p2_send, p2_recv, p4_send, p4_recv,
):
    f = lax.axis_index("fsdp")
    s = lax.axis_index("seq")
    t = lax.axis_index("tp")
    q = lax.rem(s, 8)
    x = lax.div(s, 8)
    core = lax.rem(s, 2)
    y = lax.div(q, 2)
    z = f * 8 + t

    def wrap(value):
        return lax.rem(value + 4, 4)

    def place(x_at, y_at, core_at):
        return (f, x_at * 8 + y_at * 2 + core_at, t)

    def plane(z_at):
        z_at = lax.rem(z_at + 16, 16)
        return (lax.div(z_at, 8), s, lax.rem(z_at, 8))

    sibling = place(x, y, 1 - core)
    y_next, y_far, y_prev = (place(x, wrap(y + by), core) for by in (1, 2, 3))
    x_next, x_far, x_prev = (place(wrap(x + by), y, core) for by in (1, 2, 3))
    z_next, z_prev = plane(z + 1), plane(z - 1)
    q_at = [lax.rem(q + 1 + i, 8) for i in range(7)]
    q_peers = [(f, x * 8 + at, t) for at in q_at]
    t_at = [lax.rem(t + by, 8) for by in range(8)]
    t_peers = [(f, s, at) for at in t_at]
    seq_next, seq_prev = (f, lax.min(s + 1, 31), t), (f, lax.max(s - 1, 0), t)

    ring[:, 96:, :] = jnp.zeros((16, SHARE - 96, 1024), jnp.bfloat16)
    barrier = pltpu.get_barrier_semaphore()
    for peer in (x_next, x_far, x_prev, z_next, z_prev, *q_peers, *t_peers[1:]):
        pl.semaphore_signal(barrier, inc=1, device_id=peer, device_id_type=MESH)

    @pl.when(s < 31)
    def _():
        pl.semaphore_signal(barrier, inc=1, device_id=seq_next, device_id_type=MESH)

    @pl.when(s > 0)
    def _():
        pl.semaphore_signal(barrier, inc=1, device_id=seq_prev, device_id_type=MESH)

    sends = []

    def remote(src, dst, send_sem, recv_sem, peer):
        return pltpu.make_async_remote_copy(
            src_ref=src, dst_ref=dst, send_sem=send_sem, recv_sem=recv_sem,
            device_id=peer, device_id_type=MESH,
        )

    def launch(copy, condition=None):
        if condition is None:
            copy.start()
        else:
            pl.when(condition)(copy.start)
        sends.append((copy, condition))

    def token_columns(half, x_at):
        return tok_ref.at[:, pl.ds(pl.multiple_of(half * 4096 + x_at * 1024, 1024), 1024)]

    def token_place(half, x_at, q_here):
        return x_buf.at[x_at, q_here, :, pl.ds(half * 1024, 1024)]

    locals_ = [
        pltpu.make_async_copy(token_columns(half, x), token_place(half, x, q), own_sem.at[half]) for half in range(2)
    ]
    for copy in locals_:
        copy.start()
    for tile in range(4):
        columns = slice(tile * 128, (tile + 1) * 128)
        weight = sampled(mean_ref[:, columns], [devs_ref[m, :, columns] for m in range(4)], coef_ref)
        turned = weight.astype(jnp.float32).T.astype(jnp.bfloat16)
        w_ref[2 * tile, :64, :] = turned[:64]
        w_ref[2 * tile + 1, :64, :] = turned[64:]
    for kind in range(2):
        weight = sampled(bc_mean_ref[:, kind, :], [bc_devs_ref[m, :, kind, :] for m in range(4)], coef_ref)
        turned = weight.astype(jnp.float32).T.astype(jnp.bfloat16)
        for g in range(8):
            w_ref[g, 64 + 16 * kind:80 + 16 * kind, :] = turned[16 * g:16 * g + 16]
    dt_rows = jnp.concatenate([dt_ref[...].astype(jnp.float32), jnp.zeros((8, 128), jnp.float32)], axis=0)
    for g in range(8):
        w_ref[g, 96:, :] = dt_rows.astype(jnp.bfloat16)
    lanes = pl.ds(pl.multiple_of(q * 128, 128), 128)
    locals_.append(pltpu.make_async_copy(w_ref.at[q], ring.at[z, :, lanes], own_sem.at[2]))
    locals_[2].start()
    pl.semaphore_wait(barrier, 19 + jnp.where(s > 0, 1, 0) + jnp.where(s < 31, 1, 0))

    for i in range(7):
        launch(remote(w_ref.at[q_at[i]], ring.at[z, :, lanes], p_send.at[i], p_recv.at[i], q_peers[i]))
    for i, peer in enumerate((x_next, x_far, x_prev)):
        for half in range(2):
            launch(remote(
                token_columns(half, wrap(x + 1 + i)), token_place(half, x, q), a_send.at[i, half], a_recv.at[i, half], peer
            ))

    pieces = (pl.ds(0, 48), pl.ds(48, 48), pl.ds(96, 16))

    def ring_copy(way, k, b, slot):
        piece = ring.at[lax.rem(slot + 32, 16), pieces[b]]
        return remote(piece, piece, r_send.at[way, k, b], r_recv.at[way, k, b], z_next if way == 0 else z_prev)

    def steps_here(slot):
        return lax.rem(slot + 32, 8) == q

    def ring_send(k, b):
        for way in range(2):
            slot = z - k if way == 0 else z + k
            if k < 7 or way == b:
                launch(ring_copy(way, k, b, slot))
            if b == 1 and (k < 7 or way == 0):
                launch(ring_copy(way, k, 2, slot), steps_here(slot))

    def ring_wait(k, b):
        for way in range(2):
            slot = z - 1 - k if way == 0 else z + 1 + k
            if k < 7 or way == b:
                ring_copy(way, k, b, slot).wait_recv()
            if b == 1 and (k < 7 or way == 0):
                pl.when(steps_here(slot))(ring_copy(way, k, 2, slot).wait_recv)

    def ring_step(k):
        for b in range(2):
            ring_wait(k, b)
            ring_send(k + 1, b)

    for i in range(7):
        from_q = pl.ds(pl.multiple_of(lax.rem(q + 7 - i, 8) * 128, 128), 128)
        remote(w_ref.at[q_at[i]], ring.at[z, :, from_q], p_send.at[i], p_recv.at[i], q_peers[i]).wait_recv()
    for copy in locals_:
        copy.wait()
    ring_send(0, 0)
    ring_send(0, 1)
    for i, peer in enumerate((x_next, x_far, x_prev)):
        for half in range(2):
            here = token_place(half, wrap(x - 1 - i), q)
            remote(here, here, a_send.at[i, half], a_recv.at[i, half], peer).wait_recv()

    def unit(y_by, core_at, part=None):
        member = wrap(y + y_by) * 2 + core_at
        return x_buf.at[:, member] if part is None else x_buf.at[pl.ds(2 * part, 2), member]

    def unit_copy(kind, piece):
        return remote(piece, piece, u_send.at[kind], u_recv.at[kind], y_next if kind % 2 == 0 else y_prev)

    def share(index, y_by):
        launch(remote(unit(y_by, core), unit(y_by, core), c_send.at[index], c_recv.at[index], sibling))

    launch(unit_copy(0, unit(0, core)))
    launch(unit_copy(1, unit(0, core)))
    share(0, 0)
    ring_step(0)
    ring_step(1)
    ring_step(2)
    for kind, y_by in ((0, -1), (1, 1)):
        unit_copy(kind, unit(y_by, core)).wait_recv()
        launch(unit_copy(2 + kind, unit(y_by, core, kind)))
        share(1 + kind, y_by)
    ring_step(3)
    for kind in range(2):
        unit_copy(2 + kind, unit(2, core, kind)).wait_recv()
    share(3, 2)
    ring_step(4)
    for index, y_by in enumerate((0, -1, 1, 2)):
        here = unit(y_by, 1 - core)
        remote(here, here, c_send.at[index], c_recv.at[index], sibling).wait_recv()

    def narrowed(by, tile, where_to, joined):
        steps = q == t_at[by]

        @pl.when(steps)
        def _():
            where_to[...] = pack(fold(tile) if joined else tile)

        @pl.when(jnp.logical_not(steps))
        def _():
            where_to[...] = tile.astype(jnp.bfloat16)

    def multiply(*bys):
        for owner in range(4):
            total = None
            for half in range(2):
                weight = jnp.concatenate([ring[t_at[by] + 8 * half] for by in bys], axis=0)
                units = x_buf[owner, :, :, half * 1024:(half + 1) * 1024].reshape(256, 1024)
                one = lax.dot_general(
                    units, weight, (((1,), (1,)), ((), ())), preferred_element_type=jnp.float32
                )
                total = one if total is None else total + one
            for at, by in enumerate(bys):
                tile = jnp.concatenate(
                    [total[:, at * SHARE:(at + 1) * SHARE], jnp.zeros((256, 128 - SHARE), jnp.float32)], axis=1
                )
                narrowed(by, tile, rs_out.at[by, owner], False)

                @pl.when(x == owner)
                def _():
                    rs_own[by] = tile

        for by in bys:
            for i, peer in enumerate((x_next, x_far, x_prev)):
                launch(remote(rs_out.at[by, wrap(x + 1 + i)], rs_in.at[by, i], rs_send.at[by, i], rs_recv.at[by, i], peer))

    def settle(by):
        total = rs_own[by]
        for i, peer in enumerate((x_next, x_far, x_prev)):
            remote(rs_in.at[by, i], rs_in.at[by, i], rs_send.at[by, i], rs_recv.at[by, i], peer).wait_recv()
            total = total + rs_in[by, i].astype(jnp.float32)
        if by == 0:
            narrowed(by, total, z_in.at[ORDER.index(by)], True)
        else:
            narrowed(by, total, z_out.at[by], True)
            launch(remote(z_out.at[by], z_in.at[ORDER.index(by)], z_send.at[by], z_recv.at[by], t_peers[by]))

    def spread_copy(group, i):
        slots = GROUPS_AT[group]
        owner = q if i == 7 else q_at[i]
        piece = z_in.at[slots, pl.ds(pl.multiple_of(owner * ROWS, ROWS), ROWS)]
        there = y_in.at[q, slots]
        if i == 7:
            return pltpu.make_async_copy(piece, there, own_sem.at[group])
        return remote(piece, there, y_send.at[group, i], y_recv.at[group, i], q_peers[i])

    def spread(group):
        for by in ORDER[GROUPS_AT[group]]:
            if by:
                here = z_in.at[ORDER.index(by)]
                remote(here, here, z_send.at[by], z_recv.at[by], t_peers[by]).wait_recv()
        spread_copy(group, 7).start()
        for i in range(7):
            launch(spread_copy(group, i))

    multiply(4)
    multiply(3, 5)
    ring_step(5)
    multiply(2, 6)
    settle(4)
    ring_step(6)
    settle(3)
    settle(5)
    multiply(1, 7)
    settle(2)
    settle(6)
    ring_wait(7, 0)
    ring_wait(7, 1)
    multiply(0)
    settle(1)
    settle(7)
    spread(0)
    settle(0)
    spread(1)
    spread(2)
    for group in range(3):
        spread_copy(group, 7).wait()
        for i in range(7):
            slots = GROUPS_AT[group]
            here = y_in.at[lax.rem(q + 7 - i, 8), slots]
            remote(here, here, y_send.at[group, i], y_recv.at[group, i], q_peers[i]).wait_recv()

    lane = lax.broadcasted_iota(jnp.int32, (1, 128), 1)
    for at, by in enumerate(ORDER):
        first_row = pl.multiple_of(lax.rem(t + 8 - by, 8) * ROWS, ROWS)
        rows = pl.ds(16 + first_row, ROWS)
        tiles = [y_in[g, at].astype(jnp.float32) for g in range(8)]
        for pair_at in range(4):
            both = [tiles[2 * pair_at][:, :P_SIZE], tiles[2 * pair_at + 1][:, :P_SIZE]]
            padded[rows, pair_at * 128:(pair_at + 1) * 128] = jnp.concatenate(both, axis=1)
        padded[rows, 512:640] = jnp.concatenate([tile[:, 64:80] for tile in tiles], axis=1)
        padded[rows, 640:768] = jnp.concatenate([tile[:, 80:96] for tile in tiles], axis=1)
        logits = y_in[t, at].astype(jnp.float32)
        dt_buf[pl.ds(first_row, ROWS), :] = pltpu.roll(logits, 32, 1) + pltpu.roll(logits, 24, 1)
    edge[0] = padded[256:272, :].astype(jnp.bfloat16)
    launch(remote(edge.at[0], edge.at[1], halo_send, halo_recv, seq_next), s < 31)

    def row_of(ref):
        row = jnp.zeros((1, 128), jnp.float32)
        for head in range(8):
            row = jnp.where(lane == head, ref[head], row)
        return row

    step = softplus(dt_buf[...] + row_of(bias_ref))
    rise = -step * row_of(rate_ref)
    down_to = lax.broadcasted_iota(jnp.int32, (SPAN, SPAN), 0)
    across = lax.broadcasted_iota(jnp.int32, (SPAN, SPAN), 1)
    causal = across <= down_to
    triangle = jnp.where(causal, 1.0, 0.0).astype(jnp.float32)
    steps, cums, step_rows, cum_rows, lasts = [], [], [], [], []
    for b in range(2):
        here = slice(b * SPAN, (b + 1) * SPAN)
        cum = jnp.dot(
            triangle, rise[here], precision=lax.Precision.HIGHEST, preferred_element_type=jnp.float32
        )
        steps.append(step[here])
        cums.append(cum)
        step_rows.append(step[here].T)
        cum_rows.append(cum.T)
        lasts.append(cum[SPAN - 1:, :])

    @pl.when(s > 0)
    def _():
        remote(edge.at[0], edge.at[1], halo_send, halo_recv, seq_next).wait_recv()
        padded[:16, :] = edge[1].astype(jnp.float32)

    @pl.when(s == 0)
    def _():
        padded[:16, :] = jnp.zeros((16, 768), jnp.float32)

    for tile in range(6):
        columns = slice(tile * 128, (tile + 1) * 128)
        gained = None
        for tap in range(CONV):
            if tile < 4:
                gain = conv_x_ref[tap:tap + 1, columns]
            else:
                gain = conv_bc_ref[tap, tile - 4:tile - 3, :]
            term = gain * padded[13 + tap:13 + tap + 256, columns]
            gained = term if gained is None else gained + term
        smooth = (gained * (1.0 / (1.0 + jnp.exp(-gained)))).astype(jnp.bfloat16)
        if tile < 4:
            values[:, columns] = smooth
        elif tile == 4:
            keys[...] = smooth
        else:
            reads[...] = smooth

    for b in range(2):
        here = slice(b * SPAN, (b + 1) * SPAN)
        factor = expand(jnp.exp(lasts[b] - cums[b]) * steps[b])
        scaled = (values[here, :].astype(jnp.float32) * factor).astype(jnp.bfloat16)
        states[b] = lax.dot_general(
            keys[here, :], scaled, (((0,), (0,)), ((), ())), preferred_element_type=jnp.float32
        )
    fades = [expand(jnp.exp(last)) for last in lasts]
    range_state = fades[1] * states[0] + states[1]
    range_decay = jnp.broadcast_to(fades[0] * fades[1], (8, 512))

    for side in range(2):
        half = slice(side * 256, (side + 1) * 256)
        give_state[side] = range_state[:, half].astype(jnp.bfloat16)
        give_decay[side] = range_decay[:, half]
    launch(remote(give_state.at[1 - core], pair_state, p1_send.at[0], p1_recv.at[0], sibling))
    launch(remote(give_decay.at[1 - core], pair_decay, p1_send.at[1], p1_recv.at[1], sibling))

    def inside(b):
        here = slice(b * SPAN, (b + 1) * SPAN)
        scores = lax.dot_general(
            reads[here, :], keys[here, :], (((1,), (1,)), ((), ())), preferred_element_type=jnp.float32
        )
        masked = jnp.where(causal, scores, 0.0)
        for pair_at in range(4):
            both = []
            for head in (2 * pair_at, 2 * pair_at + 1):
                gap = cums[b][:, head:head + 1] - cum_rows[b][head:head + 1, :]
                weight = masked * jnp.exp(jnp.minimum(gap, 0.0)) * step_rows[b][head:head + 1, :]
                both.append(jnp.dot(
                    weight.astype(jnp.bfloat16), values[here, head * P_SIZE:(head + 1) * P_SIZE],
                    preferred_element_type=jnp.float32,
                ))
            inner[here, pair_at * 128:(pair_at + 1) * 128] = jnp.concatenate(both, axis=1)

    remote(give_state.at[1 - core], pair_state, p1_send.at[0], p1_recv.at[0], sibling).wait_recv()
    remote(give_decay.at[1 - core], pair_decay, p1_send.at[1], p1_recv.at[1], sibling).wait_recv()
    first = core == 0
    near_state, near_decay = give_state[core].astype(jnp.float32), give_decay[core][:1]
    far_state, far_decay = pair_state[...].astype(jnp.float32), pair_decay[:1]
    state_0, decay_0 = jnp.where(first, near_state, far_state), jnp.where(first, near_decay, far_decay)
    state_1, decay_1 = jnp.where(first, far_state, near_state), jnp.where(first, far_decay, near_decay)

    def level(which, slots, decays, mine, state, decay, peers):
        slots[mine] = state.astype(jnp.bfloat16)
        decays[mine] = jnp.broadcast_to(decay, (8, 256))
        for shift, peer in enumerate(peers):
            launch(remote(slots.at[mine], slots.at[mine], p2_send.at[which, 0, shift], p2_recv.at[which, 0, shift], peer))
            launch(remote(decays.at[mine], decays.at[mine], p2_send.at[which, 1, shift], p2_recv.at[which, 1, shift], peer))

    def gather(which, slots, decays, mine, peers):
        for shift, peer in enumerate(peers):
            there = wrap(mine - 1 - shift)
            remote(slots.at[there], slots.at[there], p2_send.at[which, 0, shift], p2_recv.at[which, 0, shift], peer).wait_recv()
            remote(decays.at[there], decays.at[there], p2_send.at[which, 1, shift], p2_recv.at[which, 1, shift], peer).wait_recv()
        state, decay = jnp.zeros((N, 256), jnp.float32), jnp.ones((1, 256), jnp.float32)
        before, before_decay = state, decay
        for member in range(4):
            before = jnp.where(mine == member, state, before)
            before_decay = jnp.where(mine == member, decay, before_decay)
            fade = decays[member][:1]
            state = fade * state + slots[member].astype(jnp.float32)
            decay = decay * fade
        return before, before_decay, state, decay

    y_peers = [y_next, y_far, y_prev]
    x_peers = [x_next, x_far, x_prev]
    level(0, y_state, y_decay, y, decay_1 * state_0 + state_1, decay_0 * decay_1, y_peers)
    inside(0)
    before_y, before_y_decay, row_state, row_decay = gather(0, y_state, y_decay, y, y_peers)
    level(1, x_state, x_decay, x, row_state, row_decay, x_peers)
    inside(1)
    before_x, _, _, _ = gather(1, x_state, x_decay, x, x_peers)
    into_0 = before_y_decay * before_x + before_y
    into_1 = decay_0 * into_0 + state_0
    outflow[...] = jnp.where(first, into_1, into_0).astype(jnp.bfloat16)
    launch(remote(outflow, inflow.at[core], p4_send, p4_recv, sibling))
    inflow[core] = jnp.where(first, into_0, into_1).astype(jnp.bfloat16)
    remote(outflow, inflow.at[1 - core], p4_send, p4_recv, sibling).wait_recv()
    entering = jnp.concatenate([inflow[0], inflow[1]], axis=1)
    skips = expand(row_of(skip_ref))
    for b in range(2):
        here = slice(b * SPAN, (b + 1) * SPAN)
        outer = jnp.dot(reads[here, :], entering, preferred_element_type=jnp.float32)
        outer = expand(jnp.exp(cums[b])) * outer
        result = inner[here, :] + outer + skips * values[here, :].astype(jnp.float32)
        out_ref[here, :] = result.astype(jnp.bfloat16)
        if b == 0:
            entering = (fades[0] * entering.astype(jnp.float32) + states[0]).astype(jnp.bfloat16)
    for copy, condition in sends:
        if condition is None:
            copy.wait_send()
        else:
            pl.when(condition)(copy.wait_send)


def layer(*operands):
    vmem = pl.BlockSpec(memory_space=pltpu.VMEM)
    smem = pl.BlockSpec(memory_space=pltpu.SMEM)
    dma = pltpu.SemaphoreType.DMA
    bf16, f32 = jnp.bfloat16, jnp.float32
    return pl.pallas_call(
        layer_kernel,
        out_shape=jax.ShapeDtypeStruct((256, 512), bf16),
        in_specs=[vmem] * 6 + [smem, vmem, vmem, smem, smem, smem],
        out_specs=vmem,
        scratch_shapes=[
            pltpu.VMEM((4, 8, ROWS, 2048), bf16),
            pltpu.VMEM((8, SHARE, 128), bf16),
            pltpu.VMEM((16, SHARE, 1024), bf16),
            pltpu.VMEM((8, 4, 256, 128), bf16),
            pltpu.VMEM((8, 256, 128), f32),
            pltpu.VMEM((8, 3, 256, 128), bf16),
            pltpu.VMEM((8, 256, 128), bf16),
            pltpu.VMEM((8, 256, 128), bf16),
            pltpu.VMEM((8, 8, ROWS, 128), bf16),
            pltpu.VMEM((16 + 256, 768), f32),
            pltpu.VMEM((2, 16, 768), bf16),
            pltpu.VMEM((256, 512), bf16),
            pltpu.VMEM((256, N), bf16),
            pltpu.VMEM((256, N), bf16),
            pltpu.VMEM((256, 512), f32),
            pltpu.VMEM((2, N, 512), f32),
            pltpu.VMEM((N, 256), bf16),
            pltpu.VMEM((8, 256), f32),
            pltpu.VMEM((4, N, 256), bf16),
            pltpu.VMEM((4, 8, 256), f32),
            pltpu.VMEM((4, N, 256), bf16),
            pltpu.VMEM((4, 8, 256), f32),
            pltpu.VMEM((2, N, 256), bf16),
            pltpu.VMEM((2, 8, 256), f32),
            pltpu.VMEM((2, N, 256), bf16),
            pltpu.VMEM((N, 256), bf16),
            pltpu.VMEM((256, 128), f32),
            dma((3,)), dma((7,)), dma((7,)), dma((3, 2)), dma((3, 2)), dma((4,)), dma((4,)), dma((4,)), dma((4,)),
            dma((2, 8, 3)), dma((2, 8, 3)), dma((8, 3)), dma((8, 3)), dma((8,)), dma((8,)), dma((3, 7)), dma((3, 7)),
            dma(()), dma(()), dma((2,)), dma((2,)), dma((2, 2, 3)), dma((2, 2, 3)), dma(()), dma(()),
        ],
        compiler_params=pltpu.CompilerParams(
            collective_id=0, has_side_effects=True, vmem_limit_bytes=56 * 2**20
        ),
        name="layer",
    )(*operands)


def body(
    tokens,
    proj_mean,
    proj_devs,
    bc_mean,
    bc_devs,
    swag_coef,
    dt_weight,
    dt_bias,
    decay_rate,
    skip_gain,
    conv_proj,
    conv_bc,
):
    return layer(
        tokens, proj_mean, proj_devs, bc_mean, bc_devs, dt_weight.T, swag_coef,
        conv_proj, conv_bc, dt_bias, decay_rate, skip_gain,
    )


def solution(mesh):
    return jax.shard_map(
        body,
        mesh=mesh,
        in_specs=(
            P(("fsdp", "seq", "tp"), None),
            P(("fsdp", "seq"), "tp"),
            P(None, ("fsdp", "seq"), "tp"),
            P(("fsdp", "seq"), None, "tp"),
            P(None, ("fsdp", "seq"), None, "tp"),
            P(),
            P(("fsdp", "seq"), "tp"),
            P("tp"),
            P("tp"),
            P("tp"),
            P(None, "tp"),
            P(None, None, "tp"),
        ),
        out_specs=P(("fsdp", "seq"), "tp"),
        check_vma=False,
    )
```

```python
import jax
import jax.numpy as jnp
from jax import lax
from jax.experimental import pallas as pl
from jax.experimental.pallas import tpu as pltpu
from jax.sharding import PartitionSpec as P

P_SIZE = 64
N = 128
CONV = 4
SPAN = 128
MESH = pl.DeviceIdType.MESH
SHARE = 112
ROWS = 32
GROUPS_AT = (slice(0, 1), slice(1, 3), slice(3, 5), slice(5, 7), slice(7, 8))
ORDER = (4, 3, 5, 2, 6, 1, 7, 0)


def sampled(mean, devs, coef_ref):
    factor = (2.0 * (len(devs) - 1)) ** (-0.5)
    accum = mean.astype(jnp.float32)
    for member, dev in enumerate(devs):
        accum = accum + factor * coef_ref[member] * dev.astype(jnp.float32)
    return accum.astype(jnp.bfloat16)


def expand(heads):
    lane = lax.broadcasted_iota(jnp.int32, (heads.shape[0], 128), 1)
    return jnp.concatenate(
        [jnp.where(lane < P_SIZE, heads[:, 2 * j:2 * j + 1], heads[:, 2 * j + 1:2 * j + 2]) for j in range(4)],
        axis=1,
    )


def softplus(value):
    small = jnp.exp(-jnp.abs(value))
    series = small * (1.0 - small * (0.5 - small * (1.0 / 3.0 - small * 0.25)))
    return jnp.maximum(value, 0.0) + jnp.where(small < 0.01, series, jnp.log(1.0 + small))


def fold(tile):
    lane = lax.broadcasted_iota(jnp.int32, tile.shape, 1)
    joined = jnp.where((lane >= 96) & (lane < 104), tile + pltpu.roll(tile, 120, 1), tile)
    return jnp.where(lane >= 104, 0.0, joined)


def pack(tile):
    lane = lax.broadcasted_iota(jnp.int32, tile.shape, 1)
    high = tile.astype(jnp.bfloat16).astype(jnp.float32)
    low = pltpu.roll(tile - high, 8, 1)
    return jnp.where((lane >= 104) & (lane < 112), low, high).astype(jnp.bfloat16)


def layer_kernel(
    tok_ref, mean_ref, devs_ref, bc_mean_ref, bc_devs_ref, dt_ref, coef_ref, conv_x_ref, conv_bc_ref, bias_ref, rate_ref, skip_ref, out_ref,
    x_buf, w_ref, ring, rs_out, rs_own, rs_in, y_out, y_in, z_out, z_in, padded, edge, values, keys, reads, inner, states,
    pair_state, pair_decay, y_state, y_decay, x_state, x_decay, give_state, give_decay, inflow, outflow, dt_buf,
    own_sem, p_send, p_recv, a_send, a_recv, u_send, u_recv, c_send, c_recv, r_send, r_recv, rs_send, rs_recv,
    z_send, z_recv, y_send, y_recv, spread_sem,
    halo_send, halo_recv, p1_send, p1_recv, p2_send, p2_recv, p4_send, p4_recv,
):
    f = lax.axis_index("fsdp")
    s = lax.axis_index("seq")
    t = lax.axis_index("tp")
    q = lax.rem(s, 8)
    x = lax.div(s, 8)
    core = lax.rem(s, 2)
    y = lax.div(q, 2)
    z = f * 8 + t

    def wrap(value):
        return lax.rem(value + 4, 4)

    def place(x_at, y_at, core_at):
        return (f, x_at * 8 + y_at * 2 + core_at, t)

    def plane(z_at):
        z_at = lax.rem(z_at + 16, 16)
        return (lax.div(z_at, 8), s, lax.rem(z_at, 8))

    sibling = place(x, y, 1 - core)
    y_next, y_far, y_prev = (place(x, wrap(y + by), core) for by in (1, 2, 3))
    x_next, x_far, x_prev = (place(wrap(x + by), y, core) for by in (1, 2, 3))
    z_next, z_prev = plane(z + 1), plane(z - 1)
    q_at = [lax.rem(q + 1 + i, 8) for i in range(7)]
    q_peers = [(f, x * 8 + at, t) for at in q_at]
    t_at = [lax.rem(t + by, 8) for by in range(8)]
    t_peers = [(f, s, at) for at in t_at]
    seq_next, seq_prev = (f, lax.min(s + 1, 31), t), (f, lax.max(s - 1, 0), t)

    ring[:, 96:, :] = jnp.zeros((16, SHARE - 96, 1024), jnp.bfloat16)
    barrier = pltpu.get_barrier_semaphore()
    for peer in (x_next, x_far, x_prev, z_next, z_prev, *q_peers, *t_peers[1:]):
        pl.semaphore_signal(barrier, inc=1, device_id=peer, device_id_type=MESH)

    @pl.when(s < 31)
    def _():
        pl.semaphore_signal(barrier, inc=1, device_id=seq_next, device_id_type=MESH)

    @pl.when(s > 0)
    def _():
        pl.semaphore_signal(barrier, inc=1, device_id=seq_prev, device_id_type=MESH)

    sends = []

    def remote(src, dst, send_sem, recv_sem, peer):
        return pltpu.make_async_remote_copy(
            src_ref=src, dst_ref=dst, send_sem=send_sem, recv_sem=recv_sem,
            device_id=peer, device_id_type=MESH,
        )

    def launch(copy, condition=None):
        if condition is None:
            copy.start()
        else:
            pl.when(condition)(copy.start)
        sends.append((copy, condition))

    def token_columns(half, x_at):
        return tok_ref.at[:, pl.ds(pl.multiple_of(half * 4096 + x_at * 1024, 1024), 1024)]

    def token_place(half, x_at, q_here):
        return x_buf.at[x_at, q_here, :, pl.ds(half * 1024, 1024)]

    locals_ = [
        pltpu.make_async_copy(token_columns(half, x), token_place(half, x, q), own_sem.at[half]) for half in range(2)
    ]
    for copy in locals_:
        copy.start()
    for tile in range(4):
        columns = slice(tile * 128, (tile + 1) * 128)
        weight = sampled(mean_ref[:, columns], [devs_ref[m, :, columns] for m in range(4)], coef_ref)
        turned = weight.astype(jnp.float32).T.astype(jnp.bfloat16)
        w_ref[2 * tile, :64, :] = turned[:64]
        w_ref[2 * tile + 1, :64, :] = turned[64:]
    for kind in range(2):
        weight = sampled(bc_mean_ref[:, kind, :], [bc_devs_ref[m, :, kind, :] for m in range(4)], coef_ref)
        turned = weight.astype(jnp.float32).T.astype(jnp.bfloat16)
        for g in range(8):
            w_ref[g, 64 + 16 * kind:80 + 16 * kind, :] = turned[16 * g:16 * g + 16]
    dt_rows = jnp.concatenate([dt_ref[...].astype(jnp.float32), jnp.zeros((8, 128), jnp.float32)], axis=0)
    for g in range(8):
        w_ref[g, 96:, :] = dt_rows.astype(jnp.bfloat16)
    lanes = pl.ds(pl.multiple_of(q * 128, 128), 128)
    locals_.append(pltpu.make_async_copy(w_ref.at[q], ring.at[z, :, lanes], own_sem.at[2]))
    locals_[2].start()
    pl.semaphore_wait(barrier, 19 + jnp.where(s > 0, 1, 0) + jnp.where(s < 31, 1, 0))

    for i in range(7):
        launch(remote(w_ref.at[q_at[i]], ring.at[z, :, lanes], p_send.at[i], p_recv.at[i], q_peers[i]))
    for i, peer in enumerate((x_next, x_far, x_prev)):
        for half in range(2):
            launch(remote(
                token_columns(half, wrap(x + 1 + i)), token_place(half, x, q), a_send.at[i, half], a_recv.at[i, half], peer
            ))

    pieces = (pl.ds(0, 48), pl.ds(48, 48), pl.ds(96, 16))

    def ring_copy(way, k, b, slot):
        piece = ring.at[lax.rem(slot + 32, 16), pieces[b]]
        return remote(piece, piece, r_send.at[way, k, b], r_recv.at[way, k, b], z_next if way == 0 else z_prev)

    def steps_here(slot):
        return lax.rem(slot + 32, 8) == q

    def ring_send(k, b):
        for way in range(2):
            slot = z - k if way == 0 else z + k
            if k < 7 or way == b:
                launch(ring_copy(way, k, b, slot))
            if b == 1 and (k < 7 or way == 0):
                launch(ring_copy(way, k, 2, slot), steps_here(slot))

    def ring_wait(k, b):
        for way in range(2):
            slot = z - 1 - k if way == 0 else z + 1 + k
            if k < 7 or way == b:
                ring_copy(way, k, b, slot).wait_recv()
            if b == 1 and (k < 7 or way == 0):
                pl.when(steps_here(slot))(ring_copy(way, k, 2, slot).wait_recv)

    def ring_step(k):
        for b in range(2):
            ring_wait(k, b)
            ring_send(k + 1, b)

    for i in range(7):
        from_q = pl.ds(pl.multiple_of(lax.rem(q + 7 - i, 8) * 128, 128), 128)
        remote(w_ref.at[q_at[i]], ring.at[z, :, from_q], p_send.at[i], p_recv.at[i], q_peers[i]).wait_recv()
    for copy in locals_:
        copy.wait()
    ring_send(0, 0)
    ring_send(0, 1)
    for i, peer in enumerate((x_next, x_far, x_prev)):
        for half in range(2):
            here = token_place(half, wrap(x - 1 - i), q)
            remote(here, here, a_send.at[i, half], a_recv.at[i, half], peer).wait_recv()

    def unit(y_by, core_at, part=None):
        member = wrap(y + y_by) * 2 + core_at
        return x_buf.at[:, member] if part is None else x_buf.at[pl.ds(2 * part, 2), member]

    def unit_copy(kind, piece):
        return remote(piece, piece, u_send.at[kind], u_recv.at[kind], y_next if kind % 2 == 0 else y_prev)

    def share(index, y_by):
        launch(remote(unit(y_by, core), unit(y_by, core), c_send.at[index], c_recv.at[index], sibling))

    launch(unit_copy(0, unit(0, core)))
    launch(unit_copy(1, unit(0, core)))
    share(0, 0)
    ring_step(0)
    ring_step(1)
    ring_step(2)
    for kind, y_by in ((0, -1), (1, 1)):
        unit_copy(kind, unit(y_by, core)).wait_recv()
        launch(unit_copy(2 + kind, unit(y_by, core, kind)))
        share(1 + kind, y_by)
    ring_step(3)
    for kind in range(2):
        unit_copy(2 + kind, unit(2, core, kind)).wait_recv()
    share(3, 2)
    ring_step(4)
    for index, y_by in enumerate((0, -1, 1, 2)):
        here = unit(y_by, 1 - core)
        remote(here, here, c_send.at[index], c_recv.at[index], sibling).wait_recv()

    def narrowed(by, tile, where_to, joined):
        steps = q == t_at[by]

        @pl.when(steps)
        def _():
            where_to[...] = pack(fold(tile) if joined else tile)

        @pl.when(jnp.logical_not(steps))
        def _():
            where_to[...] = tile.astype(jnp.bfloat16)

    def multiply(*bys):
        for owner in range(4):
            total = None
            for half in range(2):
                weight = jnp.concatenate([ring[t_at[by] + 8 * half] for by in bys], axis=0)
                units = x_buf[owner, :, :, half * 1024:(half + 1) * 1024].reshape(256, 1024)
                one = lax.dot_general(
                    units, weight, (((1,), (1,)), ((), ())), preferred_element_type=jnp.float32
                )
                total = one if total is None else total + one
            for at, by in enumerate(bys):
                tile = jnp.concatenate(
                    [total[:, at * SHARE:(at + 1) * SHARE], jnp.zeros((256, 128 - SHARE), jnp.float32)], axis=1
                )
                narrowed(by, tile, rs_out.at[by, owner], False)

                @pl.when(x == owner)
                def _():
                    rs_own[by] = tile

        for by in bys:
            for i, peer in enumerate((x_next, x_far, x_prev)):
                launch(remote(rs_out.at[by, wrap(x + 1 + i)], rs_in.at[by, i], rs_send.at[by, i], rs_recv.at[by, i], peer))

    def settle(by):
        total = rs_own[by]
        for i, peer in enumerate((x_next, x_far, x_prev)):
            remote(rs_in.at[by, i], rs_in.at[by, i], rs_send.at[by, i], rs_recv.at[by, i], peer).wait_recv()
            total = total + rs_in[by, i].astype(jnp.float32)
        narrowed(by, total, y_out.at[ORDER.index(by)], True)

    def spread_copy(group, i):
        slots = GROUPS_AT[group]
        owner = q if i == 7 else q_at[i]
        piece = y_out.at[slots, pl.ds(pl.multiple_of(owner * ROWS, ROWS), ROWS)]
        there = y_in.at[slots, q]
        if i == 7:
            return pltpu.make_async_copy(piece, there, spread_sem.at[group])
        return remote(piece, there, y_send.at[group, i], y_recv.at[group, i], q_peers[i])

    def spread(group):
        spread_copy(group, 7).start()
        for i in range(7):
            launch(spread_copy(group, i))

    lane = lax.broadcasted_iota(jnp.int32, (1, 128), 1)

    def collect(group):
        slots = GROUPS_AT[group]
        spread_copy(group, 7).wait()
        for i in range(7):
            here = y_in.at[slots, lax.rem(q + 7 - i, 8)]
            remote(here, here, y_send.at[group, i], y_recv.at[group, i], q_peers[i]).wait_recv()
        for at in range(slots.start, slots.stop):
            by = ORDER[at]
            tiles = [y_in[at, g].astype(jnp.float32) for g in range(8)]
            joined = [
                jnp.concatenate([tiles[2 * j][:, :P_SIZE], tiles[2 * j + 1][:, :P_SIZE]], axis=1) for j in range(4)
            ]
            joined.append(jnp.concatenate([tile[:, 64:80] for tile in tiles], axis=1))
            joined.append(jnp.concatenate([tile[:, 80:96] for tile in tiles], axis=1))
            steps = pltpu.roll(y_in[at, t_at[by]].astype(jnp.float32), 32, 1)
            joined.append(jnp.where(lane < 16, steps, 0.0))
            whole = jnp.concatenate(joined, axis=1).astype(jnp.bfloat16)
            if by == 0:
                z_in[t] = whole
            else:
                z_out[at] = whole
                launch(remote(z_out.at[at], z_in.at[t], z_send.at[by], z_recv.at[by], t_peers[by]))

    multiply(4)
    multiply(3, 5)
    ring_step(5)
    multiply(2, 6)
    settle(4)
    spread(0)
    ring_step(6)
    settle(3)
    settle(5)
    spread(1)
    multiply(1, 7)
    collect(0)
    settle(2)
    settle(6)
    spread(2)
    ring_wait(7, 0)
    ring_wait(7, 1)
    multiply(0)
    collect(1)
    settle(1)
    settle(7)
    spread(3)
    collect(2)
    settle(0)
    spread(4)
    collect(3)
    collect(4)
    for by in range(1, 8):
        here = z_in.at[lax.rem(t + 8 - by, 8)]
        remote(here, here, z_send.at[by], z_recv.at[by], t_peers[by]).wait_recv()
    padded[16:, :] = z_in[:, :, :768].reshape(256, 768).astype(jnp.float32)
    edge[0] = z_in[7, 16:, :768]
    launch(remote(edge.at[0], edge.at[1], halo_send, halo_recv, seq_next), s < 31)
    logits = z_in[:, :, 768:].reshape(256, 128).astype(jnp.float32)
    dt_buf[...] = logits + pltpu.roll(logits, 120, 1)

    def row_of(ref):
        row = jnp.zeros((1, 128), jnp.float32)
        for head in range(8):
            row = jnp.where(lane == head, ref[head], row)
        return row

    step = softplus(dt_buf[...] + row_of(bias_ref))
    rise = -step * row_of(rate_ref)
    down_to = lax.broadcasted_iota(jnp.int32, (SPAN, SPAN), 0)
    across = lax.broadcasted_iota(jnp.int32, (SPAN, SPAN), 1)
    causal = across <= down_to
    triangle = jnp.where(causal, 1.0, 0.0).astype(jnp.float32)
    steps, cums, step_rows, cum_rows, lasts = [], [], [], [], []
    for b in range(2):
        here = slice(b * SPAN, (b + 1) * SPAN)
        cum = jnp.dot(
            triangle, rise[here], precision=lax.Precision.HIGHEST, preferred_element_type=jnp.float32
        )
        steps.append(step[here])
        cums.append(cum)
        step_rows.append(step[here].T)
        cum_rows.append(cum.T)
        lasts.append(cum[SPAN - 1:, :])

    @pl.when(s > 0)
    def _():
        remote(edge.at[0], edge.at[1], halo_send, halo_recv, seq_next).wait_recv()
        padded[:16, :] = edge[1].astype(jnp.float32)

    @pl.when(s == 0)
    def _():
        padded[:16, :] = jnp.zeros((16, 768), jnp.float32)

    for tile in range(6):
        columns = slice(tile * 128, (tile + 1) * 128)
        gained = None
        for tap in range(CONV):
            if tile < 4:
                gain = conv_x_ref[tap:tap + 1, columns]
            else:
                gain = conv_bc_ref[tap, tile - 4:tile - 3, :]
            term = gain * padded[13 + tap:13 + tap + 256, columns]
            gained = term if gained is None else gained + term
        smooth = (gained * (1.0 / (1.0 + jnp.exp(-gained)))).astype(jnp.bfloat16)
        if tile < 4:
            values[:, columns] = smooth
        elif tile == 4:
            keys[...] = smooth
        else:
            reads[...] = smooth

    for b in range(2):
        here = slice(b * SPAN, (b + 1) * SPAN)
        factor = expand(jnp.exp(lasts[b] - cums[b]) * steps[b])
        scaled = (values[here, :].astype(jnp.float32) * factor).astype(jnp.bfloat16)
        states[b] = lax.dot_general(
            keys[here, :], scaled, (((0,), (0,)), ((), ())), preferred_element_type=jnp.float32
        )
    fades = [expand(jnp.exp(last)) for last in lasts]
    range_state = fades[1] * states[0] + states[1]
    range_decay = jnp.broadcast_to(fades[0] * fades[1], (8, 512))

    for side in range(2):
        half = slice(side * 256, (side + 1) * 256)
        give_state[side] = range_state[:, half].astype(jnp.bfloat16)
        give_decay[side] = range_decay[:, half]
    launch(remote(give_state.at[1 - core], pair_state, p1_send.at[0], p1_recv.at[0], sibling))
    launch(remote(give_decay.at[1 - core], pair_decay, p1_send.at[1], p1_recv.at[1], sibling))

    def inside(b):
        here = slice(b * SPAN, (b + 1) * SPAN)
        scores = lax.dot_general(
            reads[here, :], keys[here, :], (((1,), (1,)), ((), ())), preferred_element_type=jnp.float32
        )
        masked = jnp.where(causal, scores, 0.0)
        for pair_at in range(4):
            both = []
            for head in (2 * pair_at, 2 * pair_at + 1):
                gap = cums[b][:, head:head + 1] - cum_rows[b][head:head + 1, :]
                weight = masked * jnp.exp(jnp.minimum(gap, 0.0)) * step_rows[b][head:head + 1, :]
                both.append(jnp.dot(
                    weight.astype(jnp.bfloat16), values[here, head * P_SIZE:(head + 1) * P_SIZE],
                    preferred_element_type=jnp.float32,
                ))
            inner[here, pair_at * 128:(pair_at + 1) * 128] = jnp.concatenate(both, axis=1)

    remote(give_state.at[1 - core], pair_state, p1_send.at[0], p1_recv.at[0], sibling).wait_recv()
    remote(give_decay.at[1 - core], pair_decay, p1_send.at[1], p1_recv.at[1], sibling).wait_recv()
    first = core == 0
    near_state, near_decay = give_state[core].astype(jnp.float32), give_decay[core][:1]
    far_state, far_decay = pair_state[...].astype(jnp.float32), pair_decay[:1]
    state_0, decay_0 = jnp.where(first, near_state, far_state), jnp.where(first, near_decay, far_decay)
    state_1, decay_1 = jnp.where(first, far_state, near_state), jnp.where(first, far_decay, near_decay)

    def level(which, slots, decays, mine, state, decay, peers):
        slots[mine] = state.astype(jnp.bfloat16)
        decays[mine] = jnp.broadcast_to(decay, (8, 256))
        for shift, peer in enumerate(peers):
            launch(remote(slots.at[mine], slots.at[mine], p2_send.at[which, 0, shift], p2_recv.at[which, 0, shift], peer))
            launch(remote(decays.at[mine], decays.at[mine], p2_send.at[which, 1, shift], p2_recv.at[which, 1, shift], peer))

    def gather(which, slots, decays, mine, peers):
        for shift, peer in enumerate(peers):
            there = wrap(mine - 1 - shift)
            remote(slots.at[there], slots.at[there], p2_send.at[which, 0, shift], p2_recv.at[which, 0, shift], peer).wait_recv()
            remote(decays.at[there], decays.at[there], p2_send.at[which, 1, shift], p2_recv.at[which, 1, shift], peer).wait_recv()
        state, decay = jnp.zeros((N, 256), jnp.float32), jnp.ones((1, 256), jnp.float32)
        before, before_decay = state, decay
        for member in range(4):
            before = jnp.where(mine == member, state, before)
            before_decay = jnp.where(mine == member, decay, before_decay)
            fade = decays[member][:1]
            state = fade * state + slots[member].astype(jnp.float32)
            decay = decay * fade
        return before, before_decay, state, decay

    y_peers = [y_next, y_far, y_prev]
    x_peers = [x_next, x_far, x_prev]
    level(0, y_state, y_decay, y, decay_1 * state_0 + state_1, decay_0 * decay_1, y_peers)
    inside(0)
    before_y, before_y_decay, row_state, row_decay = gather(0, y_state, y_decay, y, y_peers)
    level(1, x_state, x_decay, x, row_state, row_decay, x_peers)
    inside(1)
    before_x, _, _, _ = gather(1, x_state, x_decay, x, x_peers)
    into_0 = before_y_decay * before_x + before_y
    into_1 = decay_0 * into_0 + state_0
    outflow[...] = jnp.where(first, into_1, into_0).astype(jnp.bfloat16)
    launch(remote(outflow, inflow.at[core], p4_send, p4_recv, sibling))
    inflow[core] = jnp.where(first, into_0, into_1).astype(jnp.bfloat16)
    remote(outflow, inflow.at[1 - core], p4_send, p4_recv, sibling).wait_recv()
    entering = jnp.concatenate([inflow[0], inflow[1]], axis=1)
    skips = expand(row_of(skip_ref))
    for b in range(2):
        here = slice(b * SPAN, (b + 1) * SPAN)
        outer = jnp.dot(reads[here, :], entering, preferred_element_type=jnp.float32)
        outer = expand(jnp.exp(cums[b])) * outer
        result = inner[here, :] + outer + skips * values[here, :].astype(jnp.float32)
        out_ref[here, :] = result.astype(jnp.bfloat16)
        if b == 0:
            entering = (fades[0] * entering.astype(jnp.float32) + states[0]).astype(jnp.bfloat16)
    for copy, condition in sends:
        if condition is None:
            copy.wait_send()
        else:
            pl.when(condition)(copy.wait_send)


def layer(*operands):
    vmem = pl.BlockSpec(memory_space=pltpu.VMEM)
    smem = pl.BlockSpec(memory_space=pltpu.SMEM)
    dma = pltpu.SemaphoreType.DMA
    bf16, f32 = jnp.bfloat16, jnp.float32
    return pl.pallas_call(
        layer_kernel,
        out_shape=jax.ShapeDtypeStruct((256, 512), bf16),
        in_specs=[vmem] * 6 + [smem, vmem, vmem, smem, smem, smem],
        out_specs=vmem,
        scratch_shapes=[
            pltpu.VMEM((4, 8, ROWS, 2048), bf16),
            pltpu.VMEM((8, SHARE, 128), bf16),
            pltpu.VMEM((16, SHARE, 1024), bf16),
            pltpu.VMEM((8, 4, 256, 128), bf16),
            pltpu.VMEM((8, 256, 128), f32),
            pltpu.VMEM((8, 3, 256, 128), bf16),
            pltpu.VMEM((8, 256, 128), bf16),
            pltpu.VMEM((8, 8, ROWS, 128), bf16),
            pltpu.VMEM((8, ROWS, 896), bf16),
            pltpu.VMEM((8, ROWS, 896), bf16),
            pltpu.VMEM((16 + 256, 768), f32),
            pltpu.VMEM((2, 16, 768), bf16),
            pltpu.VMEM((256, 512), bf16),
            pltpu.VMEM((256, N), bf16),
            pltpu.VMEM((256, N), bf16),
            pltpu.VMEM((256, 512), f32),
            pltpu.VMEM((2, N, 512), f32),
            pltpu.VMEM((N, 256), bf16),
            pltpu.VMEM((8, 256), f32),
            pltpu.VMEM((4, N, 256), bf16),
            pltpu.VMEM((4, 8, 256), f32),
            pltpu.VMEM((4, N, 256), bf16),
            pltpu.VMEM((4, 8, 256), f32),
            pltpu.VMEM((2, N, 256), bf16),
            pltpu.VMEM((2, 8, 256), f32),
            pltpu.VMEM((2, N, 256), bf16),
            pltpu.VMEM((N, 256), bf16),
            pltpu.VMEM((256, 128), f32),
            dma((3,)), dma((7,)), dma((7,)), dma((3, 2)), dma((3, 2)), dma((4,)), dma((4,)), dma((4,)), dma((4,)),
            dma((2, 8, 3)), dma((2, 8, 3)), dma((8, 3)), dma((8, 3)), dma((8,)), dma((8,)), dma((5, 7)), dma((5, 7)), dma((5,)),
            dma(()), dma(()), dma((2,)), dma((2,)), dma((2, 2, 3)), dma((2, 2, 3)), dma(()), dma(()),
        ],
        compiler_params=pltpu.CompilerParams(
            collective_id=0, has_side_effects=True, vmem_limit_bytes=56 * 2**20
        ),
        name="layer",
    )(*operands)


def body(
    tokens,
    proj_mean,
    proj_devs,
    bc_mean,
    bc_devs,
    swag_coef,
    dt_weight,
    dt_bias,
    decay_rate,
    skip_gain,
    conv_proj,
    conv_bc,
):
    return layer(
        tokens, proj_mean, proj_devs, bc_mean, bc_devs, dt_weight.T, swag_coef,
        conv_proj, conv_bc, dt_bias, decay_rate, skip_gain,
    )


def solution(mesh):
    return jax.shard_map(
        body,
        mesh=mesh,
        in_specs=(
            P(("fsdp", "seq", "tp"), None),
            P(("fsdp", "seq"), "tp"),
            P(None, ("fsdp", "seq"), "tp"),
            P(("fsdp", "seq"), None, "tp"),
            P(None, ("fsdp", "seq"), None, "tp"),
            P(),
            P(("fsdp", "seq"), "tp"),
            P("tp"),
            P("tp"),
            P("tp"),
            P(None, "tp"),
            P(None, None, "tp"),
        ),
        out_specs=P(("fsdp", "seq"), "tp"),
        check_vma=False,
    )
```

```python
import jax
import jax.numpy as jnp
from jax import lax
from jax.experimental import pallas as pl
from jax.experimental.pallas import tpu as pltpu
from jax.sharding import PartitionSpec as P

P_SIZE = 64
N = 128
CONV = 4
SPAN = 128
MESH = pl.DeviceIdType.MESH
SHARE = 112
ROWS = 32
GROUPS_AT = (slice(0, 1), slice(1, 3), slice(3, 5), slice(5, 7), slice(7, 8))
ORDER = (4, 3, 5, 2, 6, 1, 7, 0)


def sampled(mean, devs, coef_ref):
    factor = (2.0 * (len(devs) - 1)) ** (-0.5)
    accum = mean.astype(jnp.float32)
    for member, dev in enumerate(devs):
        accum = accum + factor * coef_ref[member] * dev.astype(jnp.float32)
    return accum.astype(jnp.bfloat16)


def expand(heads):
    lane = lax.broadcasted_iota(jnp.int32, (heads.shape[0], 128), 1)
    return jnp.concatenate(
        [jnp.where(lane < P_SIZE, heads[:, 2 * j:2 * j + 1], heads[:, 2 * j + 1:2 * j + 2]) for j in range(4)],
        axis=1,
    )


def softplus(value):
    small = jnp.exp(-jnp.abs(value))
    series = small * (1.0 - small * (0.5 - small * (1.0 / 3.0 - small * 0.25)))
    return jnp.maximum(value, 0.0) + jnp.where(small < 0.01, series, jnp.log(1.0 + small))


def fold(tile):
    lane = lax.broadcasted_iota(jnp.int32, tile.shape, 1)
    joined = jnp.where((lane >= 96) & (lane < 104), tile + pltpu.roll(tile, 120, 1), tile)
    return jnp.where(lane >= 104, 0.0, joined)


def pack(tile):
    lane = lax.broadcasted_iota(jnp.int32, tile.shape, 1)
    high = tile.astype(jnp.bfloat16).astype(jnp.float32)
    low = pltpu.roll(tile - high, 8, 1)
    return jnp.where((lane >= 104) & (lane < 112), low, high).astype(jnp.bfloat16)


def layer_kernel(
    tok_ref, mean_ref, devs_ref, bc_mean_ref, bc_devs_ref, dt_ref, coef_ref, conv_x_ref, conv_bc_ref, bias_ref, rate_ref, skip_ref, out_ref,
    x_buf, w_ref, ring, rs_out, rs_own, rs_in, y_out, y_in, z_out, z_in, padded, edge, values, keys, reads, inner, states,
    pair_state, pair_decay, y_state, y_decay, x_state, x_decay, give_state, give_decay, inflow, outflow, dt_buf,
    own_sem, p_send, p_recv, a_send, a_recv, u_send, u_recv, c_send, c_recv, r_send, r_recv, rs_send, rs_recv,
    z_send, z_recv, y_send, y_recv, spread_sem,
    halo_send, halo_recv, p1_send, p1_recv, p2_send, p2_recv, p4_send, p4_recv,
):
    f = lax.axis_index("fsdp")
    s = lax.axis_index("seq")
    t = lax.axis_index("tp")
    q = lax.rem(s, 8)
    x = lax.div(s, 8)
    core = lax.rem(s, 2)
    y = lax.div(q, 2)
    z = f * 8 + t

    def wrap(value):
        return lax.rem(value + 4, 4)

    def place(x_at, y_at, core_at):
        return (f, x_at * 8 + y_at * 2 + core_at, t)

    def plane(z_at):
        z_at = lax.rem(z_at + 16, 16)
        return (lax.div(z_at, 8), s, lax.rem(z_at, 8))

    sibling = place(x, y, 1 - core)
    y_next, y_far, y_prev = (place(x, wrap(y + by), core) for by in (1, 2, 3))
    x_next, x_far, x_prev = (place(wrap(x + by), y, core) for by in (1, 2, 3))
    z_next, z_prev = plane(z + 1), plane(z - 1)
    q_at = [lax.rem(q + 1 + i, 8) for i in range(7)]
    q_peers = [(f, x * 8 + at, t) for at in q_at]
    t_at = [lax.rem(t + by, 8) for by in range(8)]
    t_peers = [(f, s, at) for at in t_at]
    seq_next, seq_prev = (f, lax.min(s + 1, 31), t), (f, lax.max(s - 1, 0), t)

    ring[:, 96:, :] = jnp.zeros((16, SHARE - 96, 1024), jnp.bfloat16)
    barrier = pltpu.get_barrier_semaphore()
    for peer in (x_next, x_far, x_prev, z_next, z_prev, *q_peers, *t_peers[1:]):
        pl.semaphore_signal(barrier, inc=1, device_id=peer, device_id_type=MESH)

    @pl.when(s < 31)
    def _():
        pl.semaphore_signal(barrier, inc=1, device_id=seq_next, device_id_type=MESH)

    @pl.when(s > 0)
    def _():
        pl.semaphore_signal(barrier, inc=1, device_id=seq_prev, device_id_type=MESH)

    sends = []

    def remote(src, dst, send_sem, recv_sem, peer):
        return pltpu.make_async_remote_copy(
            src_ref=src, dst_ref=dst, send_sem=send_sem, recv_sem=recv_sem,
            device_id=peer, device_id_type=MESH,
        )

    def launch(copy, condition=None):
        if condition is None:
            copy.start()
        else:
            pl.when(condition)(copy.start)
        sends.append((copy, condition))

    def token_columns(half, x_at):
        return tok_ref.at[:, pl.ds(pl.multiple_of(half * 4096 + x_at * 1024, 1024), 1024)]

    def token_place(half, x_at, q_here):
        return x_buf.at[x_at, q_here, :, pl.ds(half * 1024, 1024)]

    locals_ = [
        pltpu.make_async_copy(token_columns(half, x), token_place(half, x, q), own_sem.at[half]) for half in range(2)
    ]
    for copy in locals_:
        copy.start()
    for tile in range(4):
        columns = slice(tile * 128, (tile + 1) * 128)
        weight = sampled(mean_ref[:, columns], [devs_ref[m, :, columns] for m in range(4)], coef_ref)
        turned = weight.astype(jnp.float32).T.astype(jnp.bfloat16)
        w_ref[2 * tile, :64, :] = turned[:64]
        w_ref[2 * tile + 1, :64, :] = turned[64:]
    for kind in range(2):
        weight = sampled(bc_mean_ref[:, kind, :], [bc_devs_ref[m, :, kind, :] for m in range(4)], coef_ref)
        turned = weight.astype(jnp.float32).T.astype(jnp.bfloat16)
        for g in range(8):
            w_ref[g, 64 + 16 * kind:80 + 16 * kind, :] = turned[16 * g:16 * g + 16]
    dt_rows = jnp.concatenate([dt_ref[...].astype(jnp.float32), jnp.zeros((8, 128), jnp.float32)], axis=0)
    for g in range(8):
        w_ref[g, 96:, :] = dt_rows.astype(jnp.bfloat16)
    lanes = pl.ds(pl.multiple_of(q * 128, 128), 128)
    locals_.append(pltpu.make_async_copy(w_ref.at[q], ring.at[z, :, lanes], own_sem.at[2]))
    locals_[2].start()
    pl.semaphore_wait(barrier, 19 + jnp.where(s > 0, 1, 0) + jnp.where(s < 31, 1, 0))

    for i in range(7):
        launch(remote(w_ref.at[q_at[i]], ring.at[z, :, lanes], p_send.at[i], p_recv.at[i], q_peers[i]))
    for i, peer in enumerate((x_next, x_far, x_prev)):
        for half in range(2):
            launch(remote(
                token_columns(half, wrap(x + 1 + i)), token_place(half, x, q), a_send.at[i, half], a_recv.at[i, half], peer
            ))

    pieces = (pl.ds(0, 48), pl.ds(48, 48), pl.ds(96, 16))

    def ring_copy(way, k, b, slot):
        piece = ring.at[lax.rem(slot + 32, 16), pieces[b]]
        return remote(piece, piece, r_send.at[way, k, b], r_recv.at[way, k, b], z_next if way == 0 else z_prev)

    def steps_here(slot):
        return lax.rem(slot + 32, 8) == q

    def ring_send(k, b):
        for way in range(2):
            slot = z - k if way == 0 else z + k
            if k < 7 or way == b:
                launch(ring_copy(way, k, b, slot))
            if b == 1 and (k < 7 or way == 0):
                launch(ring_copy(way, k, 2, slot), steps_here(slot))

    def ring_wait(k, b):
        for way in range(2):
            slot = z - 1 - k if way == 0 else z + 1 + k
            if k < 7 or way == b:
                ring_copy(way, k, b, slot).wait_recv()
            if b == 1 and (k < 7 or way == 0):
                pl.when(steps_here(slot))(ring_copy(way, k, 2, slot).wait_recv)

    def ring_step(k):
        for b in range(2):
            ring_wait(k, b)
            ring_send(k + 1, b)

    for i in range(7):
        from_q = pl.ds(pl.multiple_of(lax.rem(q + 7 - i, 8) * 128, 128), 128)
        remote(w_ref.at[q_at[i]], ring.at[z, :, from_q], p_send.at[i], p_recv.at[i], q_peers[i]).wait_recv()
    for copy in locals_:
        copy.wait()
    ring_send(0, 0)
    ring_send(0, 1)
    for i, peer in enumerate((x_next, x_far, x_prev)):
        for half in range(2):
            here = token_place(half, wrap(x - 1 - i), q)
            remote(here, here, a_send.at[i, half], a_recv.at[i, half], peer).wait_recv()

    def unit(y_by, core_at, part=None):
        member = wrap(y + y_by) * 2 + core_at
        return x_buf.at[:, member] if part is None else x_buf.at[pl.ds(2 * part, 2), member]

    def unit_copy(kind, piece):
        return remote(piece, piece, u_send.at[kind], u_recv.at[kind], y_next if kind % 2 == 0 else y_prev)

    def share(index, y_by):
        launch(remote(unit(y_by, core), unit(y_by, core), c_send.at[index], c_recv.at[index], sibling))

    launch(unit_copy(0, unit(0, core)))
    launch(unit_copy(1, unit(0, core)))
    share(0, 0)
    ring_step(0)
    ring_step(1)
    ring_step(2)
    for kind, y_by in ((0, -1), (1, 1)):
        unit_copy(kind, unit(y_by, core)).wait_recv()
        launch(unit_copy(2 + kind, unit(y_by, core, kind)))
        share(1 + kind, y_by)
    ring_step(3)
    for kind in range(2):
        unit_copy(2 + kind, unit(2, core, kind)).wait_recv()
    share(3, 2)
    ring_step(4)
    for index, y_by in enumerate((0, -1, 1, 2)):
        here = unit(y_by, 1 - core)
        remote(here, here, c_send.at[index], c_recv.at[index], sibling).wait_recv()

    def narrowed(by, tile, where_to, joined):
        steps = q == t_at[by]

        @pl.when(steps)
        def _():
            where_to[...] = pack(fold(tile) if joined else tile)

        @pl.when(jnp.logical_not(steps))
        def _():
            where_to[...] = tile.astype(jnp.bfloat16)

    def multiply(*bys):
        for owner in range(4):
            total = None
            for half in range(2):
                weight = jnp.concatenate([ring[t_at[by] + 8 * half] for by in bys], axis=0)
                units = x_buf[owner, :, :, half * 1024:(half + 1) * 1024].reshape(256, 1024)
                one = lax.dot_general(
                    units, weight, (((1,), (1,)), ((), ())), preferred_element_type=jnp.float32
                )
                total = one if total is None else total + one
            for at, by in enumerate(bys):
                tile = jnp.concatenate(
                    [total[:, at * SHARE:(at + 1) * SHARE], jnp.zeros((256, 128 - SHARE), jnp.float32)], axis=1
                )
                narrowed(by, tile, rs_out.at[by, owner], False)

                @pl.when(x == owner)
                def _():
                    rs_own[by] = tile

        for by in bys:
            for i, peer in enumerate((x_next, x_far, x_prev)):
                launch(remote(rs_out.at[by, wrap(x + 1 + i)], rs_in.at[by, i], rs_send.at[by, i], rs_recv.at[by, i], peer))

    def settle(by):
        total = rs_own[by]
        for i, peer in enumerate((x_next, x_far, x_prev)):
            remote(rs_in.at[by, i], rs_in.at[by, i], rs_send.at[by, i], rs_recv.at[by, i], peer).wait_recv()
            total = total + rs_in[by, i].astype(jnp.float32)
        narrowed(by, total, y_out.at[ORDER.index(by)], True)

    def spread_copy(group, i):
        slots = GROUPS_AT[group]
        owner = q if i == 7 else q_at[i]
        piece = y_out.at[slots, pl.ds(pl.multiple_of(owner * ROWS, ROWS), ROWS)]
        there = y_in.at[slots, q]
        if i == 7:
            return pltpu.make_async_copy(piece, there, spread_sem.at[group])
        return remote(piece, there, y_send.at[group, i], y_recv.at[group, i], q_peers[i])

    def spread(group):
        spread_copy(group, 7).start()
        for i in range(7):
            launch(spread_copy(group, i))

    lane = lax.broadcasted_iota(jnp.int32, (1, 128), 1)

    def collect(group):
        slots = GROUPS_AT[group]
        spread_copy(group, 7).wait()
        for i in range(7):
            here = y_in.at[slots, lax.rem(q + 7 - i, 8)]
            remote(here, here, y_send.at[group, i], y_recv.at[group, i], q_peers[i]).wait_recv()
        for at in range(slots.start, slots.stop):
            by = ORDER[at]
            tiles = [y_in[at, g].astype(jnp.float32) for g in range(8)]
            joined = [
                jnp.concatenate([tiles[2 * j][:, :P_SIZE], tiles[2 * j + 1][:, :P_SIZE]], axis=1) for j in range(4)
            ]
            joined.append(jnp.concatenate([tile[:, 64:80] for tile in tiles], axis=1))
            joined.append(jnp.concatenate([tile[:, 80:96] for tile in tiles], axis=1))
            steps = pltpu.roll(y_in[at, t_at[by]].astype(jnp.float32), 32, 1)
            joined.append(jnp.where(lane < 16, steps, 0.0))
            whole = jnp.concatenate(joined, axis=1).astype(jnp.bfloat16)
            if by == 0:
                z_in[t] = whole
            else:
                z_out[at] = whole
                launch(remote(z_out.at[at], z_in.at[t], z_send.at[by], z_recv.at[by], t_peers[by]))

    multiply(4)
    multiply(3, 5)
    ring_step(5)
    multiply(2, 6)
    settle(4)
    spread(0)
    ring_step(6)
    settle(3)
    settle(5)
    spread(1)
    multiply(1, 7)
    collect(0)
    settle(2)
    settle(6)
    spread(2)
    ring_wait(7, 0)
    ring_wait(7, 1)
    multiply(0)
    collect(1)
    settle(1)
    settle(7)
    spread(3)
    collect(2)
    settle(0)
    spread(4)
    collect(3)
    collect(4)
    def arrived(by):
        here = z_in.at[lax.rem(t + 8 - by, 8)]
        remote(here, here, z_send.at[by], z_recv.at[by], z_next).wait_recv()

    pl.when(t < 7)(lambda: arrived(lax.rem(t + 1, 8)))
    edge[0] = z_in[7, 16:, :768]
    launch(remote(edge.at[0], edge.at[1], halo_send, halo_recv, seq_next), s < 31)
    for by in (4, 3, 5, 2, 6, 1, 7):
        pl.when(t + 1 != by)(lambda by=by: arrived(by))
    padded[16:, :] = z_in[:, :, :768].reshape(256, 768).astype(jnp.float32)
    logits = z_in[:, :, 768:].reshape(256, 128).astype(jnp.float32)
    dt_buf[...] = logits + pltpu.roll(logits, 120, 1)

    def row_of(ref):
        row = jnp.zeros((1, 128), jnp.float32)
        for head in range(8):
            row = jnp.where(lane == head, ref[head], row)
        return row

    step = softplus(dt_buf[...] + row_of(bias_ref))
    rise = -step * row_of(rate_ref)
    down_to = lax.broadcasted_iota(jnp.int32, (SPAN, SPAN), 0)
    across = lax.broadcasted_iota(jnp.int32, (SPAN, SPAN), 1)
    causal = across <= down_to
    triangle = jnp.where(causal, 1.0, 0.0).astype(jnp.float32)
    steps, cums, step_rows, cum_rows, lasts = [], [], [], [], []
    for b in range(2):
        here = slice(b * SPAN, (b + 1) * SPAN)
        cum = jnp.dot(
            triangle, rise[here], precision=lax.Precision.HIGHEST, preferred_element_type=jnp.float32
        )
        steps.append(step[here])
        cums.append(cum)
        step_rows.append(step[here].T)
        cum_rows.append(cum.T)
        lasts.append(cum[SPAN - 1:, :])

    @pl.when(s > 0)
    def _():
        remote(edge.at[0], edge.at[1], halo_send, halo_recv, seq_next).wait_recv()
        padded[:16, :] = edge[1].astype(jnp.float32)

    @pl.when(s == 0)
    def _():
        padded[:16, :] = jnp.zeros((16, 768), jnp.float32)

    for tile in range(6):
        columns = slice(tile * 128, (tile + 1) * 128)
        gained = None
        for tap in range(CONV):
            if tile < 4:
                gain = conv_x_ref[tap:tap + 1, columns]
            else:
                gain = conv_bc_ref[tap, tile - 4:tile - 3, :]
            term = gain * padded[13 + tap:13 + tap + 256, columns]
            gained = term if gained is None else gained + term
        smooth = (gained * (1.0 / (1.0 + jnp.exp(-gained)))).astype(jnp.bfloat16)
        if tile < 4:
            values[:, columns] = smooth
        elif tile == 4:
            keys[...] = smooth
        else:
            reads[...] = smooth

    for b in range(2):
        here = slice(b * SPAN, (b + 1) * SPAN)
        factor = expand(jnp.exp(lasts[b] - cums[b]) * steps[b])
        scaled = (values[here, :].astype(jnp.float32) * factor).astype(jnp.bfloat16)
        states[b] = lax.dot_general(
            keys[here, :], scaled, (((0,), (0,)), ((), ())), preferred_element_type=jnp.float32
        )
    fades = [expand(jnp.exp(last)) for last in lasts]
    range_state = fades[1] * states[0] + states[1]
    range_decay = jnp.broadcast_to(fades[0] * fades[1], (8, 512))

    for side in range(2):
        half = slice(side * 256, (side + 1) * 256)
        give_state[side] = range_state[:, half].astype(jnp.bfloat16)
        give_decay[side] = range_decay[:, half]
    launch(remote(give_state.at[1 - core], pair_state, p1_send.at[0], p1_recv.at[0], sibling))
    launch(remote(give_decay.at[1 - core], pair_decay, p1_send.at[1], p1_recv.at[1], sibling))

    def inside(b):
        here = slice(b * SPAN, (b + 1) * SPAN)
        scores = lax.dot_general(
            reads[here, :], keys[here, :], (((1,), (1,)), ((), ())), preferred_element_type=jnp.float32
        )
        masked = jnp.where(causal, scores, 0.0)
        for pair_at in range(4):
            both = []
            for head in (2 * pair_at, 2 * pair_at + 1):
                gap = cums[b][:, head:head + 1] - cum_rows[b][head:head + 1, :]
                weight = masked * jnp.exp(jnp.minimum(gap, 0.0)) * step_rows[b][head:head + 1, :]
                both.append(jnp.dot(
                    weight.astype(jnp.bfloat16), values[here, head * P_SIZE:(head + 1) * P_SIZE],
                    preferred_element_type=jnp.float32,
                ))
            inner[here, pair_at * 128:(pair_at + 1) * 128] = jnp.concatenate(both, axis=1)

    remote(give_state.at[1 - core], pair_state, p1_send.at[0], p1_recv.at[0], sibling).wait_recv()
    remote(give_decay.at[1 - core], pair_decay, p1_send.at[1], p1_recv.at[1], sibling).wait_recv()
    first = core == 0
    near_state, near_decay = give_state[core].astype(jnp.float32), give_decay[core][:1]
    far_state, far_decay = pair_state[...].astype(jnp.float32), pair_decay[:1]
    state_0, decay_0 = jnp.where(first, near_state, far_state), jnp.where(first, near_decay, far_decay)
    state_1, decay_1 = jnp.where(first, far_state, near_state), jnp.where(first, far_decay, near_decay)

    def level(which, slots, decays, mine, state, decay, peers):
        slots[mine] = state.astype(jnp.bfloat16)
        decays[mine] = jnp.broadcast_to(decay, (8, 256))
        for shift, peer in enumerate(peers):
            launch(remote(slots.at[mine], slots.at[mine], p2_send.at[which, 0, shift], p2_recv.at[which, 0, shift], peer))
            launch(remote(decays.at[mine], decays.at[mine], p2_send.at[which, 1, shift], p2_recv.at[which, 1, shift], peer))

    def gather(which, slots, decays, mine, peers):
        for shift, peer in enumerate(peers):
            there = wrap(mine - 1 - shift)
            remote(slots.at[there], slots.at[there], p2_send.at[which, 0, shift], p2_recv.at[which, 0, shift], peer).wait_recv()
            remote(decays.at[there], decays.at[there], p2_send.at[which, 1, shift], p2_recv.at[which, 1, shift], peer).wait_recv()
        state, decay = jnp.zeros((N, 256), jnp.float32), jnp.ones((1, 256), jnp.float32)
        before, before_decay = state, decay
        for member in range(4):
            before = jnp.where(mine == member, state, before)
            before_decay = jnp.where(mine == member, decay, before_decay)
            fade = decays[member][:1]
            state = fade * state + slots[member].astype(jnp.float32)
            decay = decay * fade
        return before, before_decay, state, decay

    y_peers = [y_next, y_far, y_prev]
    x_peers = [x_next, x_far, x_prev]
    level(0, y_state, y_decay, y, decay_1 * state_0 + state_1, decay_0 * decay_1, y_peers)
    inside(0)
    before_y, before_y_decay, row_state, row_decay = gather(0, y_state, y_decay, y, y_peers)
    level(1, x_state, x_decay, x, row_state, row_decay, x_peers)
    inside(1)
    before_x, _, _, _ = gather(1, x_state, x_decay, x, x_peers)
    into_0 = before_y_decay * before_x + before_y
    into_1 = decay_0 * into_0 + state_0
    outflow[...] = jnp.where(first, into_1, into_0).astype(jnp.bfloat16)
    launch(remote(outflow, inflow.at[core], p4_send, p4_recv, sibling))
    inflow[core] = jnp.where(first, into_0, into_1).astype(jnp.bfloat16)
    remote(outflow, inflow.at[1 - core], p4_send, p4_recv, sibling).wait_recv()
    entering = jnp.concatenate([inflow[0], inflow[1]], axis=1)
    skips = expand(row_of(skip_ref))
    for b in range(2):
        here = slice(b * SPAN, (b + 1) * SPAN)
        outer = jnp.dot(reads[here, :], entering, preferred_element_type=jnp.float32)
        outer = expand(jnp.exp(cums[b])) * outer
        result = inner[here, :] + outer + skips * values[here, :].astype(jnp.float32)
        out_ref[here, :] = result.astype(jnp.bfloat16)
        if b == 0:
            entering = (fades[0] * entering.astype(jnp.float32) + states[0]).astype(jnp.bfloat16)
    for copy, condition in sends:
        if condition is None:
            copy.wait_send()
        else:
            pl.when(condition)(copy.wait_send)


def layer(*operands):
    vmem = pl.BlockSpec(memory_space=pltpu.VMEM)
    smem = pl.BlockSpec(memory_space=pltpu.SMEM)
    dma = pltpu.SemaphoreType.DMA
    bf16, f32 = jnp.bfloat16, jnp.float32
    return pl.pallas_call(
        layer_kernel,
        out_shape=jax.ShapeDtypeStruct((256, 512), bf16),
        in_specs=[vmem] * 6 + [smem, vmem, vmem, smem, smem, smem],
        out_specs=vmem,
        scratch_shapes=[
            pltpu.VMEM((4, 8, ROWS, 2048), bf16),
            pltpu.VMEM((8, SHARE, 128), bf16),
            pltpu.VMEM((16, SHARE, 1024), bf16),
            pltpu.VMEM((8, 4, 256, 128), bf16),
            pltpu.VMEM((8, 256, 128), f32),
            pltpu.VMEM((8, 3, 256, 128), bf16),
            pltpu.VMEM((8, 256, 128), bf16),
            pltpu.VMEM((8, 8, ROWS, 128), bf16),
            pltpu.VMEM((8, ROWS, 896), bf16),
            pltpu.VMEM((8, ROWS, 896), bf16),
            pltpu.VMEM((16 + 256, 768), f32),
            pltpu.VMEM((2, 16, 768), bf16),
            pltpu.VMEM((256, 512), bf16),
            pltpu.VMEM((256, N), bf16),
            pltpu.VMEM((256, N), bf16),
            pltpu.VMEM((256, 512), f32),
            pltpu.VMEM((2, N, 512), f32),
            pltpu.VMEM((N, 256), bf16),
            pltpu.VMEM((8, 256), f32),
            pltpu.VMEM((4, N, 256), bf16),
            pltpu.VMEM((4, 8, 256), f32),
            pltpu.VMEM((4, N, 256), bf16),
            pltpu.VMEM((4, 8, 256), f32),
            pltpu.VMEM((2, N, 256), bf16),
            pltpu.VMEM((2, 8, 256), f32),
            pltpu.VMEM((2, N, 256), bf16),
            pltpu.VMEM((N, 256), bf16),
            pltpu.VMEM((256, 128), f32),
            dma((3,)), dma((7,)), dma((7,)), dma((3, 2)), dma((3, 2)), dma((4,)), dma((4,)), dma((4,)), dma((4,)),
            dma((2, 8, 3)), dma((2, 8, 3)), dma((8, 3)), dma((8, 3)), dma((8,)), dma((8,)), dma((5, 7)), dma((5, 7)), dma((5,)),
            dma(()), dma(()), dma((2,)), dma((2,)), dma((2, 2, 3)), dma((2, 2, 3)), dma(()), dma(()),
        ],
        compiler_params=pltpu.CompilerParams(
            collective_id=0, has_side_effects=True, vmem_limit_bytes=56 * 2**20
        ),
        name="layer",
    )(*operands)


def body(
    tokens,
    proj_mean,
    proj_devs,
    bc_mean,
    bc_devs,
    swag_coef,
    dt_weight,
    dt_bias,
    decay_rate,
    skip_gain,
    conv_proj,
    conv_bc,
):
    return layer(
        tokens, proj_mean, proj_devs, bc_mean, bc_devs, dt_weight.T, swag_coef,
        conv_proj, conv_bc, dt_bias, decay_rate, skip_gain,
    )


def solution(mesh):
    return jax.shard_map(
        body,
        mesh=mesh,
        in_specs=(
            P(("fsdp", "seq", "tp"), None),
            P(("fsdp", "seq"), "tp"),
            P(None, ("fsdp", "seq"), "tp"),
            P(("fsdp", "seq"), None, "tp"),
            P(None, ("fsdp", "seq"), None, "tp"),
            P(),
            P(("fsdp", "seq"), "tp"),
            P("tp"),
            P("tp"),
            P("tp"),
            P(None, "tp"),
            P(None, None, "tp"),
        ),
        out_specs=P(("fsdp", "seq"), "tp"),
        check_vma=False,
    )
```

```python
import jax
import jax.numpy as jnp
from jax import lax
from jax.experimental import pallas as pl
from jax.experimental.pallas import tpu as pltpu
from jax.sharding import PartitionSpec as P

P_SIZE = 64
N = 128
CONV = 4
SPAN = 128
MESH = pl.DeviceIdType.MESH
SHARE = 112
ROWS = 32
GROUPS_AT = (slice(0, 1), slice(1, 3), slice(3, 5), slice(5, 7), slice(7, 8))
ORDER = (4, 3, 5, 2, 6, 1, 7, 0)


def sampled(mean, devs, coef_ref):
    factor = (2.0 * (len(devs) - 1)) ** (-0.5)
    accum = mean.astype(jnp.float32)
    for member, dev in enumerate(devs):
        accum = accum + factor * coef_ref[member] * dev.astype(jnp.float32)
    return accum.astype(jnp.bfloat16)


def expand(heads):
    lane = lax.broadcasted_iota(jnp.int32, (heads.shape[0], 128), 1)
    return jnp.concatenate(
        [jnp.where(lane < P_SIZE, heads[:, 2 * j:2 * j + 1], heads[:, 2 * j + 1:2 * j + 2]) for j in range(4)],
        axis=1,
    )


def softplus(value):
    small = jnp.exp(-jnp.abs(value))
    series = small * (1.0 - small * (0.5 - small * (1.0 / 3.0 - small * 0.25)))
    return jnp.maximum(value, 0.0) + jnp.where(small < 0.01, series, jnp.log(1.0 + small))


def fold(tile):
    lane = lax.broadcasted_iota(jnp.int32, tile.shape, 1)
    joined = jnp.where((lane >= 96) & (lane < 104), tile + pltpu.roll(tile, 120, 1), tile)
    return jnp.where(lane >= 104, 0.0, joined)


def pack(tile):
    lane = lax.broadcasted_iota(jnp.int32, tile.shape, 1)
    high = tile.astype(jnp.bfloat16).astype(jnp.float32)
    low = pltpu.roll(tile - high, 8, 1)
    return jnp.where((lane >= 104) & (lane < 112), low, high).astype(jnp.bfloat16)


def layer_kernel(
    tok_ref, mean_ref, devs_ref, bc_mean_ref, bc_devs_ref, dt_ref, coef_ref, conv_x_ref, conv_bc_ref, bias_ref, rate_ref, skip_ref, out_ref,
    x_buf, w_ref, ring, rs_out, rs_own, rs_in, y_out, y_in, z_out, z_in, padded, edge, values, keys, reads, inner, states,
    pair_state, pair_decay, y_state, y_decay, x_state, x_decay, give_state, give_decay, inflow, outflow, dt_buf,
    own_sem, p_send, p_recv, a_send, a_recv, u_send, u_recv, c_send, c_recv, r_send, r_recv, rs_send, rs_recv,
    z_send, z_recv, y_send, y_recv, spread_sem,
    halo_send, halo_recv, p1_send, p1_recv, p2_send, p2_recv, p4_send, p4_recv,
):
    f = lax.axis_index("fsdp")
    s = lax.axis_index("seq")
    t = lax.axis_index("tp")
    q = lax.rem(s, 8)
    x = lax.div(s, 8)
    core = lax.rem(s, 2)
    y = lax.div(q, 2)
    z = f * 8 + t

    def wrap(value):
        return lax.rem(value + 4, 4)

    def place(x_at, y_at, core_at):
        return (f, x_at * 8 + y_at * 2 + core_at, t)

    def plane(z_at):
        z_at = lax.rem(z_at + 16, 16)
        return (lax.div(z_at, 8), s, lax.rem(z_at, 8))

    sibling = place(x, y, 1 - core)
    y_next, y_far, y_prev = (place(x, wrap(y + by), core) for by in (1, 2, 3))
    x_next, x_far, x_prev = (place(wrap(x + by), y, core) for by in (1, 2, 3))
    z_next, z_prev = plane(z + 1), plane(z - 1)
    q_at = [lax.rem(q + 1 + i, 8) for i in range(7)]
    q_peers = [(f, x * 8 + at, t) for at in q_at]
    t_at = [lax.rem(t + by, 8) for by in range(8)]
    t_peers = [(f, s, at) for at in t_at]
    seq_next, seq_prev = (f, lax.min(s + 1, 31), t), (f, lax.max(s - 1, 0), t)

    ring[:, 96:, :] = jnp.zeros((16, SHARE - 96, 1024), jnp.bfloat16)
    barrier = pltpu.get_barrier_semaphore()
    for peer in (x_next, x_far, x_prev, z_next, z_prev, *q_peers, *t_peers[1:]):
        pl.semaphore_signal(barrier, inc=1, device_id=peer, device_id_type=MESH)

    @pl.when(s < 31)
    def _():
        pl.semaphore_signal(barrier, inc=1, device_id=seq_next, device_id_type=MESH)

    @pl.when(s > 0)
    def _():
        pl.semaphore_signal(barrier, inc=1, device_id=seq_prev, device_id_type=MESH)

    sends = []

    def remote(src, dst, send_sem, recv_sem, peer):
        return pltpu.make_async_remote_copy(
            src_ref=src, dst_ref=dst, send_sem=send_sem, recv_sem=recv_sem,
            device_id=peer, device_id_type=MESH,
        )

    def launch(copy, condition=None):
        if condition is None:
            copy.start()
        else:
            pl.when(condition)(copy.start)
        sends.append((copy, condition))

    def token_columns(half, x_at):
        return tok_ref.at[:, pl.ds(pl.multiple_of(half * 4096 + x_at * 1024, 1024), 1024)]

    def token_place(half, x_at, q_here):
        return x_buf.at[x_at, q_here, :, pl.ds(half * 1024, 1024)]

    locals_ = [
        pltpu.make_async_copy(token_columns(half, x), token_place(half, x, q), own_sem.at[half]) for half in range(2)
    ]
    for copy in locals_:
        copy.start()
    for tile in range(4):
        columns = slice(tile * 128, (tile + 1) * 128)
        weight = sampled(mean_ref[:, columns], [devs_ref[m, :, columns] for m in range(4)], coef_ref)
        turned = weight.astype(jnp.float32).T.astype(jnp.bfloat16)
        w_ref[2 * tile, :64, :] = turned[:64]
        w_ref[2 * tile + 1, :64, :] = turned[64:]
    for kind in range(2):
        weight = sampled(bc_mean_ref[:, kind, :], [bc_devs_ref[m, :, kind, :] for m in range(4)], coef_ref)
        turned = weight.astype(jnp.float32).T.astype(jnp.bfloat16)
        for g in range(8):
            w_ref[g, 64 + 16 * kind:80 + 16 * kind, :] = turned[16 * g:16 * g + 16]
    dt_rows = jnp.concatenate([dt_ref[...].astype(jnp.float32), jnp.zeros((8, 128), jnp.float32)], axis=0)
    for g in range(8):
        w_ref[g, 96:, :] = dt_rows.astype(jnp.bfloat16)
    lanes = pl.ds(pl.multiple_of(q * 128, 128), 128)
    locals_.append(pltpu.make_async_copy(w_ref.at[q], ring.at[z, :, lanes], own_sem.at[2]))
    locals_[2].start()
    pl.semaphore_wait(barrier, 19 + jnp.where(s > 0, 1, 0) + jnp.where(s < 31, 1, 0))

    for i in range(7):
        launch(remote(w_ref.at[q_at[i]], ring.at[z, :, lanes], p_send.at[i], p_recv.at[i], q_peers[i]))
    for i, peer in enumerate((x_next, x_far, x_prev)):
        for half in range(2):
            launch(remote(
                token_columns(half, wrap(x + 1 + i)), token_place(half, x, q), a_send.at[i, half], a_recv.at[i, half], peer
            ))

    pieces = (pl.ds(0, 48), pl.ds(48, 48), pl.ds(96, 16))

    def ring_copy(way, k, b, slot):
        piece = ring.at[lax.rem(slot + 32, 16), pieces[b]]
        return remote(piece, piece, r_send.at[way, k, b], r_recv.at[way, k, b], z_next if way == 0 else z_prev)

    def steps_here(slot):
        return lax.rem(slot + 32, 8) == q

    def ring_send(k, b):
        for way in range(2):
            slot = z - k if way == 0 else z + k
            if k < 7 or way == b:
                launch(ring_copy(way, k, b, slot))
            if b == 1 and (k < 7 or way == 0):
                launch(ring_copy(way, k, 2, slot), steps_here(slot))

    def ring_wait(k, b):
        for way in range(2):
            slot = z - 1 - k if way == 0 else z + 1 + k
            if k < 7 or way == b:
                ring_copy(way, k, b, slot).wait_recv()
            if b == 1 and (k < 7 or way == 0):
                pl.when(steps_here(slot))(ring_copy(way, k, 2, slot).wait_recv)

    def ring_step(k):
        for b in range(2):
            ring_wait(k, b)
            ring_send(k + 1, b)

    for i in range(7):
        from_q = pl.ds(pl.multiple_of(lax.rem(q + 7 - i, 8) * 128, 128), 128)
        remote(w_ref.at[q_at[i]], ring.at[z, :, from_q], p_send.at[i], p_recv.at[i], q_peers[i]).wait_recv()
    for copy in locals_:
        copy.wait()
    ring_send(0, 0)
    ring_send(0, 1)
    for i, peer in enumerate((x_next, x_far, x_prev)):
        for half in range(2):
            here = token_place(half, wrap(x - 1 - i), q)
            remote(here, here, a_send.at[i, half], a_recv.at[i, half], peer).wait_recv()

    def unit(y_by, core_at, part=None):
        member = wrap(y + y_by) * 2 + core_at
        return x_buf.at[:, member] if part is None else x_buf.at[pl.ds(2 * part, 2), member]

    def unit_copy(kind, piece):
        return remote(piece, piece, u_send.at[kind], u_recv.at[kind], y_next if kind % 2 == 0 else y_prev)

    def share(index, y_by):
        launch(remote(unit(y_by, core), unit(y_by, core), c_send.at[index], c_recv.at[index], sibling))

    launch(unit_copy(0, unit(0, core)))
    launch(unit_copy(1, unit(0, core)))
    share(0, 0)
    ring_step(0)
    ring_step(1)
    ring_step(2)
    for kind, y_by in ((0, -1), (1, 1)):
        unit_copy(kind, unit(y_by, core)).wait_recv()
        launch(unit_copy(2 + kind, unit(y_by, core, kind)))
        share(1 + kind, y_by)
    ring_step(3)
    for kind in range(2):
        unit_copy(2 + kind, unit(2, core, kind)).wait_recv()
    share(3, 2)
    ring_step(4)
    for index, y_by in enumerate((0, -1, 1, 2)):
        here = unit(y_by, 1 - core)
        remote(here, here, c_send.at[index], c_recv.at[index], sibling).wait_recv()

    def narrowed(by, tile, where_to, joined):
        steps = q == t_at[by]

        @pl.when(steps)
        def _():
            where_to[...] = pack(fold(tile) if joined else tile)

        @pl.when(jnp.logical_not(steps))
        def _():
            where_to[...] = tile.astype(jnp.bfloat16)

    def multiply(*bys):
        for owner in range(4):
            total = None
            for half in range(2):
                weight = jnp.concatenate([ring[t_at[by] + 8 * half] for by in bys], axis=0)
                units = x_buf[owner, :, :, half * 1024:(half + 1) * 1024].reshape(256, 1024)
                one = lax.dot_general(
                    units, weight, (((1,), (1,)), ((), ())), preferred_element_type=jnp.float32
                )
                total = one if total is None else total + one
            for at, by in enumerate(bys):
                tile = jnp.concatenate(
                    [total[:, at * SHARE:(at + 1) * SHARE], jnp.zeros((256, 128 - SHARE), jnp.float32)], axis=1
                )
                narrowed(by, tile, rs_out.at[by, owner], False)

                @pl.when(x == owner)
                def _():
                    rs_own[by] = tile

        for by in bys:
            for i, peer in enumerate((x_next, x_far, x_prev)):
                launch(remote(rs_out.at[by, wrap(x + 1 + i)], rs_in.at[by, i], rs_send.at[by, i], rs_recv.at[by, i], peer))

    def settle(by):
        total = rs_own[by]
        for i, peer in enumerate((x_next, x_far, x_prev)):
            remote(rs_in.at[by, i], rs_in.at[by, i], rs_send.at[by, i], rs_recv.at[by, i], peer).wait_recv()
            total = total + rs_in[by, i].astype(jnp.float32)
        narrowed(by, total, y_out.at[ORDER.index(by)], True)

    def spread_copy(group, i):
        slots = GROUPS_AT[group]
        owner = q if i == 7 else q_at[i]
        piece = y_out.at[slots, pl.ds(pl.multiple_of(owner * ROWS, ROWS), ROWS)]
        there = y_in.at[slots, q]
        if i == 7:
            return pltpu.make_async_copy(piece, there, spread_sem.at[group])
        return remote(piece, there, y_send.at[group, i], y_recv.at[group, i], q_peers[i])

    def spread(group):
        spread_copy(group, 7).start()
        for i in range(7):
            launch(spread_copy(group, i))

    lane = lax.broadcasted_iota(jnp.int32, (1, 128), 1)

    def collect(group):
        slots = GROUPS_AT[group]
        spread_copy(group, 7).wait()
        for i in range(7):
            here = y_in.at[slots, lax.rem(q + 7 - i, 8)]
            remote(here, here, y_send.at[group, i], y_recv.at[group, i], q_peers[i]).wait_recv()
        for at in range(slots.start, slots.stop):
            by = ORDER[at]
            tiles = [y_in[at, g].astype(jnp.float32) for g in range(8)]
            joined = [
                jnp.concatenate([tiles[2 * j][:, :P_SIZE], tiles[2 * j + 1][:, :P_SIZE]], axis=1) for j in range(4)
            ]
            joined.append(jnp.concatenate([tile[:, 64:80] for tile in tiles], axis=1))
            joined.append(jnp.concatenate([tile[:, 80:96] for tile in tiles], axis=1))
            steps = pltpu.roll(y_in[at, t_at[by]].astype(jnp.float32), 32, 1)
            joined.append(jnp.where(lane < 16, steps, 0.0))
            whole = jnp.concatenate(joined, axis=1).astype(jnp.bfloat16)
            if by == 0:
                z_in[t] = whole
            else:
                z_out[at] = whole
                launch(remote(z_out.at[at], z_in.at[t], z_send.at[by], z_recv.at[by], t_peers[by]))

    multiply(4)
    multiply(3, 5)
    ring_step(5)
    multiply(2, 6)
    settle(4)
    spread(0)
    ring_step(6)
    settle(3)
    settle(5)
    spread(1)
    multiply(1, 7)
    collect(0)
    settle(2)
    settle(6)
    spread(2)
    ring_wait(7, 0)
    ring_wait(7, 1)
    multiply(0)
    collect(1)
    settle(1)
    settle(7)
    spread(3)
    collect(2)
    settle(0)
    spread(4)
    collect(3)
    collect(4)
    def arrived(by):
        here = z_in.at[lax.rem(t + 8 - by, 8)]
        remote(here, here, z_send.at[by], z_recv.at[by], z_next).wait_recv()

    pl.when(t < 7)(lambda: arrived(lax.rem(t + 1, 8)))
    edge[0] = z_in[7, 16:, :768]
    launch(remote(edge.at[0], edge.at[1], halo_send, halo_recv, seq_next), s < 31)
    for by in (4, 3, 5, 2, 6, 1, 7):
        pl.when(t + 1 != by)(lambda by=by: arrived(by))
    padded[16:, :] = z_in[:, :, :768].reshape(256, 768).astype(jnp.float32)
    logits = z_in[:, :, 768:].reshape(256, 128).astype(jnp.float32)
    dt_buf[...] = logits + pltpu.roll(logits, 120, 1)

    def row_of(ref):
        row = jnp.zeros((1, 128), jnp.float32)
        for head in range(8):
            row = jnp.where(lane == head, ref[head], row)
        return row

    step = softplus(dt_buf[...] + row_of(bias_ref))
    rise = -step * row_of(rate_ref)
    down_to = lax.broadcasted_iota(jnp.int32, (SPAN, SPAN), 0)
    across = lax.broadcasted_iota(jnp.int32, (SPAN, SPAN), 1)
    causal = across <= down_to
    triangle = jnp.where(causal, 1.0, 0.0).astype(jnp.float32)
    steps, cums, step_rows, cum_rows, lasts = [], [], [], [], []
    for b in range(2):
        here = slice(b * SPAN, (b + 1) * SPAN)
        cum = jnp.dot(
            triangle, rise[here], precision=lax.Precision.HIGHEST, preferred_element_type=jnp.float32
        )
        steps.append(step[here])
        cums.append(cum)
        step_rows.append(step[here].T)
        cum_rows.append(cum.T)
        lasts.append(cum[SPAN - 1:, :])

    @pl.when(s > 0)
    def _():
        remote(edge.at[0], edge.at[1], halo_send, halo_recv, seq_next).wait_recv()
        padded[:16, :] = edge[1].astype(jnp.float32)

    @pl.when(s == 0)
    def _():
        padded[:16, :] = jnp.zeros((16, 768), jnp.float32)

    for tile in range(6):
        columns = slice(tile * 128, (tile + 1) * 128)
        gained = None
        for tap in range(CONV):
            if tile < 4:
                gain = conv_x_ref[tap:tap + 1, columns]
            else:
                gain = conv_bc_ref[tap, tile - 4:tile - 3, :]
            term = gain * padded[13 + tap:13 + tap + 256, columns]
            gained = term if gained is None else gained + term
        smooth = (gained * (1.0 / (1.0 + jnp.exp(-gained)))).astype(jnp.bfloat16)
        if tile < 4:
            values[:, columns] = smooth
        elif tile == 4:
            keys[...] = smooth
        else:
            reads[...] = smooth

    for b in range(2):
        here = slice(b * SPAN, (b + 1) * SPAN)
        factor = expand(jnp.exp(lasts[b] - cums[b]) * steps[b])
        scaled = (values[here, :].astype(jnp.float32) * factor).astype(jnp.bfloat16)
        states[b] = lax.dot_general(
            keys[here, :], scaled, (((0,), (0,)), ((), ())), preferred_element_type=jnp.float32
        )
    fades = [expand(jnp.exp(last)) for last in lasts]
    range_state = fades[1] * states[0] + states[1]
    range_decay = jnp.broadcast_to(fades[0] * fades[1], (8, 512))

    for side in range(2):
        half = slice(side * 256, (side + 1) * 256)
        give_state[side] = range_state[:, half].astype(jnp.bfloat16)
        give_decay[side] = range_decay[:, half]
    launch(remote(give_state.at[1 - core], pair_state, p1_send.at[0], p1_recv.at[0], sibling))
    launch(remote(give_decay.at[1 - core], pair_decay, p1_send.at[1], p1_recv.at[1], sibling))

    def inside(b, *pairs):
        here = slice(b * SPAN, (b + 1) * SPAN)
        scores = lax.dot_general(
            reads[here, :], keys[here, :], (((1,), (1,)), ((), ())), preferred_element_type=jnp.float32
        )
        masked = jnp.where(causal, scores, 0.0)
        for pair_at in pairs:
            both = []
            for head in (2 * pair_at, 2 * pair_at + 1):
                gap = cums[b][:, head:head + 1] - cum_rows[b][head:head + 1, :]
                weight = masked * jnp.exp(jnp.minimum(gap, 0.0)) * step_rows[b][head:head + 1, :]
                both.append(jnp.dot(
                    weight.astype(jnp.bfloat16), values[here, head * P_SIZE:(head + 1) * P_SIZE],
                    preferred_element_type=jnp.float32,
                ))
            inner[here, pair_at * 128:(pair_at + 1) * 128] = jnp.concatenate(both, axis=1)

    inside(0, 0, 1)
    remote(give_state.at[1 - core], pair_state, p1_send.at[0], p1_recv.at[0], sibling).wait_recv()
    remote(give_decay.at[1 - core], pair_decay, p1_send.at[1], p1_recv.at[1], sibling).wait_recv()
    first = core == 0
    near_state, near_decay = give_state[core].astype(jnp.float32), give_decay[core][:1]
    far_state, far_decay = pair_state[...].astype(jnp.float32), pair_decay[:1]
    state_0, decay_0 = jnp.where(first, near_state, far_state), jnp.where(first, near_decay, far_decay)
    state_1, decay_1 = jnp.where(first, far_state, near_state), jnp.where(first, far_decay, near_decay)

    def level(which, slots, decays, mine, state, decay, peers):
        slots[mine] = state.astype(jnp.bfloat16)
        decays[mine] = jnp.broadcast_to(decay, (8, 256))
        for shift, peer in enumerate(peers):
            launch(remote(slots.at[mine], slots.at[mine], p2_send.at[which, 0, shift], p2_recv.at[which, 0, shift], peer))
            launch(remote(decays.at[mine], decays.at[mine], p2_send.at[which, 1, shift], p2_recv.at[which, 1, shift], peer))

    def gather(which, slots, decays, mine, peers):
        for shift, peer in enumerate(peers):
            there = wrap(mine - 1 - shift)
            remote(slots.at[there], slots.at[there], p2_send.at[which, 0, shift], p2_recv.at[which, 0, shift], peer).wait_recv()
            remote(decays.at[there], decays.at[there], p2_send.at[which, 1, shift], p2_recv.at[which, 1, shift], peer).wait_recv()
        state, decay = jnp.zeros((N, 256), jnp.float32), jnp.ones((1, 256), jnp.float32)
        before, before_decay = state, decay
        for member in range(4):
            before = jnp.where(mine == member, state, before)
            before_decay = jnp.where(mine == member, decay, before_decay)
            fade = decays[member][:1]
            state = fade * state + slots[member].astype(jnp.float32)
            decay = decay * fade
        return before, before_decay, state, decay

    y_peers = [y_next, y_far, y_prev]
    x_peers = [x_next, x_far, x_prev]
    level(0, y_state, y_decay, y, decay_1 * state_0 + state_1, decay_0 * decay_1, y_peers)
    inside(0, 2, 3)
    inside(1, 0)
    before_y, before_y_decay, row_state, row_decay = gather(0, y_state, y_decay, y, y_peers)
    level(1, x_state, x_decay, x, row_state, row_decay, x_peers)
    inside(1, 1, 2)
    before_x, _, _, _ = gather(1, x_state, x_decay, x, x_peers)
    into_0 = before_y_decay * before_x + before_y
    into_1 = decay_0 * into_0 + state_0
    outflow[...] = jnp.where(first, into_1, into_0).astype(jnp.bfloat16)
    launch(remote(outflow, inflow.at[core], p4_send, p4_recv, sibling))
    inflow[core] = jnp.where(first, into_0, into_1).astype(jnp.bfloat16)
    inside(1, 3)
    remote(outflow, inflow.at[1 - core], p4_send, p4_recv, sibling).wait_recv()
    entering = jnp.concatenate([inflow[0], inflow[1]], axis=1)
    skips = expand(row_of(skip_ref))
    for b in range(2):
        here = slice(b * SPAN, (b + 1) * SPAN)
        outer = jnp.dot(reads[here, :], entering, preferred_element_type=jnp.float32)
        outer = expand(jnp.exp(cums[b])) * outer
        result = inner[here, :] + outer + skips * values[here, :].astype(jnp.float32)
        out_ref[here, :] = result.astype(jnp.bfloat16)
        if b == 0:
            entering = (fades[0] * entering.astype(jnp.float32) + states[0]).astype(jnp.bfloat16)
    for copy, condition in sends:
        if condition is None:
            copy.wait_send()
        else:
            pl.when(condition)(copy.wait_send)


def layer(*operands):
    vmem = pl.BlockSpec(memory_space=pltpu.VMEM)
    smem = pl.BlockSpec(memory_space=pltpu.SMEM)
    dma = pltpu.SemaphoreType.DMA
    bf16, f32 = jnp.bfloat16, jnp.float32
    return pl.pallas_call(
        layer_kernel,
        out_shape=jax.ShapeDtypeStruct((256, 512), bf16),
        in_specs=[vmem] * 6 + [smem, vmem, vmem, smem, smem, smem],
        out_specs=vmem,
        scratch_shapes=[
            pltpu.VMEM((4, 8, ROWS, 2048), bf16),
            pltpu.VMEM((8, SHARE, 128), bf16),
            pltpu.VMEM((16, SHARE, 1024), bf16),
            pltpu.VMEM((8, 4, 256, 128), bf16),
            pltpu.VMEM((8, 256, 128), f32),
            pltpu.VMEM((8, 3, 256, 128), bf16),
            pltpu.VMEM((8, 256, 128), bf16),
            pltpu.VMEM((8, 8, ROWS, 128), bf16),
            pltpu.VMEM((8, ROWS, 896), bf16),
            pltpu.VMEM((8, ROWS, 896), bf16),
            pltpu.VMEM((16 + 256, 768), f32),
            pltpu.VMEM((2, 16, 768), bf16),
            pltpu.VMEM((256, 512), bf16),
            pltpu.VMEM((256, N), bf16),
            pltpu.VMEM((256, N), bf16),
            pltpu.VMEM((256, 512), f32),
            pltpu.VMEM((2, N, 512), f32),
            pltpu.VMEM((N, 256), bf16),
            pltpu.VMEM((8, 256), f32),
            pltpu.VMEM((4, N, 256), bf16),
            pltpu.VMEM((4, 8, 256), f32),
            pltpu.VMEM((4, N, 256), bf16),
            pltpu.VMEM((4, 8, 256), f32),
            pltpu.VMEM((2, N, 256), bf16),
            pltpu.VMEM((2, 8, 256), f32),
            pltpu.VMEM((2, N, 256), bf16),
            pltpu.VMEM((N, 256), bf16),
            pltpu.VMEM((256, 128), f32),
            dma((3,)), dma((7,)), dma((7,)), dma((3, 2)), dma((3, 2)), dma((4,)), dma((4,)), dma((4,)), dma((4,)),
            dma((2, 8, 3)), dma((2, 8, 3)), dma((8, 3)), dma((8, 3)), dma((8,)), dma((8,)), dma((5, 7)), dma((5, 7)), dma((5,)),
            dma(()), dma(()), dma((2,)), dma((2,)), dma((2, 2, 3)), dma((2, 2, 3)), dma(()), dma(()),
        ],
        compiler_params=pltpu.CompilerParams(
            collective_id=0, has_side_effects=True, vmem_limit_bytes=56 * 2**20
        ),
        name="layer",
    )(*operands)


def body(
    tokens,
    proj_mean,
    proj_devs,
    bc_mean,
    bc_devs,
    swag_coef,
    dt_weight,
    dt_bias,
    decay_rate,
    skip_gain,
    conv_proj,
    conv_bc,
):
    return layer(
        tokens, proj_mean, proj_devs, bc_mean, bc_devs, dt_weight.T, swag_coef,
        conv_proj, conv_bc, dt_bias, decay_rate, skip_gain,
    )


def solution(mesh):
    return jax.shard_map(
        body,
        mesh=mesh,
        in_specs=(
            P(("fsdp", "seq", "tp"), None),
            P(("fsdp", "seq"), "tp"),
            P(None, ("fsdp", "seq"), "tp"),
            P(("fsdp", "seq"), None, "tp"),
            P(None, ("fsdp", "seq"), None, "tp"),
            P(),
            P(("fsdp", "seq"), "tp"),
            P("tp"),
            P("tp"),
            P("tp"),
            P(None, "tp"),
            P(None, None, "tp"),
        ),
        out_specs=P(("fsdp", "seq"), "tp"),
        check_vma=False,
    )
```
